1024 devices in a mesh: dp: 8 (over z_hi, core), mx: 8 (over y), my: 16 (over x, z_lo).
Axes of the slice: x: 8, y: 8, z: 8 (z_hi: 4, z_lo: 2; z = z_hi * 2 + z_lo), core: 2. Of those that a mesh axis runs over, the one named last changes fastest.
Arguments:
- tokens: bfloat16 [1024, 6144], P('dp', 'my'), may hold values from -31 to 31
- ln_gain: float32 [6144], P('my'), may hold values from 0.5 to 1.5
- query_gain: float32 [128], replicated, may hold values from 0.5 to 1.5
- key_gain: float32 [128], replicated, may hold values from 0.5 to 1.5
- w_qkv: bfloat16 [3, 6144, 3072], P(None, 'my', 'mx'), may hold values from -0.078125 to 0.078125
- w_hidden: bfloat16 [6144, 12288], P('my', 'mx'), may hold values from -0.078125 to 0.078125
- w_attn_out: bfloat16 [3072, 6144], P('mx', 'my'), may hold values from -0.046875 to 0.046875
- w_mlp_out: bfloat16 [12288, 6144], P('mx', 'my'), may hold values from -0.046875 to 0.046875
- cotangent: bfloat16 [1024, 6144], P('dp', 'my'), may hold values from -6 to 6
Outputs:
- mixed: bfloat16 [1024, 6144], P(('dp', 'mx'), 'my')
- grad_tokens: bfloat16 [1024, 6144], P(('dp', 'mx'), 'my')
- grad_qkv: float32 [3, 16, 384, 3072], P(None, 'my', 'dp', 'mx')
- grad_hidden: float32 [16, 384, 12288], P('my', 'dp', 'mx')
- grad_attn_out: float32 [8, 384, 6144], P('mx', 'dp', 'my')
- grad_mlp_out: float32 [8, 1536, 6144], P('mx', 'dp', 'my')
The draws below stay inside these ranges and needn't reach their ends.
All inputs are finite; a program needn't handle non-finite values.
Results may differ from the reference program's by a relative error of at most 0.04.
Values may be sent and summed in bfloat16 or wider, within the bound.
No kernel may reach another device: no remote copies, remote signals or barrier semaphores. Data moves between devices by JAX's collectives and lax.ppermute only.
A program may use at most 32 MiB of HBM per device.

```python
import jax
import jax.numpy as jnp
from jax import lax

D = 6144
HEADS = 24
HEAD_SIZE = 128
FF = 12288
PATCHES = 128
IMAGES = 8
TOKENS = 1024
HW = 3072
D_MY = 384
HW_MX = 384
FF_MX = 1536
N_DP = 8
N_MX = 8
N_MY = 16


def draw_tokens(key, part):
    key = jax.random.fold_in(key, 7)
    first_key, second_key = jax.random.split(key, 2)
    column = 0.3 * 10.0 ** (jnp.arange(D, dtype=jnp.float32) / (D - 1))
    base = jnp.clip(jax.random.normal(first_key, (TOKENS, D), jnp.float32), -5.0, 5.0)
    row_scale = 2.0 ** jax.random.uniform(second_key, (TOKENS, 1), jnp.float32, -1.0, 1.0)
    return (base * row_scale * column).astype(jnp.bfloat16)


def steps_of(own_key, dims, cuts, least, top_value):
    def one(dim, shards_of):
        heights = jax.random.uniform(jax.random.fold_in(jax.random.fold_in(own_key, 6), dim), (shards_of,), jnp.float32, least / len(cuts), top_value / len(cuts))
        return jnp.repeat(jnp.exp(heights), dims[dim] // shards_of).reshape((-1,) + (1,) * (len(dims) - dim - 1))

    factor_of = one(*cuts[0])
    for cut in cuts[1:]:
        factor_of = factor_of * one(*cut)
    return factor_of


def normal_values(own_key, extent, deviation, reach, cuts=(), kind=jnp.bfloat16):
    factor_of = steps_of(own_key, extent, cuts, -0.22, 0.18) if cuts else 1.0
    entries = jax.random.normal(own_key, extent, jnp.float32) * deviation * factor_of
    return jnp.minimum(jnp.maximum(entries, -reach), reach).astype(kind)


def setup_inputs(seed: int = 0) -> dict:
    key_of = jax.random.split(jax.random.key(seed), 10)
    return {
        "tokens": draw_tokens(jax.random.fold_in(key_of[9], 71), 0),
        "ln_gain": jnp.clip(0.5 + 1.0 * jax.random.uniform(key_of[1], (D,), jnp.float32) ** steps_of(key_of[1], (D,), ((0, 16),), -0.2, 0.2), 0.5, 1.5),
        "query_gain": jnp.clip(jax.random.uniform(key_of[2], (HEAD_SIZE,), jnp.float32, 0.5, 1.5), 0.5, 1.5),
        "key_gain": jnp.clip(jax.random.uniform(key_of[3], (HEAD_SIZE,), jnp.float32, 0.5, 1.5), 0.5, 1.5),
        "w_qkv": normal_values(key_of[4], (3, D, HW), D ** -0.5, 0.078125, ((1, 16), (2, 8))),
        "w_hidden": normal_values(key_of[5], (D, FF), D ** -0.5, 0.078125, ((0, 16), (1, 8))),
        "w_attn_out": normal_values(key_of[6], (HW, D), (HW + FF) ** -0.5, 0.046875, ((0, 8), (1, 16))),
        "w_mlp_out": normal_values(key_of[7], (FF, D), (HW + FF) ** -0.5, 0.046875, ((0, 8), (1, 16))),
        "cotangent": normal_values(key_of[8], (TOKENS, D), 1.0, 6.0, ((0, 8), (1, 16))),
    }


EPSILON = 1e-06

def gelu_tanh(values):
    return jax.nn.gelu(values, approximate=True)

def blocked(first_op, second_op, first_dim, second_dim, blocks):
    portion = first_op.shape[first_dim] // blocks
    keep_first = [first_op.shape[axis_id] for axis_id in range(2) if axis_id != first_dim][0]
    keep_second = [second_op.shape[axis_id] for axis_id in range(2) if axis_id != second_dim][0]

    def add_block(running, block_id):
        begin = (block_id * portion).astype(jnp.int32)
        first_part = lax.dynamic_slice_in_dim(first_op, begin, portion, first_dim)
        second_part = lax.dynamic_slice_in_dim(second_op, begin, portion, second_dim)
        product = lax.dot_general(first_part, second_part, (((first_dim,), (second_dim,)), ((), ())), preferred_element_type=jnp.float32)
        rounded = lax.optimization_barrier(product.astype(jnp.bfloat16))
        return (running + rounded.astype(jnp.float32), None)
    start_value = jnp.zeros((keep_first, keep_second), jnp.float32)
    running, _ = lax.scan(add_block, start_value, jnp.arange(blocks, dtype=jnp.int32))
    return running

def head_norm(values):
    shaped = values.reshape(values.shape[0], HEADS, HEAD_SIZE)
    centred = shaped - lax.optimization_barrier(jnp.mean(shaped, axis=2, keepdims=True))
    inverse = lax.rsqrt(lax.optimization_barrier(jnp.mean(centred * centred, axis=2, keepdims=True)) + EPSILON)
    return (centred * inverse, inverse)

def norm_back(grad_norm, hat_values, inverse, gain):
    grad_hat = grad_norm * gain
    centred = grad_hat - lax.optimization_barrier(jnp.mean(grad_hat, axis=2, keepdims=True)) - hat_values * lax.optimization_barrier(jnp.mean(grad_hat * hat_values, axis=2, keepdims=True))
    return (inverse * centred).reshape(grad_norm.shape[0], HW).astype(jnp.bfloat16)

def reference(tokens, ln_gain, query_gain, key_gain, w_qkv, w_hidden, w_attn_out, w_mlp_out, cotangent):
    values = tokens.astype(jnp.float32)
    mean_row = lax.optimization_barrier(jnp.sum(values, axis=1, keepdims=True)) / D
    inverse_row = lax.rsqrt(lax.optimization_barrier(jnp.sum(values * values, axis=1, keepdims=True)) / D - mean_row * mean_row + EPSILON)
    normal_hat = (values - mean_row) * inverse_row
    normed = (normal_hat * ln_gain).astype(jnp.bfloat16)
    query = blocked(normed, w_qkv[0], 1, 0, N_MY).astype(jnp.bfloat16)
    key_pre = blocked(normed, w_qkv[1], 1, 0, N_MY).astype(jnp.bfloat16)
    value_rows = blocked(normed, w_qkv[2], 1, 0, N_MY).astype(jnp.bfloat16)
    hidden_pre = blocked(normed, w_hidden, 1, 0, N_MY).astype(jnp.bfloat16).astype(jnp.float32)
    query_hat, query_inv = head_norm(query.astype(jnp.float32))
    key_hat, key_inv = head_norm(key_pre.astype(jnp.float32))
    query_norm = (query_hat * query_gain).reshape(TOKENS, HW).astype(jnp.bfloat16)
    key_norm = (key_hat * key_gain).reshape(TOKENS, HW).astype(jnp.bfloat16)
    hidden_act = gelu_tanh(hidden_pre).astype(jnp.bfloat16)
    four_dims = (IMAGES, PATCHES, HEADS, HEAD_SIZE)
    scale_factor = HEAD_SIZE ** (-0.5)
    query_four = query_norm.reshape(four_dims).astype(jnp.float32)
    key_four = key_norm.reshape(four_dims).astype(jnp.float32)
    value_four = value_rows.reshape(four_dims).astype(jnp.float32)
    scores = jnp.einsum('bqhc,bkhc->bhqk', query_four, key_four) * scale_factor
    probs = jax.nn.softmax(scores, axis=-1)
    probs_low = probs.astype(jnp.bfloat16)
    attn_mix = jnp.einsum('bhqk,bkhc->bqhc', probs_low.astype(jnp.float32), value_four).reshape(TOKENS, HW).astype(jnp.bfloat16)
    out_sum = jnp.dot(attn_mix, w_attn_out, preferred_element_type=jnp.float32) + jnp.dot(hidden_act, w_mlp_out, preferred_element_type=jnp.float32)
    mixed = (values + out_sum).astype(jnp.bfloat16)
    grad_attn_out = blocked(attn_mix, cotangent, 0, 0, N_DP)
    grad_mlp_out = blocked(hidden_act, cotangent, 0, 0, N_DP)
    grad_mix = blocked(cotangent, w_attn_out, 1, 1, N_MY).astype(jnp.bfloat16)
    grad_act = blocked(cotangent, w_mlp_out, 1, 1, N_MY).astype(jnp.bfloat16)
    _, pullback = jax.vjp(gelu_tanh, hidden_pre)
    grad_hpre = pullback(grad_act.astype(jnp.float32))[0].astype(jnp.bfloat16)
    grad_mix_four = grad_mix.reshape(four_dims).astype(jnp.float32)
    grad_probs = jnp.einsum('bqhc,bkhc->bhqk', grad_mix_four, value_four)
    grad_value = jnp.einsum('bhqk,bqhc->bkhc', probs_low.astype(jnp.float32), grad_mix_four).reshape(TOKENS, HW).astype(jnp.bfloat16)
    grad_scores = (probs * (grad_probs - lax.optimization_barrier(jnp.sum(grad_probs * probs, axis=-1, keepdims=True)))).astype(jnp.bfloat16).astype(jnp.float32)
    grad_qn = (jnp.einsum('bhqk,bkhc->bqhc', grad_scores, key_four) * scale_factor).reshape(TOKENS, HEADS, HEAD_SIZE)
    grad_kn = (jnp.einsum('bhqk,bqhc->bkhc', grad_scores, query_four) * scale_factor).reshape(TOKENS, HEADS, HEAD_SIZE)
    grad_query = norm_back(grad_qn, query_hat, query_inv, query_gain)
    grad_key = norm_back(grad_kn, key_hat, key_inv, key_gain)
    grad_normed = jnp.dot(grad_query, w_qkv[0].T, preferred_element_type=jnp.float32)
    grad_normed = grad_normed + jnp.dot(grad_key, w_qkv[1].T, preferred_element_type=jnp.float32)
    grad_normed = grad_normed + jnp.dot(grad_value, w_qkv[2].T, preferred_element_type=jnp.float32)
    grad_normed = grad_normed + jnp.dot(grad_hpre, w_hidden.T, preferred_element_type=jnp.float32)
    grad_hat = grad_normed * ln_gain
    mean_one = lax.optimization_barrier(jnp.sum(grad_hat, axis=1, keepdims=True)) / D
    mean_two = lax.optimization_barrier(jnp.sum(grad_hat * normal_hat, axis=1, keepdims=True)) / D
    grad_values = inverse_row * (grad_hat - mean_one - normal_hat * mean_two)
    grad_tokens = (cotangent.astype(jnp.float32) + grad_values).astype(jnp.bfloat16)
    grad_qkv = jnp.stack([blocked(normed, grad_query, 0, 0, N_DP), blocked(normed, grad_key, 0, 0, N_DP), blocked(normed, grad_value, 0, 0, N_DP)])
    grad_hidden = blocked(normed, grad_hpre, 0, 0, N_DP)
    return (mixed, grad_tokens, grad_qkv.reshape(3, N_MY, D_MY, HW), grad_hidden.reshape(N_MY, D_MY, FF), grad_attn_out.reshape(N_MX, HW_MX, D), grad_mlp_out.reshape(N_MX, FF_MX, D))
```

```python
import jax
import jax.numpy as jnp
from jax import lax
from jax.experimental import pallas as pl
from jax.experimental.pallas import tpu as pltpu
from jax.sharding import PartitionSpec as P

EPSILON = 1e-06
LANES = 128
BF16 = jnp.bfloat16
F32 = jnp.float32


def dot_plain(matrix_a, matrix_b):
    return jnp.dot(matrix_a, matrix_b, preferred_element_type=F32)


def dot_first(matrix_a, matrix_b):
    return lax.dot_general(matrix_a, matrix_b, (((0,), (0,)), ((), ())), preferred_element_type=F32)


def dot_last(matrix_a, matrix_b):
    return lax.dot_general(matrix_a, matrix_b, (((1,), (1,)), ((), ())), preferred_element_type=F32)


def pieces(value, count):
    out = []
    for _ in range(count):
        part = value.astype(BF16).astype(F32)
        out.append(part)
        value = value - part
    return out


def to_lanes(columns):
    rows = columns[0].shape[0]
    lane = lax.broadcasted_iota(jnp.int32, (rows, LANES), 1)
    block = jnp.zeros((rows, LANES), F32)
    for index, column in enumerate(columns):
        block = jnp.where(lane == index, column, block)
    return block


def from_lanes(block, first, count):
    lane = lax.broadcasted_iota(jnp.int32, block.shape, block.ndim - 1)
    keep = (lane >= first) & (lane < first + count)
    return jnp.sum(jnp.where(keep, block, 0.0), axis=-1, keepdims=True)


def whole(count):
    return [pl.BlockSpec(memory_space=pltpu.VMEM)] * count


def run(kernel, operands, out_shape, scratch=(), scalar=False):
    n_out = len(out_shape)
    in_specs = whole(len(operands))
    if scalar:
        in_specs[0] = pl.BlockSpec(memory_space=pltpu.SMEM)
    return pl.pallas_call(
        kernel,
        in_specs=in_specs,
        out_specs=whole(n_out),
        out_shape=out_shape,
        scratch_shapes=list(scratch),
        compiler_params=pltpu.CompilerParams(vmem_limit_bytes=56 * 1024 * 1024),
    )(*operands)


def project_kernel(share, tokens, ln_gain, w_qkv, w_hidden, w_attn, w_mlp, cotangent, out):
    rows, width = tokens.shape
    head_width = w_qkv.shape[2]
    blocks = w_hidden.shape[1] // head_width
    values = tokens[...].astype(F32)
    mean = jnp.sum(values, axis=1, keepdims=True) / width
    centred = values - mean
    squares = jnp.sum(centred * centred, axis=1, keepdims=True)
    gain = ln_gain[...]
    scaled = (centred * gain).astype(BF16)
    high, low = pieces(gain, 2)
    row_id = lax.broadcasted_iota(jnp.int32, (16, width), 0)
    gain_rows = jnp.where(row_id == 0, high, jnp.where(row_id == 1, low, 0.0)).astype(BF16)
    share_id = lax.broadcasted_iota(jnp.int32, (share, head_width), 0)
    gain_sums = jnp.zeros((share, head_width), F32)
    for block in range(3 + blocks):
        if block < 3:
            weight = w_qkv[block]
        else:
            weight = w_hidden[:, (block - 3) * head_width : (block - 2) * head_width]
        start = block * head_width
        out[:, start : start + head_width] = dot_plain(scaled, weight).astype(BF16)
        both = dot_plain(gain_rows, weight)
        gain_sums = jnp.where(share_id == block, both[0:1] + both[1:2], gain_sums)
    start = (3 + blocks) * head_width
    back = cotangent[...]
    out[:, start : start + head_width] = dot_last(back, w_attn[...]).astype(BF16)
    start += head_width
    for block in range(blocks):
        weight = w_mlp[block * head_width : (block + 1) * head_width, :]
        out[:, start : start + head_width] = dot_last(back, weight).astype(BF16)
        start += head_width
    spread = jnp.broadcast_to(gain_sums[None], (rows // share, share, head_width))
    out[:, start : start + head_width] = spread.reshape(rows, head_width).astype(BF16)
    start += head_width
    out[:, start : start + LANES] = to_lanes(pieces(mean, 3) + pieces(squares, 3)).astype(BF16)


def share_kernel(head_width, local_width, got, out, sums_out):
    rows, columns = got.shape
    share = sums_out.shape[0]
    parts = rows // share
    hidden_width = (columns - 5 * head_width - LANES) // 2
    blocks = hidden_width // head_width
    width = parts * local_width

    def take(start, length):
        return got[:, start : start + length].astype(F32).reshape(parts, share, length)

    stats_at = columns - LANES
    stats = take(stats_at, LANES)
    local_mean = from_lanes(stats, 0, 3)
    mean = jnp.sum(local_mean, axis=0, keepdims=True) / parts
    shift = local_mean - mean
    square_sum = jnp.sum(from_lanes(stats, 3, 3) + local_width * shift * shift, axis=0)
    inverse = lax.rsqrt(square_sum / width + EPSILON)
    gain_parts = take(stats_at - head_width, head_width)
    gain_sums = jnp.sum(gain_parts, axis=0)
    sums_out[...] = gain_sums

    def spread(value):
        length = value.shape[1]
        tiled = jnp.broadcast_to(value[None], (parts, share, length))
        return tiled.reshape(rows, length).astype(BF16)

    def projected(block):
        total = jnp.sum(take(block * head_width, head_width), axis=0)
        total = total + jnp.sum(shift * gain_parts[:, block : block + 1, :], axis=0)
        return (inverse * total).astype(BF16).astype(F32)

    back_at = (3 + blocks) * head_width
    for block in range(3):
        out[:, block * head_width : (block + 1) * head_width] = spread(projected(block))
    out[:, 3 * head_width : 4 * head_width] = spread(jnp.sum(take(back_at, head_width), axis=0))
    plain_sum = jnp.zeros((share, 1), F32)
    hat_sum = jnp.zeros((share, 1), F32)
    inner_scale = 0.7978845608028654
    for block in range(blocks):
        pre = projected(3 + block)
        grad_act = jnp.sum(take(back_at + (1 + block) * head_width, head_width), axis=0)
        grad_act = grad_act.astype(BF16).astype(F32)
        squared = pre * pre
        bent = jnp.tanh(inner_scale * (pre + 0.044715 * squared * pre))
        active = 0.5 * pre * (1.0 + bent)
        slope = 0.5 * (1.0 + bent) + 0.5 * pre * (1.0 - bent * bent) * inner_scale * (
            1.0 + 3.0 * 0.044715 * squared
        )
        grad_pre = (grad_act * slope).astype(BF16).astype(F32)
        plain_sum += jnp.sum(grad_pre * gain_sums[3 + block : 4 + block], axis=1, keepdims=True)
        hat_sum += jnp.sum(grad_pre * pre, axis=1, keepdims=True)
        start = (4 + block) * head_width
        out[:, start : start + head_width] = spread(active)
        start += hidden_width
        out[:, start : start + head_width] = spread(grad_pre)
    scalars = pieces(mean[0], 3) + pieces(inverse, 3) + pieces(plain_sum, 2) + pieces(hat_sum, 2)
    out[:, 4 * head_width + 2 * hidden_width :] = spread(to_lanes(scalars))


def attend_kernel(
    full, gain_sums, tokens, ln_gain, query_gain, key_gain, w_qkv, w_hidden, w_attn, w_mlp,
    cotangent, terms, acts,
):
    head_size = query_gain.shape[1]
    head_width = w_qkv.shape[2]
    hidden_width = w_hidden.shape[1]
    local_width = tokens.shape[1]
    stats = full[:, 4 * head_width + 2 * hidden_width :].astype(F32)
    mean, inverse = from_lanes(stats, 0, 3), from_lanes(stats, 3, 3)
    plain_sum, hat_sum = from_lanes(stats, 6, 2), from_lanes(stats, 8, 2)
    normal_hat = (tokens[...].astype(F32) - mean) * inverse
    acts[:, :local_width] = (normal_hat * ln_gain[...]).astype(BF16)
    acts[:, local_width : 2 * local_width] = cotangent[...]
    hidden_at = 4 * head_width
    acts_hidden = 2 * local_width
    acts[:, acts_hidden : acts_hidden + 2 * hidden_width] = full[:, hidden_at : hidden_at + 2 * hidden_width]
    acts_heads = acts_hidden + 2 * hidden_width
    scale = head_size ** (-0.5)

    def normalise(values):
        centred = values - jnp.mean(values, axis=1, keepdims=True)
        root = lax.rsqrt(jnp.mean(centred * centred, axis=1, keepdims=True) + EPSILON)
        return centred * root, root

    def back(grad, hat, root, gain):
        grad = grad * gain
        centred = grad - jnp.mean(grad, axis=1, keepdims=True)
        centred = centred - hat * jnp.mean(grad * hat, axis=1, keepdims=True)
        return (root * centred).astype(BF16)

    for head in range(head_width // head_size):
        low, high = head * head_size, (head + 1) * head_size
        query = full[:, low:high].astype(F32)
        key = full[:, head_width + low : head_width + high].astype(F32)
        value_low = full[:, 2 * head_width + low : 2 * head_width + high]
        grad_mix = full[:, 3 * head_width + low : 3 * head_width + high]
        query_hat, query_root = normalise(query)
        key_hat, key_root = normalise(key)
        query_norm = (query_hat * query_gain[...]).astype(BF16)
        key_norm = (key_hat * key_gain[...]).astype(BF16)
        scores = dot_last(query_norm, key_norm) * scale
        weights = jnp.exp(scores - jnp.max(scores, axis=1, keepdims=True))
        probs = weights / jnp.sum(weights, axis=1, keepdims=True)
        probs_low = probs.astype(BF16)
        acts[:, acts_heads + low : acts_heads + high] = dot_plain(probs_low, value_low).astype(BF16)
        grad_probs = dot_last(grad_mix, value_low)
        grad_value = dot_first(probs_low, grad_mix).astype(BF16)
        grad_scores = probs * (grad_probs - jnp.sum(grad_probs * probs, axis=1, keepdims=True))
        grad_scores = grad_scores.astype(BF16)
        grad_query = back(
            dot_plain(grad_scores, key_norm) * scale, query_hat, query_root, query_gain[...]
        )
        grad_key = back(
            dot_first(grad_scores, query_norm) * scale, key_hat, key_root, key_gain[...]
        )
        plain = jnp.zeros_like(query)
        with_hat = jnp.zeros_like(query)
        for part, (grad, pre) in enumerate(
            ((grad_query, query), (grad_key, key), (grad_value, value_low.astype(F32)))
        ):
            start = acts_heads + (1 + part) * head_width
            acts[:, start + low : start + high] = grad
            grad = grad.astype(F32)
            plain = plain + grad * gain_sums[part : part + 1, low:high]
            with_hat = with_hat + grad * pre
        plain_sum = plain_sum + jnp.sum(plain, axis=1, keepdims=True)
        hat_sum = hat_sum + jnp.sum(with_hat, axis=1, keepdims=True)

    mixed = dot_plain(acts[:, acts_heads : acts_heads + head_width], w_attn[...])
    mixed = mixed + dot_plain(full[:, hidden_at : hidden_at + hidden_width], w_mlp[...])
    terms[:, :local_width] = mixed.astype(BF16)
    grad_normed = dot_last(full[:, hidden_at + hidden_width : hidden_at + 2 * hidden_width], w_hidden[...])
    for part in range(3):
        start = acts_heads + (1 + part) * head_width
        grad_normed = grad_normed + dot_last(acts[:, start : start + head_width], w_qkv[part])
    terms[:, local_width : 2 * local_width] = grad_normed.astype(BF16)
    terms[:, 2 * local_width :] = to_lanes(pieces(plain_sum, 2) + pieces(hat_sum, 2)).astype(BF16)


def weight_kernel(
    head_width, hidden_width, n_dp, place, own, peer, first, *rest
):
    others, (norm_t, mix_t, act_t) = rest[:-3], rest[-3:]
    local_width = norm_t.shape[0]
    hidden_at = 2 * local_width
    heads_at = hidden_at + 2 * hidden_width

    def both(start, length):
        return jnp.concatenate([own[:, start : start + length], peer[:, start : start + length]], axis=0)

    norm_t[...] = both(0, local_width).T
    mix_t[...] = both(heads_at, head_width).T
    act_t[...] = both(hidden_at, hidden_width).T
    outs = (first,) + tuple(others)
    chips = n_dp // 2
    core, chip = place[0] % 2, place[0] // 2
    owners = [2 * ((chip + step) % chips) + core for step in range(chips)]

    def rows(ref, length):
        return jnp.concatenate(
            [ref[pl.ds(pl.multiple_of(owner * length, 16), length), :] for owner in owners], axis=0
        )

    row = 0

    def emit(left, right):
        nonlocal row
        length = left.shape[0] // chips
        product = dot_plain(left, right)
        for step, out in enumerate(outs):
            out[row : row + length, :] = product[step * length : (step + 1) * length].astype(out.dtype)
        row += length

    norm_rows = rows(norm_t, local_width // n_dp)
    for part in range(3):
        emit(norm_rows, both(heads_at + (1 + part) * head_width, head_width))
    for block in range(hidden_width // head_width):
        emit(norm_rows, both(hidden_at + hidden_width + block * head_width, head_width))
    cotangent = both(local_width, local_width)
    emit(rows(mix_t, head_width // n_dp), cotangent)
    emit(rows(act_t, hidden_width // n_dp), cotangent)


def token_kernel(place, got, full, tokens, ln_gain, cotangent, mixed, grad_tokens):
    out_rows, local_width = mixed.shape
    parts = got.shape[0] // out_rows
    width = place[1]
    first = pl.multiple_of(place[0] * out_rows, 16)

    def total(start, length):
        values = got[:, start : start + length].astype(F32)
        return jnp.sum(values.reshape(parts, out_rows, length), axis=0)

    values = tokens[pl.ds(first, out_rows), :].astype(F32)
    mixed[...] = (values + total(0, local_width)).astype(BF16)
    stats = full[pl.ds(first, out_rows), full.shape[1] - LANES :].astype(F32)
    mean, inverse = from_lanes(stats, 0, 3), from_lanes(stats, 3, 3)
    normal_hat = (values - mean) * inverse
    sums = total(2 * local_width, LANES)
    share = 1.0 / width.astype(F32)
    mean_one, mean_two = from_lanes(sums, 0, 2) * share, from_lanes(sums, 2, 2) * share
    grad_hat = total(local_width, local_width) * ln_gain[...]
    grad = inverse * (grad_hat - mean_one - normal_hat * mean_two)
    back = cotangent[pl.ds(first, out_rows), :].astype(F32)
    grad_tokens[...] = (back + grad).astype(BF16)


def sum_kernel(*refs):
    parts, (qkv, hidden, attn, mlp) = refs[:-4], refs[-4:]

    def total(start, length):
        value = parts[0][start : start + length, :].astype(F32)
        for part in parts[1:]:
            value = value + part[start : start + length, :].astype(F32)
        return value

    row = 0
    length, head_width = qkv.shape[2], qkv.shape[3]
    for part in range(3):
        qkv[part, 0] = total(row, length)
        row += length
    for block in range(hidden.shape[2] // head_width):
        hidden[0, :, block * head_width : (block + 1) * head_width] = total(row, length)
        row += length
    attn[0] = total(row, attn.shape[1])
    row += attn.shape[1]
    mlp[0] = total(row, mlp.shape[1])


def exchange(values, axis):
    return lax.all_to_all(values, axis, 0, 0, tiled=True)


def per_device(
    tokens, ln_gain, query_gain, key_gain, w_qkv, w_hidden, w_attn_out, w_mlp_out, cotangent
):
    n_dp, n_mx, n_my = lax.axis_size("dp"), lax.axis_size("mx"), lax.axis_size("my")
    row_count, local_width = tokens.shape
    head_width, hidden_width = w_qkv.shape[2], w_hidden.shape[1]
    width = local_width * n_my
    share, out_rows = row_count // n_my, row_count // n_mx
    ln_row, query_row, key_row = ln_gain[None], query_gain[None], key_gain[None]

    def shape(*dims, dtype=BF16):
        return jax.ShapeDtypeStruct(dims, dtype)

    (terms,) = run(
        lambda *refs: project_kernel(share, *refs),
        (tokens, ln_row, w_qkv, w_hidden, w_attn_out, w_mlp_out, cotangent),
        (shape(row_count, 5 * head_width + 2 * hidden_width + LANES),),
    )
    got = exchange(terms, "my")
    spread, gain_sums = run(
        lambda *refs: share_kernel(head_width, local_width, *refs),
        (got,),
        (
            shape(row_count, 4 * head_width + 2 * hidden_width + LANES),
            shape(share, head_width, dtype=F32),
        ),
    )
    full = exchange(spread, "my")
    act_width = 2 * local_width + 2 * hidden_width + 4 * head_width
    out_terms, acts = run(
        attend_kernel,
        (
            full, gain_sums, tokens, ln_row, query_row, key_row,
            w_qkv, w_hidden, w_attn_out, w_mlp_out, cotangent,
        ),
        (shape(row_count, 2 * local_width + LANES), shape(row_count, act_width)),
    )
    peer_acts = lax.ppermute(acts, "dp", [(source, source ^ 1) for source in range(n_dp)])
    out_got = exchange(out_terms, "mx")
    chips = n_dp // 2
    block_rows = (3 * local_width + local_width * hidden_width // head_width + head_width + hidden_width) // n_dp
    place = lax.axis_index("dp").reshape(1)
    sums = run(
        lambda *refs: weight_kernel(head_width, hidden_width, n_dp, *refs),
        (place, acts, peer_acts),
        tuple(shape(block_rows, local_width, dtype=BF16 if step else F32) for step in range(chips)),
        scratch=(
            pltpu.VMEM((local_width, 2 * row_count), BF16),
            pltpu.VMEM((head_width, 2 * row_count), BF16),
            pltpu.VMEM((hidden_width, 2 * row_count), BF16),
        ),
        scalar=True,
    )
    parts = [sums[0]]
    for step in range(1, chips):
        pairs = [(s, 2 * ((s // 2 + step) % chips) + s % 2) for s in range(n_dp)]
        parts.append(lax.ppermute(sums[step], "dp", pairs))
    place = jnp.stack([lax.axis_index("mx"), jnp.int32(width)])
    mixed, grad_tokens = run(
        token_kernel,
        (place, out_got, full, tokens, ln_row, cotangent),
        (shape(out_rows, local_width), shape(out_rows, local_width)),
        scalar=True,
    )
    grads = run(
        sum_kernel,
        tuple(parts),
        (
            shape(3, 1, local_width // n_dp, head_width, dtype=F32),
            shape(1, local_width // n_dp, hidden_width, dtype=F32),
            shape(1, head_width // n_dp, local_width, dtype=F32),
            shape(1, hidden_width // n_dp, local_width, dtype=F32),
        ),
    )
    return (mixed, grad_tokens, *grads)


def solution(mesh):
    placed = (
        P("dp", "my"),
        P("my"),
        P(),
        P(),
        P(None, "my", "mx"),
        P("my", "mx"),
        P("mx", "my"),
        P("mx", "my"),
        P("dp", "my"),
    )
    return jax.shard_map(
        per_device,
        mesh=mesh,
        in_specs=placed,
        out_specs=(
            P(("dp", "mx"), "my"),
            P(("dp", "mx"), "my"),
            P(None, "my", "dp", "mx"),
            P("my", "dp", "mx"),
            P("mx", "dp", "my"),
            P("mx", "dp", "my"),
        ),
        check_vma=False,
    )
```

```python
import jax
import jax.numpy as jnp
from jax import lax
from jax.experimental import pallas as pl
from jax.experimental.pallas import tpu as pltpu
from jax.sharding import PartitionSpec as P

EPSILON = 1e-06
LANES = 128
BF16 = jnp.bfloat16
F32 = jnp.float32


def dot_plain(matrix_a, matrix_b):
    return jnp.dot(matrix_a, matrix_b, preferred_element_type=F32)


def dot_first(matrix_a, matrix_b):
    return lax.dot_general(matrix_a, matrix_b, (((0,), (0,)), ((), ())), preferred_element_type=F32)


def dot_last(matrix_a, matrix_b):
    return lax.dot_general(matrix_a, matrix_b, (((1,), (1,)), ((), ())), preferred_element_type=F32)


def pieces(value, count):
    out = []
    for _ in range(count):
        part = value.astype(BF16).astype(F32)
        out.append(part)
        value = value - part
    return out


def to_lanes(columns):
    rows = columns[0].shape[0]
    lane = lax.broadcasted_iota(jnp.int32, (rows, LANES), 1)
    block = jnp.zeros((rows, LANES), F32)
    for index, column in enumerate(columns):
        block = jnp.where(lane == index, column, block)
    return block


def from_lanes(block, first, count):
    lane = lax.broadcasted_iota(jnp.int32, block.shape, block.ndim - 1)
    keep = (lane >= first) & (lane < first + count)
    return jnp.sum(jnp.where(keep, block, 0.0), axis=-1, keepdims=True)


def run(kernel, operands, out_shape, scratch=(), scalar=False, sent=(), fetched=(), mebibytes=16):
    n_in, n_out, n_own = len(operands), len(out_shape), len(scratch)
    in_specs = [pl.BlockSpec(memory_space=pltpu.VMEM)] * n_in
    out_specs = [pl.BlockSpec(memory_space=pltpu.VMEM)] * n_out
    if scalar:
        in_specs[0] = pl.BlockSpec(memory_space=pltpu.SMEM)
    for index in fetched:
        in_specs[index] = pl.BlockSpec(memory_space=pltpu.HBM)
    for index in sent:
        out_specs[index] = pl.BlockSpec(memory_space=pltpu.HBM)
    staging = [pltpu.VMEM(out_shape[index].shape, out_shape[index].dtype) for index in sent]
    if sent:
        staging.append(pltpu.SemaphoreType.DMA((len(sent),)))

    def body(*refs):
        outs = list(refs[n_in : n_in + n_out])
        own = refs[n_in + n_out : n_in + n_out + n_own]
        stage = refs[n_in + n_out + n_own :]
        copies = []
        for place, index in enumerate(sent):
            copies.append(pltpu.make_async_copy(stage[place], outs[index], stage[-1].at[place]))
            outs[index] = stage[place]
        kernel(*refs[:n_in], *outs, *own)
        for copy in copies:
            copy.start()
        for copy in copies:
            copy.wait()

    return pl.pallas_call(
        body,
        in_specs=in_specs,
        out_specs=out_specs,
        out_shape=out_shape,
        scratch_shapes=list(scratch) + staging,
        compiler_params=pltpu.CompilerParams(vmem_limit_bytes=mebibytes * 1024 * 1024),
    )(*operands)


def project_kernel(
    share, tokens, ln_gain, w_qkv_far, w_hidden_far, w_attn_far, w_mlp_far, cotangent, out,
    w_qkv, w_hidden, w_attn, w_mlp, arrived,
):
    rows, width = tokens.shape
    head_width = w_qkv.shape[2]
    blocks = w_hidden.shape[1] // head_width
    pairs = ((w_qkv_far, w_qkv), (w_hidden_far, w_hidden), (w_attn_far, w_attn), (w_mlp_far, w_mlp))
    loads = [pltpu.make_async_copy(*pair, arrived.at[index]) for index, pair in enumerate(pairs)]
    for load in loads:
        load.start()
    values = tokens[...].astype(F32)
    mean = jnp.sum(values, axis=1, keepdims=True) / width
    centred = values - mean
    squares = jnp.sum(centred * centred, axis=1, keepdims=True)
    gain = ln_gain[...][None]
    scaled = (centred * gain).astype(BF16)
    high, low = pieces(gain, 2)
    row_id = lax.broadcasted_iota(jnp.int32, (16, width), 0)
    gain_rows = jnp.where(row_id == 0, high, jnp.where(row_id == 1, low, 0.0)).astype(BF16)
    share_id = lax.broadcasted_iota(jnp.int32, (share, head_width), 0)
    gain_sums = jnp.zeros((share, head_width), F32)
    for block in range(3 + blocks):
        if block == 0 or block == 3:
            loads[block // 3].wait()
        if block < 3:
            weight = w_qkv[block]
        else:
            weight = w_hidden[:, (block - 3) * head_width : (block - 2) * head_width]
        start = block * head_width
        out[:, start : start + head_width] = dot_plain(scaled, weight).astype(BF16)
        both = dot_plain(gain_rows, weight)
        gain_sums = jnp.where(share_id == block, both[0:1] + both[1:2], gain_sums)
    start = (3 + blocks) * head_width
    back = cotangent[...]
    loads[2].wait()
    out[:, start : start + head_width] = dot_last(back, w_attn[...]).astype(BF16)
    start += head_width
    loads[3].wait()
    for block in range(blocks):
        weight = w_mlp[block * head_width : (block + 1) * head_width, :]
        out[:, start : start + head_width] = dot_last(back, weight).astype(BF16)
        start += head_width
    spread = jnp.broadcast_to(gain_sums[None], (rows // share, share, head_width))
    out[:, start : start + head_width] = spread.reshape(rows, head_width).astype(BF16)
    start += head_width
    out[:, start : start + LANES] = to_lanes(pieces(mean, 3) + pieces(squares, 3)).astype(BF16)


def share_kernel(head_width, local_width, got, out, sums_out):
    rows, columns = got.shape
    share = sums_out.shape[0]
    parts = rows // share
    hidden_width = (columns - 5 * head_width - LANES) // 2
    blocks = hidden_width // head_width
    width = parts * local_width

    def take(start, length):
        return got[:, start : start + length].astype(F32).reshape(parts, share, length)

    stats_at = columns - LANES
    stats = take(stats_at, LANES)
    local_mean = from_lanes(stats, 0, 3)
    mean = jnp.sum(local_mean, axis=0, keepdims=True) / parts
    shift = local_mean - mean
    square_sum = jnp.sum(from_lanes(stats, 3, 3) + local_width * shift * shift, axis=0)
    inverse = lax.rsqrt(square_sum / width + EPSILON)
    gain_parts = take(stats_at - head_width, head_width)
    gain_sums = jnp.sum(gain_parts, axis=0)
    sums_out[...] = gain_sums

    def spread(value):
        length = value.shape[1]
        tiled = jnp.broadcast_to(value[None], (parts, share, length))
        return tiled.reshape(rows, length).astype(BF16)

    def projected(block):
        total = jnp.sum(take(block * head_width, head_width), axis=0)
        total = total + jnp.sum(shift * gain_parts[:, block : block + 1, :], axis=0)
        return (inverse * total).astype(BF16).astype(F32)

    back_at = (3 + blocks) * head_width
    for block in range(3):
        out[:, block * head_width : (block + 1) * head_width] = spread(projected(block))
    out[:, 3 * head_width : 4 * head_width] = spread(jnp.sum(take(back_at, head_width), axis=0))
    plain_sum = jnp.zeros((share, 1), F32)
    hat_sum = jnp.zeros((share, 1), F32)
    inner_scale = 0.7978845608028654
    for block in range(blocks):
        pre = projected(3 + block)
        grad_act = jnp.sum(take(back_at + (1 + block) * head_width, head_width), axis=0)
        grad_act = grad_act.astype(BF16).astype(F32)
        squared = pre * pre
        bent = jnp.tanh(inner_scale * (pre + 0.044715 * squared * pre))
        active = 0.5 * pre * (1.0 + bent)
        slope = 0.5 * (1.0 + bent) + 0.5 * pre * (1.0 - bent * bent) * inner_scale * (
            1.0 + 3.0 * 0.044715 * squared
        )
        grad_pre = (grad_act * slope).astype(BF16).astype(F32)
        plain_sum += jnp.sum(grad_pre * gain_sums[3 + block : 4 + block], axis=1, keepdims=True)
        hat_sum += jnp.sum(grad_pre * pre, axis=1, keepdims=True)
        start = (4 + block) * head_width
        out[:, start : start + head_width] = spread(active)
        start += hidden_width
        out[:, start : start + head_width] = spread(grad_pre)
    scalars = pieces(mean[0], 3) + pieces(inverse, 3) + pieces(plain_sum, 2) + pieces(hat_sum, 2)
    out[:, 4 * head_width + 2 * hidden_width :] = spread(to_lanes(scalars))


def attend_kernel(
    full, gain_sums, tokens, ln_gain, query_gain, key_gain, w_qkv, w_hidden, w_attn, w_mlp,
    cotangent, terms, acts,
):
    head_size = query_gain.shape[0]
    query_row, key_row = query_gain[...][None], key_gain[...][None]
    head_width = w_qkv.shape[2]
    hidden_width = w_hidden.shape[1]
    local_width = tokens.shape[1]
    stats = full[:, 4 * head_width + 2 * hidden_width :].astype(F32)
    mean, inverse = from_lanes(stats, 0, 3), from_lanes(stats, 3, 3)
    plain_sum, hat_sum = from_lanes(stats, 6, 2), from_lanes(stats, 8, 2)
    normal_hat = (tokens[...].astype(F32) - mean) * inverse
    acts[:, :local_width] = (normal_hat * ln_gain[...][None]).astype(BF16)
    acts[:, local_width : 2 * local_width] = cotangent[...]
    hidden_at = 4 * head_width
    acts_hidden = 2 * local_width
    acts[:, acts_hidden : acts_hidden + 2 * hidden_width] = full[:, hidden_at : hidden_at + 2 * hidden_width]
    acts_heads = acts_hidden + 2 * hidden_width
    scale = head_size ** (-0.5)

    def normalise(values):
        centred = values - jnp.mean(values, axis=1, keepdims=True)
        root = lax.rsqrt(jnp.mean(centred * centred, axis=1, keepdims=True) + EPSILON)
        return centred * root, root

    def back(grad, hat, root, gain):
        grad = grad * gain
        centred = grad - jnp.mean(grad, axis=1, keepdims=True)
        centred = centred - hat * jnp.mean(grad * hat, axis=1, keepdims=True)
        return (root * centred).astype(BF16)

    for head in range(head_width // head_size):
        low, high = head * head_size, (head + 1) * head_size
        query = full[:, low:high].astype(F32)
        key = full[:, head_width + low : head_width + high].astype(F32)
        value_low = full[:, 2 * head_width + low : 2 * head_width + high]
        grad_mix = full[:, 3 * head_width + low : 3 * head_width + high]
        query_hat, query_root = normalise(query)
        key_hat, key_root = normalise(key)
        query_norm = (query_hat * query_row).astype(BF16)
        key_norm = (key_hat * key_row).astype(BF16)
        scores = dot_last(query_norm, key_norm) * scale
        weights = jnp.exp(scores - jnp.max(scores, axis=1, keepdims=True))
        probs = weights / jnp.sum(weights, axis=1, keepdims=True)
        probs_low = probs.astype(BF16)
        acts[:, acts_heads + low : acts_heads + high] = dot_plain(probs_low, value_low).astype(BF16)
        grad_probs = dot_last(grad_mix, value_low)
        grad_value = dot_first(probs_low, grad_mix).astype(BF16)
        grad_scores = probs * (grad_probs - jnp.sum(grad_probs * probs, axis=1, keepdims=True))
        grad_scores = grad_scores.astype(BF16)
        grad_query = back(
            dot_plain(grad_scores, key_norm) * scale, query_hat, query_root, query_row
        )
        grad_key = back(
            dot_first(grad_scores, query_norm) * scale, key_hat, key_root, key_row
        )
        plain = jnp.zeros_like(query)
        with_hat = jnp.zeros_like(query)
        for part, (grad, pre) in enumerate(
            ((grad_query, query), (grad_key, key), (grad_value, value_low.astype(F32)))
        ):
            start = acts_heads + (1 + part) * head_width
            acts[:, start + low : start + high] = grad
            grad = grad.astype(F32)
            plain = plain + grad * gain_sums[part : part + 1, low:high]
            with_hat = with_hat + grad * pre
        plain_sum = plain_sum + jnp.sum(plain, axis=1, keepdims=True)
        hat_sum = hat_sum + jnp.sum(with_hat, axis=1, keepdims=True)

    mixed = dot_plain(acts[:, acts_heads : acts_heads + head_width], w_attn[...])
    mixed = mixed + dot_plain(full[:, hidden_at : hidden_at + hidden_width], w_mlp[...])
    terms[:, :local_width] = mixed.astype(BF16)
    grad_normed = dot_last(full[:, hidden_at + hidden_width : hidden_at + 2 * hidden_width], w_hidden[...])
    for part in range(3):
        start = acts_heads + (1 + part) * head_width
        grad_normed = grad_normed + dot_last(acts[:, start : start + head_width], w_qkv[part])
    terms[:, local_width : 2 * local_width] = grad_normed.astype(BF16)
    terms[:, 2 * local_width :] = to_lanes(pieces(plain_sum, 2) + pieces(hat_sum, 2)).astype(BF16)


def weight_kernel(
    head_width, hidden_width, n_dp, place, own, peer,
    here, next_a, next_b, last_a, last_b, far_a, far_b, norm_t, mix_t, act_t,
):
    local_width = norm_t.shape[0]
    hidden_at = 2 * local_width
    heads_at = hidden_at + 2 * hidden_width

    def both(start, length):
        return jnp.concatenate([own[:, start : start + length], peer[:, start : start + length]], axis=0)

    norm_t[...] = both(0, local_width).T
    mix_t[...] = both(heads_at, head_width).T
    act_t[...] = both(hidden_at, hidden_width).T
    half = next_a.shape[0]
    core, chip = place[0] % 2, place[0] // 2
    owners = [2 * ((chip + step) % (n_dp // 2)) + core for step in range(n_dp // 2)]
    outs = ((next_a, next_b), (far_a, far_b), (last_a, last_b))

    def rows(ref, length):
        return jnp.concatenate(
            [ref[pl.ds(pl.multiple_of(owner * length, 16), length), :] for owner in owners], axis=0
        )

    row = 0

    def emit(left, right):
        nonlocal row
        length = left.shape[0] // len(owners)
        product = dot_plain(left, right)
        here[row : row + length, :] = product[:length]
        for step, pair in enumerate(outs, 1):
            start = row % half
            out = pair[row // half]
            out[start : start + length, :] = product[step * length : (step + 1) * length].astype(BF16)
        row += length

    norm_rows = rows(norm_t, local_width // n_dp)
    for part in range(3):
        emit(norm_rows, both(heads_at + (1 + part) * head_width, head_width))
    for block in range(hidden_width // head_width):
        emit(norm_rows, both(hidden_at + hidden_width + block * head_width, head_width))
    cotangent = both(local_width, local_width)
    emit(rows(mix_t, head_width // n_dp), cotangent)
    emit(rows(act_t, hidden_width // n_dp), cotangent)


def relay_kernel(next_a, last_b, from_last, from_next, to_next, to_last):
    to_next[...] = (next_a[...].astype(F32) + from_last[...].astype(F32)).astype(BF16)
    to_last[...] = (last_b[...].astype(F32) + from_next[...].astype(F32)).astype(BF16)


def token_kernel(place, got, full, tokens, ln_gain, cotangent, mixed, grad_tokens):
    out_rows, local_width = mixed.shape
    parts = got.shape[0] // out_rows
    width = place[1]
    first = pl.multiple_of(place[0] * out_rows, 16)

    def total(start, length):
        values = got[:, start : start + length].astype(F32)
        return jnp.sum(values.reshape(parts, out_rows, length), axis=0)

    values = tokens[pl.ds(first, out_rows), :].astype(F32)
    mixed[...] = (values + total(0, local_width)).astype(BF16)
    stats = full[pl.ds(first, out_rows), full.shape[1] - LANES :].astype(F32)
    mean, inverse = from_lanes(stats, 0, 3), from_lanes(stats, 3, 3)
    normal_hat = (values - mean) * inverse
    sums = total(2 * local_width, LANES)
    share = 1.0 / width.astype(F32)
    mean_one, mean_two = from_lanes(sums, 0, 2) * share, from_lanes(sums, 2, 2) * share
    grad_hat = total(local_width, local_width) * ln_gain[...][None]
    grad = inverse * (grad_hat - mean_one - normal_hat * mean_two)
    back = cotangent[pl.ds(first, out_rows), :].astype(F32)
    grad_tokens[...] = (back + grad).astype(BF16)


def sum_kernel(here, last_a, last_b, next_a, next_b, qkv, hidden, attn, mlp):
    half = last_a.shape[0]

    def total(start, length):
        pair = (last_a, next_a) if start < half else (last_b, next_b)
        value = here[start : start + length, :]
        for part in pair:
            value = value + part[start % half : start % half + length, :].astype(F32)
        return value

    row = 0
    length, head_width = qkv.shape[2], qkv.shape[3]
    for part in range(3):
        qkv[part, 0] = total(row, length)
        row += length
    for block in range(hidden.shape[2] // head_width):
        hidden[0, :, block * head_width : (block + 1) * head_width] = total(row, length)
        row += length
    attn[0] = total(row, attn.shape[1])
    row += attn.shape[1]
    mlp[0] = total(row, mlp.shape[1])


def exchange(values, axis):
    return lax.all_to_all(values, axis, 0, 0, tiled=True)


def per_device(
    tokens, ln_gain, query_gain, key_gain, w_qkv, w_hidden, w_attn_out, w_mlp_out, cotangent
):
    n_dp, n_mx, n_my = lax.axis_size("dp"), lax.axis_size("mx"), lax.axis_size("my")
    row_count, local_width = tokens.shape
    head_width, hidden_width = w_qkv.shape[2], w_hidden.shape[1]
    width = local_width * n_my
    share, out_rows = row_count // n_my, row_count // n_mx

    weights = (w_qkv, w_hidden, w_attn_out, w_mlp_out)

    def shape(*dims, dtype=BF16):
        return jax.ShapeDtypeStruct(dims, dtype)

    (terms,) = run(
        lambda *refs: project_kernel(share, *refs),
        (tokens, ln_gain, *weights, cotangent),
        (shape(row_count, 5 * head_width + 2 * hidden_width + LANES),),
        scratch=[pltpu.VMEM(array.shape, BF16) for array in weights] + [pltpu.SemaphoreType.DMA((4,))],
        fetched=(2, 3, 4, 5),
        mebibytes=56,
    )
    got = exchange(terms, "my")
    spread, gain_sums = run(
        lambda *refs: share_kernel(head_width, local_width, *refs),
        (got,),
        (
            shape(row_count, 4 * head_width + 2 * hidden_width + LANES),
            shape(share, head_width, dtype=F32),
        ),
    )
    full = exchange(spread, "my")
    act_width = 2 * local_width + 2 * hidden_width + 4 * head_width
    out_terms, acts = run(
        attend_kernel,
        (
            full, gain_sums, tokens, ln_gain, query_gain, key_gain,
            *weights, cotangent,
        ),
        (shape(row_count, 2 * local_width + LANES), shape(row_count, act_width)),
        mebibytes=16,
    )
    peer_acts = lax.ppermute(acts, "dp", [(source, source ^ 1) for source in range(n_dp)])
    out_got = exchange(out_terms, "mx")
    block_rows = (3 * local_width + local_width * hidden_width // head_width + head_width + hidden_width) // n_dp
    halves = shape(block_rows // 2, local_width)
    place = lax.axis_index("dp").reshape(1)
    here, next_a, next_b, last_a, last_b, far_a, far_b = run(
        lambda *refs: weight_kernel(head_width, hidden_width, n_dp, *refs),
        (place, acts, peer_acts),
        (shape(block_rows, local_width, dtype=F32),) + (halves,) * 6,
        scratch=(
            pltpu.VMEM((local_width, 2 * row_count), BF16),
            pltpu.VMEM((head_width, 2 * row_count), BF16),
            pltpu.VMEM((hidden_width, 2 * row_count), BF16),
        ),
        scalar=True,
        mebibytes=60,
    )

    def pass_on(values, step):
        return lax.ppermute(values, "dp", [(s, (s + 2 * step) % n_dp) for s in range(n_dp)])

    from_last, from_next = pass_on(far_a, 1), pass_on(far_b, -1)
    got_last_b, got_next_a = pass_on(next_b, 1), pass_on(last_a, -1)
    to_next, to_last = run(relay_kernel, (next_a, last_b, from_last, from_next), (halves,) * 2)
    got_last_a, got_next_b = pass_on(to_next, 1), pass_on(to_last, -1)
    place = jnp.stack([lax.axis_index("mx"), jnp.int32(width)])
    mixed, grad_tokens = run(
        token_kernel,
        (place, out_got, full, tokens, ln_gain, cotangent),
        (shape(out_rows, local_width), shape(out_rows, local_width)),
        scalar=True,
    )
    grads = run(
        sum_kernel,
        (here, got_last_a, got_last_b, got_next_a, got_next_b),
        (
            shape(3, 1, local_width // n_dp, head_width, dtype=F32),
            shape(1, local_width // n_dp, hidden_width, dtype=F32),
            shape(1, head_width // n_dp, local_width, dtype=F32),
            shape(1, hidden_width // n_dp, local_width, dtype=F32),
        ),
    )
    return (mixed, grad_tokens, *grads)


def solution(mesh):
    placed = (
        P("dp", "my"),
        P("my"),
        P(),
        P(),
        P(None, "my", "mx"),
        P("my", "mx"),
        P("mx", "my"),
        P("mx", "my"),
        P("dp", "my"),
    )
    return jax.shard_map(
        per_device,
        mesh=mesh,
        in_specs=placed,
        out_specs=(
            P(("dp", "mx"), "my"),
            P(("dp", "mx"), "my"),
            P(None, "my", "dp", "mx"),
            P("my", "dp", "mx"),
            P("mx", "dp", "my"),
            P("mx", "dp", "my"),
        ),
        check_vma=False,
    )
```

```python
import jax
import jax.numpy as jnp
from jax import lax
from jax.experimental import pallas as pl
from jax.experimental.pallas import tpu as pltpu
from jax.sharding import PartitionSpec as P

EPSILON = 1e-06
LANES = 128
BF16 = jnp.bfloat16
F32 = jnp.float32


def dot_plain(matrix_a, matrix_b):
    return jnp.dot(matrix_a, matrix_b, preferred_element_type=F32)


def dot_first(matrix_a, matrix_b):
    return lax.dot_general(matrix_a, matrix_b, (((0,), (0,)), ((), ())), preferred_element_type=F32)


def dot_last(matrix_a, matrix_b):
    return lax.dot_general(matrix_a, matrix_b, (((1,), (1,)), ((), ())), preferred_element_type=F32)


def pieces(value, count):
    out = []
    for _ in range(count):
        part = value.astype(BF16).astype(F32)
        out.append(part)
        value = value - part
    return out


def to_lanes(columns):
    rows = columns[0].shape[0]
    lane = lax.broadcasted_iota(jnp.int32, (rows, LANES), 1)
    block = jnp.zeros((rows, LANES), F32)
    for index, column in enumerate(columns):
        block = jnp.where(lane == index, column, block)
    return block


def from_lanes(block, first, count):
    lane = lax.broadcasted_iota(jnp.int32, block.shape, block.ndim - 1)
    keep = (lane >= first) & (lane < first + count)
    return jnp.sum(jnp.where(keep, block, 0.0), axis=-1, keepdims=True)


def run(kernel, operands, out_shape, scratch=(), scalar=False, sent=(), fetched=(), mebibytes=16, work=None):
    n_in, n_out, n_own = len(operands), len(out_shape), len(scratch)
    in_specs = [pl.BlockSpec(memory_space=pltpu.VMEM)] * n_in
    out_specs = [pl.BlockSpec(memory_space=pltpu.VMEM)] * n_out
    if scalar:
        in_specs[0] = pl.BlockSpec(memory_space=pltpu.SMEM)
    for index in fetched:
        in_specs[index] = pl.BlockSpec(memory_space=pltpu.HBM)
    for index in sent:
        out_specs[index] = pl.BlockSpec(memory_space=pltpu.HBM)
    staging = [pltpu.VMEM(out_shape[index].shape, out_shape[index].dtype) for index in sent]
    if sent:
        staging.append(pltpu.SemaphoreType.DMA((len(sent),)))

    def body(*refs):
        outs = list(refs[n_in : n_in + n_out])
        own = refs[n_in + n_out : n_in + n_out + n_own]
        stage = refs[n_in + n_out + n_own :]
        copies = []
        for place, index in enumerate(sent):
            copies.append(pltpu.make_async_copy(stage[place], outs[index], stage[-1].at[place]))
            outs[index] = stage[place]
        kernel(*refs[:n_in], *outs, *own)
        for copy in copies:
            copy.start()
        for copy in copies:
            copy.wait()

    return pl.pallas_call(
        body,
        in_specs=in_specs,
        out_specs=out_specs,
        out_shape=out_shape,
        scratch_shapes=list(scratch) + staging,
        compiler_params=pltpu.CompilerParams(vmem_limit_bytes=mebibytes * 1024 * 1024),
        cost_estimate=work and pl.CostEstimate(flops=work, bytes_accessed=work, transcendentals=0),
    )(*operands)


def project_kernel(
    share, tokens, ln_gain, w_qkv_far, w_hidden_far, w_attn_far, w_mlp_far, cotangent, out,
    w_qkv, w_hidden, w_attn, w_mlp, arrived,
):
    rows, width = tokens.shape
    head_width = w_qkv.shape[2]
    blocks = w_hidden.shape[1] // head_width
    pairs = ((w_qkv_far, w_qkv), (w_hidden_far, w_hidden), (w_attn_far, w_attn), (w_mlp_far, w_mlp))
    loads = [pltpu.make_async_copy(*pair, arrived.at[index]) for index, pair in enumerate(pairs)]
    for load in loads:
        load.start()
    values = tokens[...].astype(F32)
    mean = jnp.sum(values, axis=1, keepdims=True) / width
    centred = values - mean
    squares = jnp.sum(centred * centred, axis=1, keepdims=True)
    gain = ln_gain[...][None]
    scaled = (centred * gain).astype(BF16)
    high, low = pieces(gain, 2)
    row_id = lax.broadcasted_iota(jnp.int32, (16, width), 0)
    gain_rows = jnp.where(row_id == 0, high, jnp.where(row_id == 1, low, 0.0)).astype(BF16)
    left = jnp.concatenate([scaled, gain_rows], axis=0)
    share_id = lax.broadcasted_iota(jnp.int32, (share, head_width), 0)
    gain_sums = jnp.zeros((share, head_width), F32)
    for block in range(3 + blocks):
        if block == 0 or block == 3:
            loads[block // 3].wait()
        if block < 3:
            weight = w_qkv[block]
        else:
            weight = w_hidden[:, (block - 3) * head_width : (block - 2) * head_width]
        start = block * head_width
        product = dot_plain(left, weight)
        out[:, start : start + head_width] = product[:rows].astype(BF16)
        both = product[rows : rows + 1] + product[rows + 1 : rows + 2]
        gain_sums = jnp.where(share_id == block, both, gain_sums)
    start = (3 + blocks) * head_width
    back = cotangent[...]
    loads[2].wait()
    out[:, start : start + head_width] = dot_last(back, w_attn[...]).astype(BF16)
    start += head_width
    loads[3].wait()
    for block in range(blocks):
        weight = w_mlp[block * head_width : (block + 1) * head_width, :]
        out[:, start : start + head_width] = dot_last(back, weight).astype(BF16)
        start += head_width
    spread = jnp.broadcast_to(gain_sums[None], (rows // share, share, head_width))
    out[:, start : start + head_width] = spread.reshape(rows, head_width).astype(BF16)
    start += head_width
    out[:, start : start + LANES] = to_lanes(pieces(mean, 3) + pieces(squares, 3)).astype(BF16)


def share_kernel(head_width, local_width, got, out, sums_out):
    rows, columns = got.shape
    share = sums_out.shape[0]
    parts = rows // share
    hidden_width = (columns - 5 * head_width - LANES) // 2
    blocks = hidden_width // head_width
    width = parts * local_width

    def take(start, length):
        return got[:, start : start + length].astype(F32).reshape(parts, share, length)

    stats_at = columns - LANES
    stats = take(stats_at, LANES)
    local_mean = from_lanes(stats, 0, 3)
    mean = jnp.sum(local_mean, axis=0, keepdims=True) / parts
    shift = local_mean - mean
    square_sum = jnp.sum(from_lanes(stats, 3, 3) + local_width * shift * shift, axis=0)
    inverse = lax.rsqrt(square_sum / width + EPSILON)
    gain_parts = take(stats_at - head_width, head_width)
    gain_sums = jnp.sum(gain_parts, axis=0)
    sums_out[...] = gain_sums

    def spread(value):
        length = value.shape[1]
        tiled = jnp.broadcast_to(value[None], (parts, share, length))
        return tiled.reshape(rows, length).astype(BF16)

    def projected(block):
        total = jnp.sum(take(block * head_width, head_width), axis=0)
        total = total + jnp.sum(shift * gain_parts[:, block : block + 1, :], axis=0)
        return (inverse * total).astype(BF16).astype(F32)

    back_at = (3 + blocks) * head_width
    for block in range(3):
        out[:, block * head_width : (block + 1) * head_width] = spread(projected(block))
    out[:, 3 * head_width : 4 * head_width] = spread(jnp.sum(take(back_at, head_width), axis=0))
    plain_sum = jnp.zeros((share, 1), F32)
    hat_sum = jnp.zeros((share, 1), F32)
    inner_scale = 0.7978845608028654
    for block in range(blocks):
        pre = projected(3 + block)
        grad_act = jnp.sum(take(back_at + (1 + block) * head_width, head_width), axis=0)
        grad_act = grad_act.astype(BF16).astype(F32)
        squared = pre * pre
        bent = jnp.tanh(inner_scale * (pre + 0.044715 * squared * pre))
        active = 0.5 * pre * (1.0 + bent)
        slope = 0.5 * (1.0 + bent) + 0.5 * pre * (1.0 - bent * bent) * inner_scale * (
            1.0 + 3.0 * 0.044715 * squared
        )
        grad_pre = (grad_act * slope).astype(BF16).astype(F32)
        plain_sum += jnp.sum(grad_pre * gain_sums[3 + block : 4 + block], axis=1, keepdims=True)
        hat_sum += jnp.sum(grad_pre * pre, axis=1, keepdims=True)
        start = (4 + block) * head_width
        out[:, start : start + head_width] = spread(active)
        start += hidden_width
        out[:, start : start + head_width] = spread(grad_pre)
    scalars = pieces(mean[0], 3) + pieces(inverse, 3) + pieces(plain_sum, 2) + pieces(hat_sum, 2)
    out[:, 4 * head_width + 2 * hidden_width :] = spread(to_lanes(scalars))


def attend_kernel(
    full, gain_sums, tokens, ln_gain, query_gain, key_gain, w_qkv, w_hidden, w_attn, w_mlp,
    cotangent, terms, acts,
):
    head_size = query_gain.shape[0]
    query_row, key_row = query_gain[...][None], key_gain[...][None]
    head_width = w_qkv.shape[2]
    hidden_width = w_hidden.shape[1]
    local_width = tokens.shape[1]
    stats = full[:, 4 * head_width + 2 * hidden_width :].astype(F32)
    mean, inverse = from_lanes(stats, 0, 3), from_lanes(stats, 3, 3)
    plain_sum, hat_sum = from_lanes(stats, 6, 2), from_lanes(stats, 8, 2)
    normal_hat = (tokens[...].astype(F32) - mean) * inverse
    acts[:, :local_width] = (normal_hat * ln_gain[...][None]).astype(BF16)
    acts[:, local_width : 2 * local_width] = cotangent[...]
    hidden_at = 4 * head_width
    acts_hidden = 2 * local_width
    acts[:, acts_hidden : acts_hidden + 2 * hidden_width] = full[:, hidden_at : hidden_at + 2 * hidden_width]
    acts_heads = acts_hidden + 2 * hidden_width
    scale = head_size ** (-0.5)

    def normalise(values):
        centred = values - jnp.mean(values, axis=1, keepdims=True)
        root = lax.rsqrt(jnp.mean(centred * centred, axis=1, keepdims=True) + EPSILON)
        return centred * root, root

    def back(grad, hat, root, gain):
        grad = grad * gain
        centred = grad - jnp.mean(grad, axis=1, keepdims=True)
        centred = centred - hat * jnp.mean(grad * hat, axis=1, keepdims=True)
        return (root * centred).astype(BF16)

    for head in range(head_width // head_size):
        low, high = head * head_size, (head + 1) * head_size
        query = full[:, low:high].astype(F32)
        key = full[:, head_width + low : head_width + high].astype(F32)
        value_low = full[:, 2 * head_width + low : 2 * head_width + high]
        grad_mix = full[:, 3 * head_width + low : 3 * head_width + high]
        query_hat, query_root = normalise(query)
        key_hat, key_root = normalise(key)
        query_norm = (query_hat * query_row).astype(BF16)
        key_norm = (key_hat * key_row).astype(BF16)
        scores = dot_last(query_norm, key_norm) * scale
        weights = jnp.exp(scores - jnp.max(scores, axis=1, keepdims=True))
        probs = weights / jnp.sum(weights, axis=1, keepdims=True)
        probs_low = probs.astype(BF16)
        acts[:, acts_heads + low : acts_heads + high] = dot_plain(probs_low, value_low).astype(BF16)
        grad_probs = dot_last(grad_mix, value_low)
        grad_value = dot_first(probs_low, grad_mix).astype(BF16)
        grad_scores = probs * (grad_probs - jnp.sum(grad_probs * probs, axis=1, keepdims=True))
        grad_scores = grad_scores.astype(BF16)
        grad_query = back(
            dot_plain(grad_scores, key_norm) * scale, query_hat, query_root, query_row
        )
        grad_key = back(
            dot_first(grad_scores, query_norm) * scale, key_hat, key_root, key_row
        )
        plain = jnp.zeros_like(query)
        with_hat = jnp.zeros_like(query)
        for part, (grad, pre) in enumerate(
            ((grad_query, query), (grad_key, key), (grad_value, value_low.astype(F32)))
        ):
            start = acts_heads + (1 + part) * head_width
            acts[:, start + low : start + high] = grad
            grad = grad.astype(F32)
            plain = plain + grad * gain_sums[part : part + 1, low:high]
            with_hat = with_hat + grad * pre
        plain_sum = plain_sum + jnp.sum(plain, axis=1, keepdims=True)
        hat_sum = hat_sum + jnp.sum(with_hat, axis=1, keepdims=True)

    mixed = dot_plain(acts[:, acts_heads : acts_heads + head_width], w_attn[...])
    mixed = mixed + dot_plain(full[:, hidden_at : hidden_at + hidden_width], w_mlp[...])
    terms[:, :local_width] = mixed.astype(BF16)
    grad_normed = dot_last(full[:, hidden_at + hidden_width : hidden_at + 2 * hidden_width], w_hidden[...])
    for part in range(3):
        start = acts_heads + (1 + part) * head_width
        grad_normed = grad_normed + dot_last(acts[:, start : start + head_width], w_qkv[part])
    terms[:, local_width : 2 * local_width] = grad_normed.astype(BF16)
    terms[:, 2 * local_width :] = to_lanes(pieces(plain_sum, 2) + pieces(hat_sum, 2)).astype(BF16)


def weight_kernel(
    head_width, hidden_width, n_dp, place, own, peer,
    here, next_a, next_b, last_a, last_b, far_a, far_b, norm_t, mix_t, act_t,
):
    local_width = norm_t.shape[0]
    hidden_at = 2 * local_width
    heads_at = hidden_at + 2 * hidden_width

    def both(start, length):
        return jnp.concatenate([own[:, start : start + length], peer[:, start : start + length]], axis=0)

    norm_t[...] = both(0, local_width).T
    mix_t[...] = both(heads_at, head_width).T
    act_t[...] = both(hidden_at, hidden_width).T
    half = next_a.shape[0]
    core, chip = place[0] % 2, place[0] // 2
    owners = [2 * ((chip + step) % (n_dp // 2)) + core for step in range(n_dp // 2)]
    outs = ((next_a, next_b), (far_a, far_b), (last_a, last_b))

    def rows(ref, length):
        return jnp.concatenate(
            [ref[pl.ds(pl.multiple_of(owner * length, 16), length), :] for owner in owners], axis=0
        )

    row = 0

    def emit(left, right):
        nonlocal row
        length = left.shape[0] // len(owners)
        product = dot_plain(left, right)
        here[row : row + length, :] = product[:length]
        for step, pair in enumerate(outs, 1):
            start = row % half
            out = pair[row // half]
            out[start : start + length, :] = product[step * length : (step + 1) * length].astype(BF16)
        row += length

    norm_rows = rows(norm_t, local_width // n_dp)
    for part in range(3):
        emit(norm_rows, both(heads_at + (1 + part) * head_width, head_width))
    for block in range(hidden_width // head_width):
        emit(norm_rows, both(hidden_at + hidden_width + block * head_width, head_width))
    cotangent = both(local_width, local_width)
    emit(rows(mix_t, head_width // n_dp), cotangent)
    emit(rows(act_t, hidden_width // n_dp), cotangent)


def relay_kernel(next_a, last_b, from_last, from_next, out_got, to_next, to_last):
    to_next[...] = (next_a[...].astype(F32) + from_last[...].astype(F32)).astype(BF16)
    to_last[...] = (last_b[...].astype(F32) + from_next[...].astype(F32)).astype(BF16)


def token_kernel(place, got, full, tokens, ln_gain, cotangent, mixed, grad_tokens):
    out_rows, local_width = mixed.shape
    parts = got.shape[0] // out_rows
    width = place[1]
    first = pl.multiple_of(place[0] * out_rows, 16)

    def total(start, length):
        values = got[:, start : start + length].astype(F32)
        return jnp.sum(values.reshape(parts, out_rows, length), axis=0)

    values = tokens[pl.ds(first, out_rows), :].astype(F32)
    mixed[...] = (values + total(0, local_width)).astype(BF16)
    stats = full[pl.ds(first, out_rows), full.shape[1] - LANES :].astype(F32)
    mean, inverse = from_lanes(stats, 0, 3), from_lanes(stats, 3, 3)
    normal_hat = (values - mean) * inverse
    sums = total(2 * local_width, LANES)
    share = 1.0 / width.astype(F32)
    mean_one, mean_two = from_lanes(sums, 0, 2) * share, from_lanes(sums, 2, 2) * share
    grad_hat = total(local_width, local_width) * ln_gain[...][None]
    grad = inverse * (grad_hat - mean_one - normal_hat * mean_two)
    back = cotangent[pl.ds(first, out_rows), :].astype(F32)
    grad_tokens[...] = (back + grad).astype(BF16)


def sum_kernel(here, last_a, last_b, next_a, next_b, qkv, hidden, attn, mlp):
    half = last_a.shape[0]

    def total(start, length):
        pair = (last_a, next_a) if start < half else (last_b, next_b)
        value = here[start : start + length, :]
        for part in pair:
            value = value + part[start % half : start % half + length, :].astype(F32)
        return value

    row = 0
    length, head_width = qkv.shape[2], qkv.shape[3]
    for part in range(3):
        qkv[part, 0] = total(row, length)
        row += length
    for block in range(hidden.shape[2] // head_width):
        hidden[0, :, block * head_width : (block + 1) * head_width] = total(row, length)
        row += length
    attn[0] = total(row, attn.shape[1])
    row += attn.shape[1]
    mlp[0] = total(row, mlp.shape[1])


def exchange(values, axis):
    return lax.all_to_all(values, axis, 0, 0, tiled=True)


def per_device(
    tokens, ln_gain, query_gain, key_gain, w_qkv, w_hidden, w_attn_out, w_mlp_out, cotangent
):
    n_dp, n_mx, n_my = lax.axis_size("dp"), lax.axis_size("mx"), lax.axis_size("my")
    row_count, local_width = tokens.shape
    head_width, hidden_width = w_qkv.shape[2], w_hidden.shape[1]
    width = local_width * n_my
    share, out_rows = row_count // n_my, row_count // n_mx

    weights = (w_qkv, w_hidden, w_attn_out, w_mlp_out)

    def shape(*dims, dtype=BF16):
        return jax.ShapeDtypeStruct(dims, dtype)

    (terms,) = run(
        lambda *refs: project_kernel(share, *refs),
        (tokens, ln_gain, *weights, cotangent),
        (shape(row_count, 5 * head_width + 2 * hidden_width + LANES),),
        scratch=[pltpu.VMEM(array.shape, BF16) for array in weights] + [pltpu.SemaphoreType.DMA((4,))],
        fetched=(2, 3, 4, 5),
        mebibytes=56,
    )
    got = exchange(terms, "my")
    spread, gain_sums = run(
        lambda *refs: share_kernel(head_width, local_width, *refs),
        (got,),
        (
            shape(row_count, 4 * head_width + 2 * hidden_width + LANES),
            shape(share, head_width, dtype=F32),
        ),
    )
    full = exchange(spread, "my")
    act_width = 2 * local_width + 2 * hidden_width + 4 * head_width
    out_terms, acts = run(
        attend_kernel,
        (
            full, gain_sums, tokens, ln_gain, query_gain, key_gain,
            *weights, cotangent,
        ),
        (shape(row_count, 2 * local_width + LANES), shape(row_count, act_width)),
        mebibytes=16,
    )
    peer_acts = lax.ppermute(acts, "dp", [(source, source ^ 1) for source in range(n_dp)])
    out_got = exchange(out_terms, "mx")
    block_rows = (3 * local_width + local_width * hidden_width // head_width + head_width + hidden_width) // n_dp
    halves = shape(block_rows // 2, local_width)
    place = lax.axis_index("dp").reshape(1)
    here, next_a, next_b, last_a, last_b, far_a, far_b = run(
        lambda *refs: weight_kernel(head_width, hidden_width, n_dp, *refs),
        (place, acts, peer_acts),
        (shape(block_rows, local_width, dtype=F32),) + (halves,) * 6,
        scratch=(
            pltpu.VMEM((local_width, 2 * row_count), BF16),
            pltpu.VMEM((head_width, 2 * row_count), BF16),
            pltpu.VMEM((hidden_width, 2 * row_count), BF16),
        ),
        scalar=True,
        mebibytes=60,
    )

    def pass_on(values, step):
        return lax.ppermute(values, "dp", [(s, (s + 2 * step) % n_dp) for s in range(n_dp)])

    from_last, from_next = pass_on(far_a, 1), pass_on(far_b, -1)
    got_last_b, got_next_a = pass_on(next_b, 1), pass_on(last_a, -1)
    to_next, to_last = run(
        relay_kernel,
        (next_a, last_b, from_last, from_next, out_got),
        (halves,) * 2,
        fetched=(4,),
        mebibytes=16,
    )
    got_last_a, got_next_b = pass_on(to_next, 1), pass_on(to_last, -1)
    place = jnp.stack([lax.axis_index("mx"), jnp.int32(width)])
    mixed, grad_tokens = run(
        token_kernel,
        (place, out_got, full, tokens, ln_gain, cotangent),
        (shape(out_rows, local_width), shape(out_rows, local_width)),
        scalar=True,
    )
    grads = run(
        sum_kernel,
        (here, got_last_a, got_last_b, got_next_a, got_next_b),
        (
            shape(3, 1, local_width // n_dp, head_width, dtype=F32),
            shape(1, local_width // n_dp, hidden_width, dtype=F32),
            shape(1, head_width // n_dp, local_width, dtype=F32),
            shape(1, hidden_width // n_dp, local_width, dtype=F32),
        ),
    )
    return (mixed, grad_tokens, *grads)


def solution(mesh):
    placed = (
        P("dp", "my"),
        P("my"),
        P(),
        P(),
        P(None, "my", "mx"),
        P("my", "mx"),
        P("mx", "my"),
        P("mx", "my"),
        P("dp", "my"),
    )
    return jax.shard_map(
        per_device,
        mesh=mesh,
        in_specs=placed,
        out_specs=(
            P(("dp", "mx"), "my"),
            P(("dp", "mx"), "my"),
            P(None, "my", "dp", "mx"),
            P("my", "dp", "mx"),
            P("mx", "dp", "my"),
            P("mx", "dp", "my"),
        ),
        check_vma=False,
    )
```

```python
import jax
import jax.numpy as jnp
from jax import lax
from jax.experimental import pallas as pl
from jax.experimental.pallas import tpu as pltpu
from jax.sharding import PartitionSpec as P

EPSILON = 1e-06
LANES = 128
BF16 = jnp.bfloat16
F32 = jnp.float32


def dot_plain(matrix_a, matrix_b):
    return jnp.dot(matrix_a, matrix_b, preferred_element_type=F32)


def dot_first(matrix_a, matrix_b):
    return lax.dot_general(matrix_a, matrix_b, (((0,), (0,)), ((), ())), preferred_element_type=F32)


def dot_last(matrix_a, matrix_b):
    return lax.dot_general(matrix_a, matrix_b, (((1,), (1,)), ((), ())), preferred_element_type=F32)


def pieces(value, count):
    out = []
    for _ in range(count):
        part = value.astype(BF16).astype(F32)
        out.append(part)
        value = value - part
    return out


def to_lanes(columns):
    rows = columns[0].shape[0]
    lane = lax.broadcasted_iota(jnp.int32, (rows, LANES), 1)
    block = jnp.zeros((rows, LANES), F32)
    for index, column in enumerate(columns):
        block = jnp.where(lane == index, column, block)
    return block


def from_lanes(block, first, count):
    lane = lax.broadcasted_iota(jnp.int32, block.shape, block.ndim - 1)
    keep = (lane >= first) & (lane < first + count)
    return jnp.sum(jnp.where(keep, block, 0.0), axis=-1, keepdims=True)


def run(kernel, operands, out_shape, scratch=(), scalar=False, fetched=(), written=(), mebibytes=16):
    in_specs = [pl.BlockSpec(memory_space=pltpu.VMEM)] * len(operands)
    out_specs = [pl.BlockSpec(memory_space=pltpu.VMEM)] * len(out_shape)
    if scalar:
        in_specs[0] = pl.BlockSpec(memory_space=pltpu.SMEM)
    for index in fetched:
        in_specs[index] = pl.BlockSpec(memory_space=pltpu.HBM)
    for index in written:
        out_specs[index] = pl.BlockSpec(memory_space=pltpu.HBM)
    return pl.pallas_call(
        kernel,
        in_specs=in_specs,
        out_specs=out_specs,
        out_shape=out_shape,
        scratch_shapes=list(scratch),
        compiler_params=pltpu.CompilerParams(vmem_limit_bytes=mebibytes * 1024 * 1024),
    )(*operands)


def project_kernel(share, *refs):
    far, out_far, near, out, arrived, left_for = refs[:7], refs[7], refs[8:15], refs[15], refs[16], refs[17]
    tokens, ln_gain, w_qkv, w_hidden, cotangent, w_attn, w_mlp = near
    rows, width = tokens.shape
    head_width = w_qkv.shape[2]
    blocks = w_hidden.shape[1] // head_width
    loads = [
        pltpu.make_async_copy(source, target, arrived.at[index])
        for index, (source, target) in enumerate(zip(far, near))
    ]
    for load in loads:
        load.start()
    sends = []

    def emit(values):
        columns = pl.ds(sum(send[1] for send in sends), values.shape[1])
        out[:, columns] = values.astype(BF16)
        copy = pltpu.make_async_copy(out.at[:, columns], out_far.at[:, columns], left_for.at[len(sends)])
        copy.start()
        sends.append((copy, values.shape[1]))

    loads[0].wait()
    loads[1].wait()
    values = tokens[...].astype(F32)
    mean = jnp.sum(values, axis=1, keepdims=True) / width
    centred = values - mean
    squares = jnp.sum(centred * centred, axis=1, keepdims=True)
    gain = ln_gain[...][None]
    scaled = (centred * gain).astype(BF16)
    high, low = pieces(gain, 2)
    row_id = lax.broadcasted_iota(jnp.int32, (16, width), 0)
    gain_rows = jnp.where(row_id == 0, high, jnp.where(row_id == 1, low, 0.0)).astype(BF16)
    left = jnp.concatenate([scaled, gain_rows], axis=0)
    share_id = lax.broadcasted_iota(jnp.int32, (share, head_width), 0)
    gain_sums = jnp.zeros((share, head_width), F32)
    for block in range(3 + blocks):
        if block == 0 or block == 3:
            loads[2 + block // 3].wait()
        if block < 3:
            weight = w_qkv[block]
        else:
            weight = w_hidden[:, (block - 3) * head_width : (block - 2) * head_width]
        product = dot_plain(left, weight)
        emit(product[:rows])
        both = product[rows : rows + 1] + product[rows + 1 : rows + 2]
        gain_sums = jnp.where(share_id == block, both, gain_sums)
    loads[4].wait()
    loads[5].wait()
    back = cotangent[...]
    emit(dot_last(back, w_attn[...]))
    loads[6].wait()
    for block in range(blocks):
        emit(dot_last(back, w_mlp[block * head_width : (block + 1) * head_width, :]))
    spread = jnp.broadcast_to(gain_sums[None], (rows // share, share, head_width))
    emit(spread.reshape(rows, head_width))
    emit(to_lanes(pieces(mean, 3) + pieces(squares, 3)))
    for copy, _ in sends:
        copy.wait()


def share_kernel(head_width, local_width, got, out, sums_out):
    rows, columns = got.shape
    share = sums_out.shape[0]
    parts = rows // share
    hidden_width = (columns - 5 * head_width - LANES) // 2
    blocks = hidden_width // head_width
    width = parts * local_width

    def take(start, length):
        return got[:, start : start + length].astype(F32).reshape(parts, share, length)

    stats_at = columns - LANES
    stats = take(stats_at, LANES)
    local_mean = from_lanes(stats, 0, 3)
    mean = jnp.sum(local_mean, axis=0, keepdims=True) / parts
    shift = local_mean - mean
    square_sum = jnp.sum(from_lanes(stats, 3, 3) + local_width * shift * shift, axis=0)
    inverse = lax.rsqrt(square_sum / width + EPSILON)
    gain_parts = take(stats_at - head_width, head_width)
    gain_sums = jnp.sum(gain_parts, axis=0)
    sums_out[...] = gain_sums

    def spread(value):
        length = value.shape[1]
        tiled = jnp.broadcast_to(value[None], (parts, share, length))
        return tiled.reshape(rows, length).astype(BF16)

    def projected(block):
        total = jnp.sum(take(block * head_width, head_width), axis=0)
        total = total + jnp.sum(shift * gain_parts[:, block : block + 1, :], axis=0)
        return (inverse * total).astype(BF16).astype(F32)

    back_at = (3 + blocks) * head_width
    for block in range(3):
        out[:, block * head_width : (block + 1) * head_width] = spread(projected(block))
    out[:, 3 * head_width : 4 * head_width] = spread(jnp.sum(take(back_at, head_width), axis=0))
    plain_sum = jnp.zeros((share, 1), F32)
    hat_sum = jnp.zeros((share, 1), F32)
    inner_scale = 0.7978845608028654
    for block in range(blocks):
        pre = projected(3 + block)
        grad_act = jnp.sum(take(back_at + (1 + block) * head_width, head_width), axis=0)
        grad_act = grad_act.astype(BF16).astype(F32)
        squared = pre * pre
        bent = jnp.tanh(inner_scale * (pre + 0.044715 * squared * pre))
        active = 0.5 * pre * (1.0 + bent)
        slope = 0.5 * (1.0 + bent) + 0.5 * pre * (1.0 - bent * bent) * inner_scale * (
            1.0 + 3.0 * 0.044715 * squared
        )
        grad_pre = (grad_act * slope).astype(BF16).astype(F32)
        plain_sum += jnp.sum(grad_pre * gain_sums[3 + block : 4 + block], axis=1, keepdims=True)
        hat_sum += jnp.sum(grad_pre * pre, axis=1, keepdims=True)
        start = (4 + block) * head_width
        out[:, start : start + head_width] = spread(active)
        start += hidden_width
        out[:, start : start + head_width] = spread(grad_pre)
    scalars = pieces(mean[0], 3) + pieces(inverse, 3) + pieces(plain_sum, 2) + pieces(hat_sum, 2)
    out[:, 4 * head_width + 2 * hidden_width :] = spread(to_lanes(scalars))


def attend_kernel(
    full, gain_sums, tokens, ln_gain, query_gain, key_gain, w_qkv, w_hidden, w_attn, w_mlp,
    cotangent, terms, acts,
):
    head_size = query_gain.shape[0]
    query_row, key_row = query_gain[...][None], key_gain[...][None]
    head_width = w_qkv.shape[2]
    hidden_width = w_hidden.shape[1]
    local_width = tokens.shape[1]
    stats = full[:, 4 * head_width + 2 * hidden_width :].astype(F32)
    mean, inverse = from_lanes(stats, 0, 3), from_lanes(stats, 3, 3)
    plain_sum, hat_sum = from_lanes(stats, 6, 2), from_lanes(stats, 8, 2)
    normal_hat = (tokens[...].astype(F32) - mean) * inverse
    acts[:, :local_width] = (normal_hat * ln_gain[...][None]).astype(BF16)
    acts[:, local_width : 2 * local_width] = cotangent[...]
    hidden_at = 4 * head_width
    acts_hidden = 2 * local_width
    acts[:, acts_hidden : acts_hidden + 2 * hidden_width] = full[:, hidden_at : hidden_at + 2 * hidden_width]
    acts_heads = acts_hidden + 2 * hidden_width
    scale = head_size ** (-0.5)

    def normalise(values):
        centred = values - jnp.mean(values, axis=1, keepdims=True)
        root = lax.rsqrt(jnp.mean(centred * centred, axis=1, keepdims=True) + EPSILON)
        return centred * root, root

    def back(grad, hat, root, gain):
        grad = grad * gain
        centred = grad - jnp.mean(grad, axis=1, keepdims=True)
        centred = centred - hat * jnp.mean(grad * hat, axis=1, keepdims=True)
        return (root * centred).astype(BF16)

    for head in range(head_width // head_size):
        low, high = head * head_size, (head + 1) * head_size
        query = full[:, low:high].astype(F32)
        key = full[:, head_width + low : head_width + high].astype(F32)
        value_low = full[:, 2 * head_width + low : 2 * head_width + high]
        grad_mix = full[:, 3 * head_width + low : 3 * head_width + high]
        query_hat, query_root = normalise(query)
        key_hat, key_root = normalise(key)
        query_norm = (query_hat * query_row).astype(BF16)
        key_norm = (key_hat * key_row).astype(BF16)
        scores = dot_last(query_norm, key_norm) * scale
        weights = jnp.exp(scores - jnp.max(scores, axis=1, keepdims=True))
        probs = weights / jnp.sum(weights, axis=1, keepdims=True)
        probs_low = probs.astype(BF16)
        acts[:, acts_heads + low : acts_heads + high] = dot_plain(probs_low, value_low).astype(BF16)
        grad_probs = dot_last(grad_mix, value_low)
        grad_value = dot_first(probs_low, grad_mix).astype(BF16)
        grad_scores = probs * (grad_probs - jnp.sum(grad_probs * probs, axis=1, keepdims=True))
        grad_scores = grad_scores.astype(BF16)
        grad_query = back(
            dot_plain(grad_scores, key_norm) * scale, query_hat, query_root, query_row
        )
        grad_key = back(
            dot_first(grad_scores, query_norm) * scale, key_hat, key_root, key_row
        )
        plain = jnp.zeros_like(query)
        with_hat = jnp.zeros_like(query)
        for part, (grad, pre) in enumerate(
            ((grad_query, query), (grad_key, key), (grad_value, value_low.astype(F32)))
        ):
            start = acts_heads + (1 + part) * head_width
            acts[:, start + low : start + high] = grad
            grad = grad.astype(F32)
            plain = plain + grad * gain_sums[part : part + 1, low:high]
            with_hat = with_hat + grad * pre
        plain_sum = plain_sum + jnp.sum(plain, axis=1, keepdims=True)
        hat_sum = hat_sum + jnp.sum(with_hat, axis=1, keepdims=True)

    mixed = dot_plain(acts[:, acts_heads : acts_heads + head_width], w_attn[...])
    mixed = mixed + dot_plain(full[:, hidden_at : hidden_at + hidden_width], w_mlp[...])
    terms[:, :local_width] = mixed.astype(BF16)
    grad_normed = dot_last(full[:, hidden_at + hidden_width : hidden_at + 2 * hidden_width], w_hidden[...])
    for part in range(3):
        start = acts_heads + (1 + part) * head_width
        grad_normed = grad_normed + dot_last(acts[:, start : start + head_width], w_qkv[part])
    terms[:, local_width : 2 * local_width] = grad_normed.astype(BF16)
    terms[:, 2 * local_width :] = to_lanes(pieces(plain_sum, 2) + pieces(hat_sum, 2)).astype(BF16)


def weight_kernel(
    head_width, hidden_width, n_dp, place, own, peer, here, far, relayed, direct, norm_t, mix_t, act_t,
):
    local_width = norm_t.shape[0]
    hidden_at = 2 * local_width
    heads_at = hidden_at + 2 * hidden_width
    core, chip, chips = place[0] % 2, place[0] // 2, n_dp // 2
    toward = 1 - 2 * core
    outs = (here, far, relayed, direct)
    owners = [2 * ((chip + chips + step) % chips) + core for step in (0, 2, toward, -toward)]

    def both(start, length):
        return jnp.concatenate([own[:, start : start + length], peer[:, start : start + length]], axis=0)

    norm_t[...] = both(0, local_width).T
    mix_t[...] = both(heads_at, head_width).T
    act_t[...] = both(hidden_at, hidden_width).T
    def rows(ref, length):
        return jnp.concatenate(
            [ref[pl.ds(pl.multiple_of(owner * length, 16), length), :] for owner in owners], axis=0
        )

    row = 0

    def emit(left, right):
        nonlocal row
        length = left.shape[0] // len(owners)
        product = dot_plain(left, right)
        for step, out in enumerate(outs):
            out[row : row + length, :] = product[step * length : (step + 1) * length].astype(out.dtype)
        row += length

    norm_rows = rows(norm_t, local_width // n_dp)
    for part in range(3):
        emit(norm_rows, both(heads_at + (1 + part) * head_width, head_width))
    for block in range(hidden_width // head_width):
        emit(norm_rows, both(hidden_at + hidden_width + block * head_width, head_width))
    cotangent = both(local_width, local_width)
    emit(rows(mix_t, head_width // n_dp), cotangent)
    emit(rows(act_t, hidden_width // n_dp), cotangent)


def token_kernel(place, got, full, tokens, ln_gain, cotangent, mixed, grad_tokens):
    out_rows, local_width = mixed.shape
    parts = got.shape[0] // out_rows
    width = place[1]
    first = pl.multiple_of(place[0] * out_rows, 16)

    def total(start, length):
        values = got[:, start : start + length].astype(F32)
        return jnp.sum(values.reshape(parts, out_rows, length), axis=0)

    values = tokens[pl.ds(first, out_rows), :].astype(F32)
    mixed[...] = (values + total(0, local_width)).astype(BF16)
    stats = full[pl.ds(first, out_rows), full.shape[1] - LANES :].astype(F32)
    mean, inverse = from_lanes(stats, 0, 3), from_lanes(stats, 3, 3)
    normal_hat = (values - mean) * inverse
    sums = total(2 * local_width, LANES)
    share = 1.0 / width.astype(F32)
    mean_one, mean_two = from_lanes(sums, 0, 2) * share, from_lanes(sums, 2, 2) * share
    grad_hat = total(local_width, local_width) * ln_gain[...][None]
    grad = inverse * (grad_hat - mean_one - normal_hat * mean_two)
    back = cotangent[pl.ds(first, out_rows), :].astype(F32)
    grad_tokens[...] = (back + grad).astype(BF16)


def sum_kernel(here, relayed, direct, qkv, hidden, attn, mlp):
    def total(start, length):
        value = here[start : start + length, :]
        for part in (relayed, direct):
            value = value + part[start : start + length, :].astype(F32)
        return value

    row = 0
    length, head_width = qkv.shape[2], qkv.shape[3]
    for part in range(3):
        qkv[part, 0] = total(row, length)
        row += length
    for block in range(hidden.shape[2] // head_width):
        hidden[0, :, block * head_width : (block + 1) * head_width] = total(row, length)
        row += length
    attn[0] = total(row, attn.shape[1])
    row += attn.shape[1]
    mlp[0] = total(row, mlp.shape[1])


def exchange(values, axis):
    return lax.all_to_all(values, axis, 0, 0, tiled=True)


def per_device(
    tokens, ln_gain, query_gain, key_gain, w_qkv, w_hidden, w_attn_out, w_mlp_out, cotangent
):
    n_dp, n_mx, n_my = lax.axis_size("dp"), lax.axis_size("mx"), lax.axis_size("my")
    row_count, local_width = tokens.shape
    head_width, hidden_width = w_qkv.shape[2], w_hidden.shape[1]
    width = local_width * n_my
    share, out_rows = row_count // n_my, row_count // n_mx

    weights = (w_qkv, w_hidden, w_attn_out, w_mlp_out)

    def shape(*dims, dtype=BF16):
        return jax.ShapeDtypeStruct(dims, dtype)

    term_width = 5 * head_width + 2 * hidden_width + LANES
    inputs = (tokens, ln_gain, w_qkv, w_hidden, cotangent, w_attn_out, w_mlp_out)
    (terms,) = run(
        lambda *refs: project_kernel(share, *refs),
        inputs,
        (shape(row_count, term_width),),
        scratch=[pltpu.VMEM(array.shape, array.dtype) for array in inputs]
        + [
            pltpu.VMEM((row_count, term_width), BF16),
            pltpu.SemaphoreType.DMA((len(inputs),)),
            pltpu.SemaphoreType.DMA((term_width // head_width + 1,)),
        ],
        fetched=range(len(inputs)),
        written=(0,),
        mebibytes=60,
    )
    got = exchange(terms, "my")
    spread, gain_sums = run(
        lambda *refs: share_kernel(head_width, local_width, *refs),
        (got,),
        (
            shape(row_count, 4 * head_width + 2 * hidden_width + LANES),
            shape(share, head_width, dtype=F32),
        ),
    )
    full = exchange(spread, "my")
    act_width = 2 * local_width + 2 * hidden_width + 4 * head_width
    out_terms, acts = run(
        attend_kernel,
        (
            full, gain_sums, tokens, ln_gain, query_gain, key_gain,
            *weights, cotangent,
        ),
        (shape(row_count, 2 * local_width + LANES), shape(row_count, act_width)),
        mebibytes=16,
    )
    peer_acts = lax.ppermute(acts, "dp", [(source, source ^ 1) for source in range(n_dp)])
    out_got = exchange(out_terms, "mx")
    block_rows = (3 * local_width + local_width * hidden_width // head_width + head_width + hidden_width) // n_dp
    block = shape(block_rows, local_width)
    place = lax.axis_index("dp").reshape(1)
    here, far, relayed, direct = run(
        lambda *refs: weight_kernel(head_width, hidden_width, n_dp, *refs),
        (place, acts, peer_acts),
        (shape(block_rows, local_width, dtype=F32),) + (block,) * 3,
        scratch=(
            pltpu.VMEM((local_width, 2 * row_count), BF16),
            pltpu.VMEM((head_width, 2 * row_count), BF16),
            pltpu.VMEM((hidden_width, 2 * row_count), BF16),
        ),
        scalar=True,
        mebibytes=60,
    )

    def pass_on(values, step):
        ways = [(s, (s + 2 * step * (1 - 2 * (s % 2))) % n_dp) for s in range(n_dp)]
        return lax.ppermute(values, "dp", ways)

    passing = pass_on(far, 1)
    got_direct = pass_on(direct, -1)
    passing, out_got = lax.optimization_barrier((passing, out_got))
    joined = (relayed.astype(F32) + passing.astype(F32)).astype(BF16)
    got_relayed = pass_on(joined, 1)
    place = jnp.stack([lax.axis_index("mx"), jnp.int32(width)])
    mixed, grad_tokens = run(
        token_kernel,
        (place, out_got, full, tokens, ln_gain, cotangent),
        (shape(out_rows, local_width), shape(out_rows, local_width)),
        scalar=True,
    )
    grads = run(
        sum_kernel,
        (here, got_relayed, got_direct),
        (
            shape(3, 1, local_width // n_dp, head_width, dtype=F32),
            shape(1, local_width // n_dp, hidden_width, dtype=F32),
            shape(1, head_width // n_dp, local_width, dtype=F32),
            shape(1, hidden_width // n_dp, local_width, dtype=F32),
        ),
    )
    return (mixed, grad_tokens, *grads)


def solution(mesh):
    placed = (
        P("dp", "my"),
        P("my"),
        P(),
        P(),
        P(None, "my", "mx"),
        P("my", "mx"),
        P("mx", "my"),
        P("mx", "my"),
        P("dp", "my"),
    )
    return jax.shard_map(
        per_device,
        mesh=mesh,
        in_specs=placed,
        out_specs=(
            P(("dp", "mx"), "my"),
            P(("dp", "mx"), "my"),
            P(None, "my", "dp", "mx"),
            P("my", "dp", "mx"),
            P("mx", "dp", "my"),
            P("mx", "dp", "my"),
        ),
        check_vma=False,
    )
```

```python
import jax
import jax.numpy as jnp
from jax import lax
from jax.experimental import pallas as pl
from jax.experimental.pallas import tpu as pltpu
from jax.sharding import PartitionSpec as P

EPSILON = 1e-06
LANES = 128
BF16 = jnp.bfloat16
F32 = jnp.float32


def dot_plain(matrix_a, matrix_b):
    return jnp.dot(matrix_a, matrix_b, preferred_element_type=F32)


def dot_first(matrix_a, matrix_b):
    return lax.dot_general(matrix_a, matrix_b, (((0,), (0,)), ((), ())), preferred_element_type=F32)


def dot_last(matrix_a, matrix_b):
    return lax.dot_general(matrix_a, matrix_b, (((1,), (1,)), ((), ())), preferred_element_type=F32)


def pieces(value, count):
    out = []
    for _ in range(count):
        part = value.astype(BF16).astype(F32)
        out.append(part)
        value = value - part
    return out


def to_lanes(columns):
    rows = columns[0].shape[0]
    lane = lax.broadcasted_iota(jnp.int32, (rows, LANES), 1)
    block = jnp.zeros((rows, LANES), F32)
    for index, column in enumerate(columns):
        block = jnp.where(lane == index, column, block)
    return block


def from_lanes(block, first, count):
    lane = lax.broadcasted_iota(jnp.int32, block.shape, block.ndim - 1)
    keep = (lane >= first) & (lane < first + count)
    return jnp.sum(jnp.where(keep, block, 0.0), axis=-1, keepdims=True)


def run(kernel, operands, out_shape, scratch=(), scalar=False, fetched=(), written=(), mebibytes=16):
    in_specs = [pl.BlockSpec(memory_space=pltpu.VMEM)] * len(operands)
    out_specs = [pl.BlockSpec(memory_space=pltpu.VMEM)] * len(out_shape)
    if scalar:
        in_specs[0] = pl.BlockSpec(memory_space=pltpu.SMEM)
    for index in fetched:
        in_specs[index] = pl.BlockSpec(memory_space=pltpu.HBM)
    for index in written:
        out_specs[index] = pl.BlockSpec(memory_space=pltpu.HBM)
    return pl.pallas_call(
        kernel,
        in_specs=in_specs,
        out_specs=out_specs,
        out_shape=out_shape,
        scratch_shapes=list(scratch),
        compiler_params=pltpu.CompilerParams(vmem_limit_bytes=mebibytes * 1024 * 1024),
    )(*operands)


def project_kernel(share, *refs):
    far, out_far, near, out, arrived, left_for = refs[:7], refs[7], refs[8:15], refs[15], refs[16], refs[17]
    tokens, ln_gain, w_qkv, w_hidden, cotangent, w_attn, w_mlp = near
    rows, width = tokens.shape
    head_width = w_qkv.shape[2]
    blocks = w_hidden.shape[1] // head_width
    loads = [
        pltpu.make_async_copy(source, target, arrived.at[index])
        for index, (source, target) in enumerate(zip(far, near))
    ]
    for load in loads:
        load.start()
    sends = []

    def emit(values):
        columns = pl.ds(sum(send[1] for send in sends), values.shape[1])
        out[:, columns] = values.astype(BF16)
        copy = pltpu.make_async_copy(out.at[:, columns], out_far.at[:, columns], left_for.at[len(sends)])
        copy.start()
        sends.append((copy, values.shape[1]))

    loads[0].wait()
    loads[1].wait()
    values = tokens[...].astype(F32)
    mean = jnp.sum(values, axis=1, keepdims=True) / width
    centred = values - mean
    squares = jnp.sum(centred * centred, axis=1, keepdims=True)
    gain = ln_gain[...][None]
    scaled = (centred * gain).astype(BF16)
    high, low = pieces(gain, 2)
    row_id = lax.broadcasted_iota(jnp.int32, (16, width), 0)
    gain_rows = jnp.where(row_id == 0, high, jnp.where(row_id == 1, low, 0.0)).astype(BF16)
    left = jnp.concatenate([scaled, gain_rows], axis=0)
    share_id = lax.broadcasted_iota(jnp.int32, (share, head_width), 0)
    gain_sums = jnp.zeros((share, head_width), F32)
    for block in range(3 + blocks):
        if block == 0 or block == 3:
            loads[2 + block // 3].wait()
        if block < 3:
            weight = w_qkv[block]
        else:
            weight = w_hidden[:, (block - 3) * head_width : (block - 2) * head_width]
        product = dot_plain(left, weight)
        emit(product[:rows])
        both = product[rows : rows + 1] + product[rows + 1 : rows + 2]
        gain_sums = jnp.where(share_id == block, both, gain_sums)
    loads[4].wait()
    loads[5].wait()
    back = cotangent[...]
    emit(dot_last(back, w_attn[...]))
    loads[6].wait()
    for block in range(blocks):
        emit(dot_last(back, w_mlp[block * head_width : (block + 1) * head_width, :]))
    spread = jnp.broadcast_to(gain_sums[None], (rows // share, share, head_width))
    emit(spread.reshape(rows, head_width))
    emit(to_lanes(pieces(mean, 3) + pieces(squares, 3)))
    for copy, _ in sends:
        copy.wait()


def share_kernel(head_width, local_width, got, out, sums_out):
    rows, columns = got.shape
    share = sums_out.shape[0]
    parts = rows // share
    hidden_width = (columns - 5 * head_width - LANES) // 2
    blocks = hidden_width // head_width
    width = parts * local_width

    def take(start, length):
        return got[:, start : start + length].astype(F32).reshape(parts, share, length)

    stats_at = columns - LANES
    stats = take(stats_at, LANES)
    local_mean = from_lanes(stats, 0, 3)
    mean = jnp.sum(local_mean, axis=0, keepdims=True) / parts
    shift = local_mean - mean
    square_sum = jnp.sum(from_lanes(stats, 3, 3) + local_width * shift * shift, axis=0)
    inverse = lax.rsqrt(square_sum / width + EPSILON)
    gain_parts = take(stats_at - head_width, head_width)
    gain_sums = jnp.sum(gain_parts, axis=0)
    sums_out[...] = gain_sums

    def spread(value):
        length = value.shape[1]
        tiled = jnp.broadcast_to(value[None], (parts, share, length))
        return tiled.reshape(rows, length).astype(BF16)

    def projected(block):
        total = jnp.sum(take(block * head_width, head_width), axis=0)
        total = total + jnp.sum(shift * gain_parts[:, block : block + 1, :], axis=0)
        return (inverse * total).astype(BF16).astype(F32)

    back_at = (3 + blocks) * head_width
    for block in range(3):
        out[:, block * head_width : (block + 1) * head_width] = spread(projected(block))
    out[:, 3 * head_width : 4 * head_width] = spread(jnp.sum(take(back_at, head_width), axis=0))
    plain_sum = jnp.zeros((share, 1), F32)
    hat_sum = jnp.zeros((share, 1), F32)
    inner_scale = 0.7978845608028654
    for block in range(blocks):
        pre = projected(3 + block)
        grad_act = jnp.sum(take(back_at + (1 + block) * head_width, head_width), axis=0)
        grad_act = grad_act.astype(BF16).astype(F32)
        squared = pre * pre
        bent = jnp.tanh(inner_scale * (pre + 0.044715 * squared * pre))
        active = 0.5 * pre * (1.0 + bent)
        slope = 0.5 * (1.0 + bent) + 0.5 * pre * (1.0 - bent * bent) * inner_scale * (
            1.0 + 3.0 * 0.044715 * squared
        )
        grad_pre = (grad_act * slope).astype(BF16).astype(F32)
        plain_sum += jnp.sum(grad_pre * gain_sums[3 + block : 4 + block], axis=1, keepdims=True)
        hat_sum += jnp.sum(grad_pre * pre, axis=1, keepdims=True)
        start = (4 + block) * head_width
        out[:, start : start + head_width] = spread(active)
        start += hidden_width
        out[:, start : start + head_width] = spread(grad_pre)
    scalars = pieces(mean[0], 3) + pieces(inverse, 3) + pieces(plain_sum, 2) + pieces(hat_sum, 2)
    out[:, 4 * head_width + 2 * hidden_width :] = spread(to_lanes(scalars))


def attend_kernel(
    full, gain_sums, tokens, ln_gain, query_gain, key_gain, w_qkv, w_hidden, w_attn, w_mlp,
    cotangent, terms, acts,
):
    head_size = query_gain.shape[0]
    query_row, key_row = query_gain[...][None], key_gain[...][None]
    head_width = w_qkv.shape[2]
    hidden_width = w_hidden.shape[1]
    local_width = tokens.shape[1]
    stats = full[:, 4 * head_width + 2 * hidden_width :].astype(F32)
    mean, inverse = from_lanes(stats, 0, 3), from_lanes(stats, 3, 3)
    plain_sum, hat_sum = from_lanes(stats, 6, 2), from_lanes(stats, 8, 2)
    normal_hat = (tokens[...].astype(F32) - mean) * inverse
    acts[:, :local_width] = (normal_hat * ln_gain[...][None]).astype(BF16)
    acts[:, local_width : 2 * local_width] = cotangent[...]
    hidden_at = 4 * head_width
    acts_hidden = 2 * local_width
    acts[:, acts_hidden : acts_hidden + 2 * hidden_width] = full[:, hidden_at : hidden_at + 2 * hidden_width]
    acts_heads = acts_hidden + 2 * hidden_width
    scale = head_size ** (-0.5)

    def normalise(values):
        centred = values - jnp.mean(values, axis=1, keepdims=True)
        root = lax.rsqrt(jnp.mean(centred * centred, axis=1, keepdims=True) + EPSILON)
        return centred * root, root

    def back(grad, hat, root, gain):
        grad = grad * gain
        centred = grad - jnp.mean(grad, axis=1, keepdims=True)
        centred = centred - hat * jnp.mean(grad * hat, axis=1, keepdims=True)
        return (root * centred).astype(BF16)

    for head in range(head_width // head_size):
        low, high = head * head_size, (head + 1) * head_size
        query = full[:, low:high].astype(F32)
        key = full[:, head_width + low : head_width + high].astype(F32)
        value_low = full[:, 2 * head_width + low : 2 * head_width + high]
        grad_mix = full[:, 3 * head_width + low : 3 * head_width + high]
        query_hat, query_root = normalise(query)
        key_hat, key_root = normalise(key)
        query_norm = (query_hat * query_row).astype(BF16)
        key_norm = (key_hat * key_row).astype(BF16)
        scores = dot_last(query_norm, key_norm) * scale
        weights = jnp.exp(scores - jnp.max(scores, axis=1, keepdims=True))
        probs = weights / jnp.sum(weights, axis=1, keepdims=True)
        probs_low = probs.astype(BF16)
        acts[:, acts_heads + low : acts_heads + high] = dot_plain(probs_low, value_low).astype(BF16)
        grad_probs = dot_last(grad_mix, value_low)
        grad_value = dot_first(probs_low, grad_mix).astype(BF16)
        grad_scores = probs * (grad_probs - jnp.sum(grad_probs * probs, axis=1, keepdims=True))
        grad_scores = grad_scores.astype(BF16)
        grad_query = back(
            dot_plain(grad_scores, key_norm) * scale, query_hat, query_root, query_row
        )
        grad_key = back(
            dot_first(grad_scores, query_norm) * scale, key_hat, key_root, key_row
        )
        plain = jnp.zeros_like(query)
        with_hat = jnp.zeros_like(query)
        for part, (grad, pre) in enumerate(
            ((grad_query, query), (grad_key, key), (grad_value, value_low.astype(F32)))
        ):
            start = acts_heads + (1 + part) * head_width
            acts[:, start + low : start + high] = grad
            grad = grad.astype(F32)
            plain = plain + grad * gain_sums[part : part + 1, low:high]
            with_hat = with_hat + grad * pre
        plain_sum = plain_sum + jnp.sum(plain, axis=1, keepdims=True)
        hat_sum = hat_sum + jnp.sum(with_hat, axis=1, keepdims=True)

    mixed = dot_plain(acts[:, acts_heads : acts_heads + head_width], w_attn[...])
    mixed = mixed + dot_plain(full[:, hidden_at : hidden_at + hidden_width], w_mlp[...])
    terms[:, :local_width] = mixed.astype(BF16)
    grad_normed = dot_last(full[:, hidden_at + hidden_width : hidden_at + 2 * hidden_width], w_hidden[...])
    for part in range(3):
        start = acts_heads + (1 + part) * head_width
        grad_normed = grad_normed + dot_last(acts[:, start : start + head_width], w_qkv[part])
    terms[:, local_width : 2 * local_width] = grad_normed.astype(BF16)
    terms[:, 2 * local_width :] = to_lanes(pieces(plain_sum, 2) + pieces(hat_sum, 2)).astype(BF16)


def weight_kernel(
    head_width, hidden_width, n_dp, place, own, peer, here_far, far_far, relayed_far, direct_far,
    acts, norm_t, mix_t, act_t, here, far, relayed, direct, arrived, left_for,
):
    row_count, local_width = own.shape[0], norm_t.shape[0]
    hidden_at = 2 * local_width
    heads_at = hidden_at + 2 * hidden_width
    core, chip, chips = place[0] % 2, place[0] // 2, n_dp // 2
    toward = 1 - 2 * core
    outs = (far, relayed, direct, here)
    outs_far = (far_far, relayed_far, direct_far, here_far)
    owners = [2 * ((chip + chips + step) % chips) + core for step in (2, toward, -toward, 0)]
    spans = (
        (0, local_width),
        (heads_at + head_width, 3 * head_width),
        (hidden_at + hidden_width, hidden_width),
        (hidden_at, hidden_width),
        (local_width, local_width),
        (heads_at, head_width),
    )
    loads = []
    for index, (start, length) in enumerate(spans):
        columns = pl.ds(start, length)
        for side, source in enumerate((own, peer)):
            target = acts.at[pl.ds(side * row_count, row_count), columns]
            load = pltpu.make_async_copy(source.at[:, columns], target, arrived.at[2 * index + side])
            load.start()
            loads.append(load)

    def ready(index):
        loads[2 * index].wait()
        loads[2 * index + 1].wait()

    def both(start, length):
        return acts[:, start : start + length]

    def rows(ref, length):
        return jnp.concatenate(
            [ref[pl.ds(pl.multiple_of(owner * length, 16), length), :] for owner in owners], axis=0
        )

    row, sent, sends = 0, 0, []

    def emit(left, right):
        nonlocal row
        length = left.shape[0] // len(owners)
        product = dot_plain(left, right)
        for step, out in enumerate(outs):
            out[row : row + length, :] = product[step * length : (step + 1) * length].astype(out.dtype)
        row += length

    def send():
        nonlocal sent
        part = pl.ds(sent, row - sent)
        for out, out_far in zip(outs, outs_far):
            copy = pltpu.make_async_copy(out.at[part, :], out_far.at[part, :], left_for.at[len(sends)])
            copy.start()
            sends.append(copy)
        sent = row

    ready(0)
    norm_t[...] = both(0, local_width).T
    norm_rows = rows(norm_t, local_width // n_dp)
    ready(1)
    for part in range(3):
        emit(norm_rows, both(heads_at + (1 + part) * head_width, head_width))
    send()
    ready(2)
    for block in range(hidden_width // head_width):
        emit(norm_rows, both(hidden_at + hidden_width + block * head_width, head_width))
    send()
    for index in (3, 4, 5):
        ready(index)
    mix_t[...] = both(heads_at, head_width).T
    act_t[...] = both(hidden_at, hidden_width).T
    cotangent = both(local_width, local_width)
    emit(rows(mix_t, head_width // n_dp), cotangent)
    emit(rows(act_t, hidden_width // n_dp), cotangent)
    send()
    for copy in sends:
        copy.wait()


def token_kernel(place, got, full, tokens, ln_gain, cotangent, mixed, grad_tokens):
    out_rows, local_width = mixed.shape
    parts = got.shape[0] // out_rows
    width = place[1]
    first = pl.multiple_of(place[0] * out_rows, 16)

    def total(start, length):
        values = got[:, start : start + length].astype(F32)
        return jnp.sum(values.reshape(parts, out_rows, length), axis=0)

    values = tokens[pl.ds(first, out_rows), :].astype(F32)
    mixed[...] = (values + total(0, local_width)).astype(BF16)
    stats = full[pl.ds(first, out_rows), full.shape[1] - LANES :].astype(F32)
    mean, inverse = from_lanes(stats, 0, 3), from_lanes(stats, 3, 3)
    normal_hat = (values - mean) * inverse
    sums = total(2 * local_width, LANES)
    share = 1.0 / width.astype(F32)
    mean_one, mean_two = from_lanes(sums, 0, 2) * share, from_lanes(sums, 2, 2) * share
    grad_hat = total(local_width, local_width) * ln_gain[...][None]
    grad = inverse * (grad_hat - mean_one - normal_hat * mean_two)
    back = cotangent[pl.ds(first, out_rows), :].astype(F32)
    grad_tokens[...] = (back + grad).astype(BF16)


def sum_kernel(
    here, relayed, direct, qkv_far, hidden_far, attn_far, mlp_far, qkv, hidden, attn, mlp, left_for
):
    length, head_width = qkv.shape[2], qkv.shape[3]
    blocks = hidden.shape[2] // head_width
    cuts = (0, 3 * length, (3 + blocks) * length, here.shape[0])

    def total(start, count):
        value = here[start : start + count, :]
        for part in (relayed, direct):
            value = value + part[start : start + count, :].astype(F32)
        return value

    sends = []

    def send(source, target):
        copy = pltpu.make_async_copy(source, target, left_for.at[len(sends)])
        copy.start()
        sends.append(copy)

    for part in range(3):
        qkv[part, 0] = total(part * length, length)
    send(qkv, qkv_far)
    for block in range(blocks):
        columns = slice(block * head_width, (block + 1) * head_width)
        hidden[0, :, columns] = total(cuts[1] + block * length, length)
    send(hidden, hidden_far)
    attn[0] = total(cuts[2], attn.shape[1])
    send(attn, attn_far)
    mlp[0] = total(cuts[2] + attn.shape[1], mlp.shape[1])
    send(mlp, mlp_far)
    for copy in sends:
        copy.wait()


def exchange(values, axis):
    return lax.all_to_all(values, axis, 0, 0, tiled=True)


def per_device(
    tokens, ln_gain, query_gain, key_gain, w_qkv, w_hidden, w_attn_out, w_mlp_out, cotangent
):
    n_dp, n_mx, n_my = lax.axis_size("dp"), lax.axis_size("mx"), lax.axis_size("my")
    row_count, local_width = tokens.shape
    head_width, hidden_width = w_qkv.shape[2], w_hidden.shape[1]
    width = local_width * n_my
    share, out_rows = row_count // n_my, row_count // n_mx

    weights = (w_qkv, w_hidden, w_attn_out, w_mlp_out)

    def shape(*dims, dtype=BF16):
        return jax.ShapeDtypeStruct(dims, dtype)

    term_width = 5 * head_width + 2 * hidden_width + LANES
    inputs = (tokens, ln_gain, w_qkv, w_hidden, cotangent, w_attn_out, w_mlp_out)
    (terms,) = run(
        lambda *refs: project_kernel(share, *refs),
        inputs,
        (shape(row_count, term_width),),
        scratch=[pltpu.VMEM(array.shape, array.dtype) for array in inputs]
        + [
            pltpu.VMEM((row_count, term_width), BF16),
            pltpu.SemaphoreType.DMA((len(inputs),)),
            pltpu.SemaphoreType.DMA((term_width // head_width + 1,)),
        ],
        fetched=range(len(inputs)),
        written=(0,),
        mebibytes=60,
    )
    got = exchange(terms, "my")
    spread, gain_sums = run(
        lambda *refs: share_kernel(head_width, local_width, *refs),
        (got,),
        (
            shape(row_count, 4 * head_width + 2 * hidden_width + LANES),
            shape(share, head_width, dtype=F32),
        ),
    )
    full = exchange(spread, "my")
    act_width = 2 * local_width + 2 * hidden_width + 4 * head_width
    out_terms, acts = run(
        attend_kernel,
        (
            full, gain_sums, tokens, ln_gain, query_gain, key_gain,
            *weights, cotangent,
        ),
        (shape(row_count, 2 * local_width + LANES), shape(row_count, act_width)),
        mebibytes=16,
    )
    peer_acts = lax.ppermute(acts, "dp", [(source, source ^ 1) for source in range(n_dp)])
    out_got = exchange(out_terms, "mx")
    block_rows = (3 * local_width + local_width * hidden_width // head_width + head_width + hidden_width) // n_dp
    block = shape(block_rows, local_width)
    place = lax.axis_index("dp").reshape(1)
    weight_outs = (shape(block_rows, local_width, dtype=F32),) + (block,) * 3
    here, far, relayed, direct = run(
        lambda *refs: weight_kernel(head_width, hidden_width, n_dp, *refs),
        (place, acts, peer_acts),
        weight_outs,
        scratch=[
            pltpu.VMEM((2 * row_count, act_width), BF16),
            pltpu.VMEM((local_width, 2 * row_count), BF16),
            pltpu.VMEM((head_width, 2 * row_count), BF16),
            pltpu.VMEM((hidden_width, 2 * row_count), BF16),
            *(pltpu.VMEM(out.shape, out.dtype) for out in weight_outs),
            pltpu.SemaphoreType.DMA((12,)),
            pltpu.SemaphoreType.DMA((12,)),
        ],
        scalar=True,
        fetched=(1, 2),
        written=(0, 1, 2, 3),
        mebibytes=60,
    )

    def pass_on(values, step):
        ways = [(s, (s + 2 * step * (1 - 2 * (s % 2))) % n_dp) for s in range(n_dp)]
        return lax.ppermute(values, "dp", ways)

    passing = pass_on(far, 1)
    got_direct = pass_on(direct, -1)
    joined = (relayed.astype(F32) + passing.astype(F32)).astype(BF16)
    joined, out_got = lax.optimization_barrier((joined, out_got))
    got_relayed = pass_on(joined, 1)
    place = jnp.stack([lax.axis_index("mx"), jnp.int32(width)])
    mixed, grad_tokens = run(
        token_kernel,
        (place, out_got, full, tokens, ln_gain, cotangent),
        (shape(out_rows, local_width), shape(out_rows, local_width)),
        scalar=True,
    )
    grad_shapes = (
        shape(3, 1, local_width // n_dp, head_width, dtype=F32),
        shape(1, local_width // n_dp, hidden_width, dtype=F32),
        shape(1, head_width // n_dp, local_width, dtype=F32),
        shape(1, hidden_width // n_dp, local_width, dtype=F32),
    )
    grads = run(
        sum_kernel,
        (here, got_relayed, got_direct),
        grad_shapes,
        scratch=[pltpu.VMEM(grad.shape, grad.dtype) for grad in grad_shapes] + [pltpu.SemaphoreType.DMA((4,))],
        written=(0, 1, 2, 3),
    )
    return (mixed, grad_tokens, *grads)


def solution(mesh):
    placed = (
        P("dp", "my"),
        P("my"),
        P(),
        P(),
        P(None, "my", "mx"),
        P("my", "mx"),
        P("mx", "my"),
        P("mx", "my"),
        P("dp", "my"),
    )
    return jax.shard_map(
        per_device,
        mesh=mesh,
        in_specs=placed,
        out_specs=(
            P(("dp", "mx"), "my"),
            P(("dp", "mx"), "my"),
            P(None, "my", "dp", "mx"),
            P("my", "dp", "mx"),
            P("mx", "dp", "my"),
            P("mx", "dp", "my"),
        ),
        check_vma=False,
    )
```

```python
import jax
import jax.numpy as jnp
from jax import lax
from jax.experimental import pallas as pl
from jax.experimental.pallas import tpu as pltpu
from jax.sharding import PartitionSpec as P

EPSILON = 1e-06
LANES = 128
BF16 = jnp.bfloat16
F32 = jnp.float32


def dot_plain(matrix_a, matrix_b):
    return jnp.dot(matrix_a, matrix_b, preferred_element_type=F32)


def dot_first(matrix_a, matrix_b):
    return lax.dot_general(matrix_a, matrix_b, (((0,), (0,)), ((), ())), preferred_element_type=F32)


def dot_last(matrix_a, matrix_b):
    return lax.dot_general(matrix_a, matrix_b, (((1,), (1,)), ((), ())), preferred_element_type=F32)


def pieces(value, count):
    out = []
    for _ in range(count):
        part = value.astype(BF16).astype(F32)
        out.append(part)
        value = value - part
    return out


def to_lanes(columns):
    rows = columns[0].shape[0]
    lane = lax.broadcasted_iota(jnp.int32, (rows, LANES), 1)
    block = jnp.zeros((rows, LANES), F32)
    for index, column in enumerate(columns):
        block = jnp.where(lane == index, column, block)
    return block


def from_lanes(block, first, count):
    lane = lax.broadcasted_iota(jnp.int32, block.shape, block.ndim - 1)
    keep = (lane >= first) & (lane < first + count)
    return jnp.sum(jnp.where(keep, block, 0.0), axis=-1, keepdims=True)


def run(kernel, operands, out_shape, scratch=(), scalar=False, fetched=(), written=(), mebibytes=16):
    in_specs = [pl.BlockSpec(memory_space=pltpu.VMEM)] * len(operands)
    out_specs = [pl.BlockSpec(memory_space=pltpu.VMEM)] * len(out_shape)
    if scalar:
        in_specs[0] = pl.BlockSpec(memory_space=pltpu.SMEM)
    for index in fetched:
        in_specs[index] = pl.BlockSpec(memory_space=pltpu.HBM)
    for index in written:
        out_specs[index] = pl.BlockSpec(memory_space=pltpu.HBM)
    return pl.pallas_call(
        kernel,
        in_specs=in_specs,
        out_specs=out_specs,
        out_shape=out_shape,
        scratch_shapes=list(scratch),
        compiler_params=pltpu.CompilerParams(vmem_limit_bytes=mebibytes * 1024 * 1024),
    )(*operands)


def project_kernel(share, *refs):
    far, out_far, near, out, arrived, left_for = refs[:7], refs[7], refs[8:15], refs[15], refs[16], refs[17]
    tokens, ln_gain, w_qkv, w_hidden, cotangent, w_attn, w_mlp = near
    rows, width = tokens.shape
    head_width = w_qkv.shape[2]
    blocks = w_hidden.shape[1] // head_width
    loads = [
        pltpu.make_async_copy(source, target, arrived.at[index])
        for index, (source, target) in enumerate(zip(far, near))
    ]
    for load in loads:
        load.start()
    sends = []

    def emit(values):
        columns = pl.ds(sum(send[1] for send in sends), values.shape[1])
        out[:, columns] = values.astype(BF16)
        copy = pltpu.make_async_copy(out.at[:, columns], out_far.at[:, columns], left_for.at[len(sends)])
        copy.start()
        sends.append((copy, values.shape[1]))

    loads[0].wait()
    loads[1].wait()
    values = tokens[...].astype(F32)
    mean = jnp.sum(values, axis=1, keepdims=True) / width
    centred = values - mean
    squares = jnp.sum(centred * centred, axis=1, keepdims=True)
    gain = ln_gain[...][None]
    scaled = (centred * gain).astype(BF16)
    high, low = pieces(gain, 2)
    row_id = lax.broadcasted_iota(jnp.int32, (16, width), 0)
    gain_rows = jnp.where(row_id == 0, high, jnp.where(row_id == 1, low, 0.0)).astype(BF16)
    left = jnp.concatenate([scaled, gain_rows], axis=0)
    share_id = lax.broadcasted_iota(jnp.int32, (share, head_width), 0)
    gain_sums = jnp.zeros((share, head_width), F32)
    for block in range(3 + blocks):
        if block == 0 or block == 3:
            loads[2 + block // 3].wait()
        if block < 3:
            weight = w_qkv[block]
        else:
            weight = w_hidden[:, (block - 3) * head_width : (block - 2) * head_width]
        product = dot_plain(left, weight)
        emit(product[:rows])
        both = product[rows : rows + 1] + product[rows + 1 : rows + 2]
        gain_sums = jnp.where(share_id == block, both, gain_sums)
    loads[4].wait()
    loads[5].wait()
    back = cotangent[...]
    emit(dot_last(back, w_attn[...]))
    loads[6].wait()
    for block in range(blocks):
        emit(dot_last(back, w_mlp[block * head_width : (block + 1) * head_width, :]))
    stats = pieces(mean, 3) + pieces(squares, 3)
    lane = lax.broadcasted_iota(jnp.int32, (rows, head_width), 1)
    token = lax.broadcasted_iota(jnp.int32, (rows, head_width), 0) % share
    block = jnp.zeros((rows, head_width), F32)
    for index, value in enumerate(stats):
        block = jnp.where(lane == token * len(stats) + index, value, block)
    row = jnp.sum(block.reshape(rows // share, share, head_width), axis=1, keepdims=True)
    spread = jnp.where(share_id[None] == share - 1, row, gain_sums[None])
    emit(spread.reshape(rows, head_width))
    for copy, _ in sends:
        copy.wait()


def share_kernel(head_width, local_width, got, out, sums_out):
    rows, columns = got.shape
    share = sums_out.shape[0]
    parts = rows // share
    hidden_width = (columns - 5 * head_width) // 2
    blocks = hidden_width // head_width
    width = parts * local_width

    def take(start, length):
        return got[:, start : start + length].astype(F32).reshape(parts, share, length)

    gain_parts = take(columns - head_width, head_width)
    stats = jnp.broadcast_to(gain_parts[:, share - 1 : share, :], gain_parts.shape)
    lane = lax.broadcasted_iota(jnp.int32, stats.shape, 2)
    first = lax.broadcasted_iota(jnp.int32, stats.shape, 1) * 6

    def stat(offset):
        keep = (lane >= first + offset) & (lane < first + offset + 3)
        return jnp.sum(jnp.where(keep, stats, 0.0), axis=2, keepdims=True)

    local_mean = stat(0)
    mean = jnp.sum(local_mean, axis=0, keepdims=True) / parts
    shift = local_mean - mean
    square_sum = jnp.sum(stat(3) + local_width * shift * shift, axis=0)
    inverse = lax.rsqrt(square_sum / width + EPSILON)
    gain_sums = jnp.sum(gain_parts, axis=0)
    sums_out[...] = gain_sums

    def spread(value):
        length = value.shape[1]
        tiled = jnp.broadcast_to(value[None], (parts, share, length))
        return tiled.reshape(rows, length).astype(BF16)

    def projected(block):
        total = jnp.sum(take(block * head_width, head_width), axis=0)
        total = total + jnp.sum(shift * gain_parts[:, block : block + 1, :], axis=0)
        return (inverse * total).astype(BF16).astype(F32)

    back_at = (3 + blocks) * head_width
    for block in range(3):
        out[:, block * head_width : (block + 1) * head_width] = spread(projected(block))
    out[:, 3 * head_width : 4 * head_width] = spread(jnp.sum(take(back_at, head_width), axis=0))
    plain_sum = jnp.zeros((share, 1), F32)
    hat_sum = jnp.zeros((share, 1), F32)
    inner_scale = 0.7978845608028654
    for block in range(blocks):
        pre = projected(3 + block)
        grad_act = jnp.sum(take(back_at + (1 + block) * head_width, head_width), axis=0)
        grad_act = grad_act.astype(BF16).astype(F32)
        squared = pre * pre
        bent = jnp.tanh(inner_scale * (pre + 0.044715 * squared * pre))
        active = 0.5 * pre * (1.0 + bent)
        slope = 0.5 * (1.0 + bent) + 0.5 * pre * (1.0 - bent * bent) * inner_scale * (
            1.0 + 3.0 * 0.044715 * squared
        )
        grad_pre = (grad_act * slope).astype(BF16).astype(F32)
        plain_sum += jnp.sum(grad_pre * gain_sums[3 + block : 4 + block], axis=1, keepdims=True)
        hat_sum += jnp.sum(grad_pre * pre, axis=1, keepdims=True)
        start = (4 + block) * head_width
        out[:, start : start + head_width] = spread(active)
        start += hidden_width
        out[:, start : start + head_width] = spread(grad_pre)
    scalars = pieces(mean[0], 3) + pieces(inverse, 3) + pieces(plain_sum, 2) + pieces(hat_sum, 2)
    out[:, 4 * head_width + 2 * hidden_width :] = spread(to_lanes(scalars))


def attend_kernel(
    head_width, hidden_width, full, gain_sums, tokens, ln_gain, query_gain, key_gain, cotangent, acts
):
    head_size = query_gain.shape[0]
    query_row, key_row = query_gain[...][None], key_gain[...][None]
    local_width = tokens.shape[1]
    stats = full[:, 4 * head_width + 2 * hidden_width :].astype(F32)
    mean, inverse = from_lanes(stats, 0, 3), from_lanes(stats, 3, 3)
    plain_sum, hat_sum = from_lanes(stats, 6, 2), from_lanes(stats, 8, 2)
    normal_hat = (tokens[...].astype(F32) - mean) * inverse
    acts[:, :local_width] = (normal_hat * ln_gain[...][None]).astype(BF16)
    acts[:, local_width : 2 * local_width] = cotangent[...]
    hidden_at = 4 * head_width
    acts_hidden = 2 * local_width
    acts[:, acts_hidden : acts_hidden + 2 * hidden_width] = full[:, hidden_at : hidden_at + 2 * hidden_width]
    acts_heads = acts_hidden + 2 * hidden_width
    scale = head_size ** (-0.5)

    def normalise(values):
        centred = values - jnp.mean(values, axis=1, keepdims=True)
        root = lax.rsqrt(jnp.mean(centred * centred, axis=1, keepdims=True) + EPSILON)
        return centred * root, root

    def back(grad, hat, root, gain):
        grad = grad * gain
        centred = grad - jnp.mean(grad, axis=1, keepdims=True)
        centred = centred - hat * jnp.mean(grad * hat, axis=1, keepdims=True)
        return (root * centred).astype(BF16)

    for head in range(head_width // head_size):
        low, high = head * head_size, (head + 1) * head_size
        query = full[:, low:high].astype(F32)
        key = full[:, head_width + low : head_width + high].astype(F32)
        value_low = full[:, 2 * head_width + low : 2 * head_width + high]
        grad_mix = full[:, 3 * head_width + low : 3 * head_width + high]
        query_hat, query_root = normalise(query)
        key_hat, key_root = normalise(key)
        query_norm = (query_hat * query_row).astype(BF16)
        key_norm = (key_hat * key_row).astype(BF16)
        scores = dot_last(query_norm, key_norm) * scale
        weights = jnp.exp(scores - jnp.max(scores, axis=1, keepdims=True))
        probs = weights / jnp.sum(weights, axis=1, keepdims=True)
        probs_low = probs.astype(BF16)
        acts[:, acts_heads + low : acts_heads + high] = dot_plain(probs_low, value_low).astype(BF16)
        grad_probs = dot_last(grad_mix, value_low)
        grad_value = dot_first(probs_low, grad_mix).astype(BF16)
        grad_scores = probs * (grad_probs - jnp.sum(grad_probs * probs, axis=1, keepdims=True))
        grad_scores = grad_scores.astype(BF16)
        grad_query = back(
            dot_plain(grad_scores, key_norm) * scale, query_hat, query_root, query_row
        )
        grad_key = back(
            dot_first(grad_scores, query_norm) * scale, key_hat, key_root, key_row
        )
        plain = jnp.zeros_like(query)
        with_hat = jnp.zeros_like(query)
        for part, (grad, pre) in enumerate(
            ((grad_query, query), (grad_key, key), (grad_value, value_low.astype(F32)))
        ):
            start = acts_heads + (1 + part) * head_width
            acts[:, start + low : start + high] = grad
            grad = grad.astype(F32)
            plain = plain + grad * gain_sums[part : part + 1, low:high]
            with_hat = with_hat + grad * pre
        plain_sum = plain_sum + jnp.sum(plain, axis=1, keepdims=True)
        hat_sum = hat_sum + jnp.sum(with_hat, axis=1, keepdims=True)

    acts[:, acts_heads + 4 * head_width :] = to_lanes(pieces(plain_sum, 2) + pieces(hat_sum, 2)).astype(BF16)


def terms_kernel(
    acts_far, w_mlp_far, w_hidden_far, w_attn_far, w_qkv_far, terms,
    acts, w_mlp, w_hidden, w_attn, w_qkv, arrived,
):
    head_width = w_qkv.shape[2]
    hidden_width, local_width = w_mlp.shape
    hidden_at = 2 * local_width
    heads_at = hidden_at + 2 * hidden_width
    loads = []

    def load(source, target):
        copy = pltpu.make_async_copy(source, target, arrived.at[len(loads)])
        copy.start()
        loads.append(copy)

    def load_acts(start, length):
        load(acts_far.at[:, pl.ds(start, length)], acts.at[:, pl.ds(start, length)])

    load_acts(hidden_at, hidden_width)
    load(w_mlp_far, w_mlp)
    load_acts(hidden_at + hidden_width, hidden_width)
    load(w_hidden_far, w_hidden)
    load_acts(heads_at, 4 * head_width + LANES)
    load(w_attn_far, w_attn)
    load(w_qkv_far, w_qkv)

    loads[0].wait()
    loads[1].wait()
    mixed = dot_plain(acts[:, hidden_at : hidden_at + hidden_width], w_mlp[...])
    loads[2].wait()
    loads[3].wait()
    grad_normed = dot_last(acts[:, hidden_at + hidden_width : heads_at], w_hidden[...])
    for copy in loads[4:]:
        copy.wait()
    mixed = mixed + dot_plain(acts[:, heads_at : heads_at + head_width], w_attn[...])
    terms[:, :local_width] = mixed.astype(BF16)
    for part in range(3):
        start = heads_at + (1 + part) * head_width
        grad_normed = grad_normed + dot_last(acts[:, start : start + head_width], w_qkv[part])
    terms[:, local_width : 2 * local_width] = grad_normed.astype(BF16)
    terms[:, 2 * local_width :] = acts[:, heads_at + 4 * head_width :]


def weight_kernel(
    head_width, hidden_width, n_dp, place, own, peer, here_far, far_far, relayed_far, direct_far,
    acts, norm_t, mix_t, act_t, here, far, relayed, direct, arrived, left_for,
):
    row_count, local_width = own.shape[0], norm_t.shape[0]
    hidden_at = 2 * local_width
    heads_at = hidden_at + 2 * hidden_width
    core, chip, chips = place[0] % 2, place[0] // 2, n_dp // 2
    toward = 1 - 2 * core
    outs = (far, relayed, direct, here)
    outs_far = (far_far, relayed_far, direct_far, here_far)
    owners = [2 * ((chip + chips + step) % chips) + core for step in (2, toward, -toward, 0)]
    spans = (
        (0, local_width),
        (heads_at + head_width, 3 * head_width),
        (hidden_at + hidden_width, hidden_width),
        (hidden_at, hidden_width),
        (local_width, local_width),
        (heads_at, head_width),
    )
    loads = []
    for index, (start, length) in enumerate(spans):
        columns = pl.ds(start, length)
        for side, source in enumerate((own, peer)):
            target = acts.at[pl.ds(side * row_count, row_count), columns]
            load = pltpu.make_async_copy(source.at[:, columns], target, arrived.at[2 * index + side])
            load.start()
            loads.append(load)

    def ready(index):
        loads[2 * index].wait()
        loads[2 * index + 1].wait()

    def both(start, length):
        return acts[:, start : start + length]

    def rows(ref, length):
        return jnp.concatenate(
            [ref[pl.ds(pl.multiple_of(owner * length, 16), length), :] for owner in owners], axis=0
        )

    row, sent, sends = 0, 0, []

    def emit(left, right):
        nonlocal row
        length = left.shape[0] // len(owners)
        product = dot_plain(left, right)
        for step, out in enumerate(outs):
            out[row : row + length, :] = product[step * length : (step + 1) * length].astype(out.dtype)
        row += length

    def send():
        nonlocal sent
        part = pl.ds(sent, row - sent)
        for out, out_far in zip(outs, outs_far):
            copy = pltpu.make_async_copy(out.at[part, :], out_far.at[part, :], left_for.at[len(sends)])
            copy.start()
            sends.append(copy)
        sent = row

    ready(0)
    norm_t[...] = both(0, local_width).T
    norm_rows = rows(norm_t, local_width // n_dp)
    ready(1)
    for part in range(3):
        emit(norm_rows, both(heads_at + (1 + part) * head_width, head_width))
    send()
    ready(2)
    for block in range(hidden_width // head_width):
        emit(norm_rows, both(hidden_at + hidden_width + block * head_width, head_width))
    send()
    for index in (3, 4, 5):
        ready(index)
    mix_t[...] = both(heads_at, head_width).T
    act_t[...] = both(hidden_at, hidden_width).T
    cotangent = both(local_width, local_width)
    emit(rows(mix_t, head_width // n_dp), cotangent)
    emit(rows(act_t, hidden_width // n_dp), cotangent)
    send()
    for copy in sends:
        copy.wait()


def token_kernel(place, got, full, tokens, ln_gain, cotangent, mixed, grad_tokens):
    out_rows, local_width = mixed.shape
    parts = got.shape[0] // out_rows
    width = place[1]
    first = pl.multiple_of(place[0] * out_rows, 16)

    def total(start, length):
        values = got[:, start : start + length].astype(F32)
        return jnp.sum(values.reshape(parts, out_rows, length), axis=0)

    values = tokens[pl.ds(first, out_rows), :].astype(F32)
    mixed[...] = (values + total(0, local_width)).astype(BF16)
    stats = full[pl.ds(first, out_rows), full.shape[1] - LANES :].astype(F32)
    mean, inverse = from_lanes(stats, 0, 3), from_lanes(stats, 3, 3)
    normal_hat = (values - mean) * inverse
    sums = total(2 * local_width, LANES)
    share = 1.0 / width.astype(F32)
    mean_one, mean_two = from_lanes(sums, 0, 2) * share, from_lanes(sums, 2, 2) * share
    grad_hat = total(local_width, local_width) * ln_gain[...][None]
    grad = inverse * (grad_hat - mean_one - normal_hat * mean_two)
    back = cotangent[pl.ds(first, out_rows), :].astype(F32)
    grad_tokens[...] = (back + grad).astype(BF16)


def sum_kernel(
    here, relayed, direct, qkv_far, hidden_far, attn_far, mlp_far, qkv, hidden, attn, mlp, left_for
):
    length, head_width = qkv.shape[2], qkv.shape[3]
    blocks = hidden.shape[2] // head_width
    cuts = (0, 3 * length, (3 + blocks) * length, here.shape[0])

    def total(start, count):
        value = here[start : start + count, :]
        for part in (relayed, direct):
            value = value + part[start : start + count, :].astype(F32)
        return value

    sends = []

    def send(source, target):
        copy = pltpu.make_async_copy(source, target, left_for.at[len(sends)])
        copy.start()
        sends.append(copy)

    for part in range(3):
        qkv[part, 0] = total(part * length, length)
    send(qkv, qkv_far)
    for block in range(blocks):
        columns = slice(block * head_width, (block + 1) * head_width)
        hidden[0, :, columns] = total(cuts[1] + block * length, length)
    send(hidden, hidden_far)
    attn[0] = total(cuts[2], attn.shape[1])
    send(attn, attn_far)
    mlp[0] = total(cuts[2] + attn.shape[1], mlp.shape[1])
    send(mlp, mlp_far)
    for copy in sends:
        copy.wait()


def exchange(values, axis):
    return lax.all_to_all(values, axis, 0, 0, tiled=True)


def per_device(
    tokens, ln_gain, query_gain, key_gain, w_qkv, w_hidden, w_attn_out, w_mlp_out, cotangent
):
    n_dp, n_mx, n_my = lax.axis_size("dp"), lax.axis_size("mx"), lax.axis_size("my")
    row_count, local_width = tokens.shape
    head_width, hidden_width = w_qkv.shape[2], w_hidden.shape[1]
    width = local_width * n_my
    share, out_rows = row_count // n_my, row_count // n_mx


    def shape(*dims, dtype=BF16):
        return jax.ShapeDtypeStruct(dims, dtype)

    term_width = 5 * head_width + 2 * hidden_width
    inputs = (tokens, ln_gain, w_qkv, w_hidden, cotangent, w_attn_out, w_mlp_out)
    (terms,) = run(
        lambda *refs: project_kernel(share, *refs),
        inputs,
        (shape(row_count, term_width),),
        scratch=[pltpu.VMEM(array.shape, array.dtype) for array in inputs]
        + [
            pltpu.VMEM((row_count, term_width), BF16),
            pltpu.SemaphoreType.DMA((len(inputs),)),
            pltpu.SemaphoreType.DMA((term_width // head_width,)),
        ],
        fetched=range(len(inputs)),
        written=(0,),
        mebibytes=60,
    )
    got = exchange(terms, "my")
    spread, gain_sums = run(
        lambda *refs: share_kernel(head_width, local_width, *refs),
        (got,),
        (
            shape(row_count, 4 * head_width + 2 * hidden_width + LANES),
            shape(share, head_width, dtype=F32),
        ),
    )
    full = exchange(spread, "my")
    act_width = 2 * local_width + 2 * hidden_width + 4 * head_width + LANES
    (acts,) = run(
        lambda *refs: attend_kernel(head_width, hidden_width, *refs),
        (full, gain_sums, tokens, ln_gain, query_gain, key_gain, cotangent),
        (shape(row_count, act_width),),
    )
    peer_acts = lax.ppermute(acts, "dp", [(source, source ^ 1) for source in range(n_dp)])
    (out_terms,) = run(
        terms_kernel,
        (acts, w_mlp_out, w_hidden, w_attn_out, w_qkv),
        (shape(row_count, 2 * local_width + LANES),),
        scratch=[
            pltpu.VMEM(array.shape, BF16) for array in (acts, w_mlp_out, w_hidden, w_attn_out, w_qkv)
        ]
        + [pltpu.SemaphoreType.DMA((7,))],
        fetched=(0, 1, 2, 3, 4),
        mebibytes=60,
    )
    peer_acts, out_terms = lax.optimization_barrier((peer_acts, out_terms))
    out_got = exchange(out_terms, "mx")
    block_rows = (3 * local_width + local_width * hidden_width // head_width + head_width + hidden_width) // n_dp
    block = shape(block_rows, local_width)
    place = lax.axis_index("dp").reshape(1)
    weight_outs = (shape(block_rows, local_width, dtype=F32),) + (block,) * 3
    here, far, relayed, direct = run(
        lambda *refs: weight_kernel(head_width, hidden_width, n_dp, *refs),
        (place, acts, peer_acts),
        weight_outs,
        scratch=[
            pltpu.VMEM((2 * row_count, act_width), BF16),
            pltpu.VMEM((local_width, 2 * row_count), BF16),
            pltpu.VMEM((head_width, 2 * row_count), BF16),
            pltpu.VMEM((hidden_width, 2 * row_count), BF16),
            *(pltpu.VMEM(out.shape, out.dtype) for out in weight_outs),
            pltpu.SemaphoreType.DMA((12,)),
            pltpu.SemaphoreType.DMA((12,)),
        ],
        scalar=True,
        fetched=(1, 2),
        written=(0, 1, 2, 3),
        mebibytes=60,
    )

    def pass_on(values, step):
        ways = [(s, (s + 2 * step * (1 - 2 * (s % 2))) % n_dp) for s in range(n_dp)]
        return lax.ppermute(values, "dp", ways)

    passing = pass_on(far, 1)
    got_direct = pass_on(direct, -1)
    joined = (relayed.astype(F32) + passing.astype(F32)).astype(BF16)
    joined, out_got = lax.optimization_barrier((joined, out_got))
    got_relayed = pass_on(joined, 1)
    place = jnp.stack([lax.axis_index("mx"), jnp.int32(width)])
    mixed, grad_tokens = run(
        token_kernel,
        (place, out_got, full, tokens, ln_gain, cotangent),
        (shape(out_rows, local_width), shape(out_rows, local_width)),
        scalar=True,
    )
    grad_shapes = (
        shape(3, 1, local_width // n_dp, head_width, dtype=F32),
        shape(1, local_width // n_dp, hidden_width, dtype=F32),
        shape(1, head_width // n_dp, local_width, dtype=F32),
        shape(1, hidden_width // n_dp, local_width, dtype=F32),
    )
    grads = run(
        sum_kernel,
        (here, got_relayed, got_direct),
        grad_shapes,
        scratch=[pltpu.VMEM(grad.shape, grad.dtype) for grad in grad_shapes] + [pltpu.SemaphoreType.DMA((4,))],
        written=(0, 1, 2, 3),
    )
    return (mixed, grad_tokens, *grads)


def solution(mesh):
    placed = (
        P("dp", "my"),
        P("my"),
        P(),
        P(),
        P(None, "my", "mx"),
        P("my", "mx"),
        P("mx", "my"),
        P("mx", "my"),
        P("dp", "my"),
    )
    return jax.shard_map(
        per_device,
        mesh=mesh,
        in_specs=placed,
        out_specs=(
            P(("dp", "mx"), "my"),
            P(("dp", "mx"), "my"),
            P(None, "my", "dp", "mx"),
            P("my", "dp", "mx"),
            P("mx", "dp", "my"),
            P("mx", "dp", "my"),
        ),
        check_vma=False,
    )
```

```python
import jax
import jax.numpy as jnp
from jax import lax
from jax.experimental import pallas as pl
from jax.experimental.pallas import tpu as pltpu
from jax.sharding import PartitionSpec as P

EPSILON = 1e-06
LANES = 128
BF16 = jnp.bfloat16
F32 = jnp.float32


def dot_plain(matrix_a, matrix_b):
    return jnp.dot(matrix_a, matrix_b, preferred_element_type=F32)


def dot_first(matrix_a, matrix_b):
    return lax.dot_general(matrix_a, matrix_b, (((0,), (0,)), ((), ())), preferred_element_type=F32)


def dot_last(matrix_a, matrix_b):
    return lax.dot_general(matrix_a, matrix_b, (((1,), (1,)), ((), ())), preferred_element_type=F32)


def pieces(value, count):
    out = []
    for _ in range(count):
        part = value.astype(BF16).astype(F32)
        out.append(part)
        value = value - part
    return out


def to_lanes(columns):
    rows = columns[0].shape[0]
    lane = lax.broadcasted_iota(jnp.int32, (rows, LANES), 1)
    block = jnp.zeros((rows, LANES), F32)
    for index, column in enumerate(columns):
        block = jnp.where(lane == index, column, block)
    return block


def from_lanes(block, first, count):
    lane = lax.broadcasted_iota(jnp.int32, block.shape, block.ndim - 1)
    keep = (lane >= first) & (lane < first + count)
    return jnp.sum(jnp.where(keep, block, 0.0), axis=-1, keepdims=True)


def pack_stats(mean, squares, share, width):
    rows = mean.shape[0]
    stats = pieces(mean, 3) + pieces(squares, 3)
    lane = lax.broadcasted_iota(jnp.int32, (rows, width), 1)
    token = lax.broadcasted_iota(jnp.int32, (rows, width), 0) % share
    block = jnp.zeros((rows, width), F32)
    for index, value in enumerate(stats):
        block = jnp.where(lane == token * len(stats) + index, value, block)
    return jnp.sum(block.reshape(rows // share, share, width), axis=1, keepdims=True)


def unpack_stats(blocks, offset):
    share = blocks.shape[1]
    stats = jnp.broadcast_to(blocks[:, share - 1 : share, :], blocks.shape)
    lane = lax.broadcasted_iota(jnp.int32, blocks.shape, 2)
    first = lax.broadcasted_iota(jnp.int32, blocks.shape, 1) * 6 + offset
    keep = (lane >= first) & (lane < first + 3)
    return jnp.sum(jnp.where(keep, stats, 0.0), axis=2, keepdims=True)


class Merge:
    def __init__(self, got, share, parts, part_width, head_width):
        self.got, self.share, self.parts, self.head_width = got, share, parts, head_width
        rows, columns = got.shape
        self.rows, self.kept = rows, rows // parts
        self.gains = self.take(columns - head_width, head_width).reshape(rows // share, share, head_width)
        local_mean = unpack_stats(self.gains, 0)
        self.mean = self.add(local_mean.reshape(rows, 1)) / parts
        everywhere = jnp.broadcast_to(self.mean[None], (parts, self.kept, 1))
        self.shift = local_mean - everywhere.reshape(rows // share, share, 1)
        squares = unpack_stats(self.gains, 3) + part_width * self.shift * self.shift
        self.squares = self.add(squares.reshape(rows, 1))

    def take(self, start, length):
        return self.got[:, start : start + length].astype(F32)

    def add(self, values):
        return jnp.sum(values.reshape(self.parts, self.kept, values.shape[1]), axis=0)

    def plain(self, block):
        return self.add(self.take(block * self.head_width, self.head_width))

    def projected(self, block):
        change = self.shift * self.gains[:, block : block + 1, :]
        return self.plain(block) + self.add(change.reshape(self.rows, self.head_width))

    def gain_sums(self):
        return self.add(self.gains.reshape(self.rows, self.head_width))


def run(kernel, operands, out_shape, scratch=(), scalar=False, fetched=(), written=(), mebibytes=16):
    in_specs = [pl.BlockSpec(memory_space=pltpu.VMEM)] * len(operands)
    out_specs = [pl.BlockSpec(memory_space=pltpu.VMEM)] * len(out_shape)
    if scalar:
        in_specs[0] = pl.BlockSpec(memory_space=pltpu.SMEM)
    for index in fetched:
        in_specs[index] = pl.BlockSpec(memory_space=pltpu.HBM)
    for index in written:
        out_specs[index] = pl.BlockSpec(memory_space=pltpu.HBM)
    return pl.pallas_call(
        kernel,
        in_specs=in_specs,
        out_specs=out_specs,
        out_shape=out_shape,
        scratch_shapes=list(scratch),
        compiler_params=pltpu.CompilerParams(vmem_limit_bytes=mebibytes * 1024 * 1024),
    )(*operands)


def project_kernel(share, *refs):
    far, out_far, near, out, arrived, left_for = refs[:7], refs[7], refs[8:15], refs[15], refs[16], refs[17]
    tokens, ln_gain, w_qkv, w_hidden, cotangent, w_attn, w_mlp = near
    rows, width = tokens.shape
    head_width = w_qkv.shape[2]
    blocks = w_hidden.shape[1] // head_width
    loads = [
        pltpu.make_async_copy(source, target, arrived.at[index])
        for index, (source, target) in enumerate(zip(far, near))
    ]
    for load in loads:
        load.start()
    sends = []

    def emit(values):
        columns = pl.ds(sum(send[1] for send in sends), values.shape[1])
        out[:, columns] = values.astype(BF16)
        copy = pltpu.make_async_copy(out.at[:, columns], out_far.at[:, columns], left_for.at[len(sends)])
        copy.start()
        sends.append((copy, values.shape[1]))

    loads[0].wait()
    loads[1].wait()
    values = tokens[...].astype(F32)
    mean = jnp.sum(values, axis=1, keepdims=True) / width
    centred = values - mean
    squares = jnp.sum(centred * centred, axis=1, keepdims=True)
    gain = ln_gain[...][None]
    scaled = (centred * gain).astype(BF16)
    high, low = pieces(gain, 2)
    row_id = lax.broadcasted_iota(jnp.int32, (16, width), 0)
    gain_rows = jnp.where(row_id == 0, high, jnp.where(row_id == 1, low, 0.0)).astype(BF16)
    left = jnp.concatenate([scaled, gain_rows], axis=0)
    share_id = lax.broadcasted_iota(jnp.int32, (share, head_width), 0)
    gain_sums = jnp.zeros((share, head_width), F32)
    for block in range(3 + blocks):
        if block == 0 or block == 3:
            loads[2 + block // 3].wait()
        if block < 3:
            weight = w_qkv[block]
        else:
            weight = w_hidden[:, (block - 3) * head_width : (block - 2) * head_width]
        product = dot_plain(left, weight)
        emit(product[:rows])
        both = product[rows : rows + 1] + product[rows + 1 : rows + 2]
        gain_sums = jnp.where(share_id == block, both, gain_sums)
    loads[4].wait()
    loads[5].wait()
    back = cotangent[...]
    emit(dot_last(back, w_attn[...]))
    loads[6].wait()
    for block in range(blocks):
        emit(dot_last(back, w_mlp[block * head_width : (block + 1) * head_width, :]))
    row = pack_stats(mean, squares, share, head_width)
    spread = jnp.where(share_id[None] == share - 1, row, gain_sums[None])
    emit(spread.reshape(rows, head_width))
    for copy, _ in sends:
        copy.wait()


def merge_kernel(share, parts, part_width, head_width, got, out):
    merge = Merge(got, share, parts, part_width, head_width)
    last = got.shape[1] // head_width - 1
    blocks = (last - 4) // 2
    for block in range(last):
        value = merge.projected(block) if block < 3 + blocks else merge.plain(block)
        out[:, block * head_width : (block + 1) * head_width] = value.astype(BF16)
    row = pack_stats(merge.mean, merge.squares, share, head_width)
    sums = merge.gain_sums().reshape(merge.kept // share, share, head_width)
    share_id = lax.broadcasted_iota(jnp.int32, sums.shape, 1)
    sums = jnp.where(share_id == share - 1, row, sums)
    out[:, last * head_width :] = sums.reshape(merge.kept, head_width).astype(BF16)


def share_kernel(parts, part_width, head_width, got, out, sums_out):
    rows, columns = got.shape
    share = rows // parts
    hidden_width = (columns - 5 * head_width) // 2
    blocks = hidden_width // head_width
    merge = Merge(got, share, parts, part_width, head_width)
    inverse = lax.rsqrt(merge.squares / (parts * part_width) + EPSILON)
    gain_sums = merge.gain_sums()
    sums_out[...] = gain_sums

    def spread(value):
        length = value.shape[1]
        tiled = jnp.broadcast_to(value[None], (out.shape[0] // share, share, length))
        return tiled.reshape(out.shape[0], length).astype(BF16)

    def projected(block):
        return (inverse * merge.projected(block)).astype(BF16).astype(F32)

    back_at = 3 + blocks
    for block in range(3):
        out[:, block * head_width : (block + 1) * head_width] = spread(projected(block))
    out[:, 3 * head_width : 4 * head_width] = spread(merge.plain(back_at))
    plain_sum = jnp.zeros((share, 1), F32)
    hat_sum = jnp.zeros((share, 1), F32)
    inner_scale = 0.7978845608028654
    for block in range(blocks):
        pre = projected(3 + block)
        grad_act = merge.plain(back_at + 1 + block).astype(BF16).astype(F32)
        squared = pre * pre
        bent = jnp.tanh(inner_scale * (pre + 0.044715 * squared * pre))
        active = 0.5 * pre * (1.0 + bent)
        slope = 0.5 * (1.0 + bent) + 0.5 * pre * (1.0 - bent * bent) * inner_scale * (
            1.0 + 3.0 * 0.044715 * squared
        )
        grad_pre = (grad_act * slope).astype(BF16).astype(F32)
        plain_sum += jnp.sum(grad_pre * gain_sums[3 + block : 4 + block], axis=1, keepdims=True)
        hat_sum += jnp.sum(grad_pre * pre, axis=1, keepdims=True)
        start = (4 + block) * head_width
        out[:, start : start + head_width] = spread(active)
        start += hidden_width
        out[:, start : start + head_width] = spread(grad_pre)
    scalars = pieces(merge.mean, 3) + pieces(inverse, 3) + pieces(plain_sum, 2) + pieces(hat_sum, 2)
    out[:, 4 * head_width + 2 * hidden_width :] = spread(to_lanes(scalars))


def attend_kernel(
    head_width, hidden_width, full, gain_sums, tokens, ln_gain, query_gain, key_gain, cotangent, acts
):
    head_size = query_gain.shape[0]
    query_row, key_row = query_gain[...][None], key_gain[...][None]
    local_width = tokens.shape[1]
    stats = full[:, 4 * head_width + 2 * hidden_width :].astype(F32)
    mean, inverse = from_lanes(stats, 0, 3), from_lanes(stats, 3, 3)
    plain_sum, hat_sum = from_lanes(stats, 6, 2), from_lanes(stats, 8, 2)
    normal_hat = (tokens[...].astype(F32) - mean) * inverse
    acts[:, :local_width] = (normal_hat * ln_gain[...][None]).astype(BF16)
    acts[:, local_width : 2 * local_width] = cotangent[...]
    hidden_at = 4 * head_width
    acts_hidden = 2 * local_width
    acts[:, acts_hidden : acts_hidden + 2 * hidden_width] = full[:, hidden_at : hidden_at + 2 * hidden_width]
    acts_heads = acts_hidden + 2 * hidden_width
    scale = head_size ** (-0.5)

    def normalise(values):
        centred = values - jnp.mean(values, axis=1, keepdims=True)
        root = lax.rsqrt(jnp.mean(centred * centred, axis=1, keepdims=True) + EPSILON)
        return centred * root, root

    def back(grad, hat, root, gain):
        grad = grad * gain
        centred = grad - jnp.mean(grad, axis=1, keepdims=True)
        centred = centred - hat * jnp.mean(grad * hat, axis=1, keepdims=True)
        return (root * centred).astype(BF16)

    for head in range(head_width // head_size):
        low, high = head * head_size, (head + 1) * head_size
        query = full[:, low:high].astype(F32)
        key = full[:, head_width + low : head_width + high].astype(F32)
        value_low = full[:, 2 * head_width + low : 2 * head_width + high]
        grad_mix = full[:, 3 * head_width + low : 3 * head_width + high]
        query_hat, query_root = normalise(query)
        key_hat, key_root = normalise(key)
        query_norm = (query_hat * query_row).astype(BF16)
        key_norm = (key_hat * key_row).astype(BF16)
        scores = dot_last(query_norm, key_norm) * scale
        weights = jnp.exp(scores - jnp.max(scores, axis=1, keepdims=True))
        probs = weights / jnp.sum(weights, axis=1, keepdims=True)
        probs_low = probs.astype(BF16)
        acts[:, acts_heads + low : acts_heads + high] = dot_plain(probs_low, value_low).astype(BF16)
        grad_probs = dot_last(grad_mix, value_low)
        grad_value = dot_first(probs_low, grad_mix).astype(BF16)
        grad_scores = probs * (grad_probs - jnp.sum(grad_probs * probs, axis=1, keepdims=True))
        grad_scores = grad_scores.astype(BF16)
        grad_query = back(
            dot_plain(grad_scores, key_norm) * scale, query_hat, query_root, query_row
        )
        grad_key = back(
            dot_first(grad_scores, query_norm) * scale, key_hat, key_root, key_row
        )
        plain = jnp.zeros_like(query)
        with_hat = jnp.zeros_like(query)
        for part, (grad, pre) in enumerate(
            ((grad_query, query), (grad_key, key), (grad_value, value_low.astype(F32)))
        ):
            start = acts_heads + (1 + part) * head_width
            acts[:, start + low : start + high] = grad
            grad = grad.astype(F32)
            plain = plain + grad * gain_sums[part : part + 1, low:high]
            with_hat = with_hat + grad * pre
        plain_sum = plain_sum + jnp.sum(plain, axis=1, keepdims=True)
        hat_sum = hat_sum + jnp.sum(with_hat, axis=1, keepdims=True)

    acts[:, acts_heads + 4 * head_width :] = to_lanes(pieces(plain_sum, 2) + pieces(hat_sum, 2)).astype(BF16)


def terms_kernel(
    acts_far, w_mlp_far, w_hidden_far, w_attn_far, w_qkv_far, terms,
    acts, w_mlp, w_hidden, w_attn, w_qkv, arrived,
):
    head_width = w_qkv.shape[2]
    hidden_width, local_width = w_mlp.shape
    hidden_at = 2 * local_width
    heads_at = hidden_at + 2 * hidden_width
    loads = []

    def load(source, target):
        copy = pltpu.make_async_copy(source, target, arrived.at[len(loads)])
        copy.start()
        loads.append(copy)

    def load_acts(start, length):
        load(acts_far.at[:, pl.ds(start, length)], acts.at[:, pl.ds(start, length)])

    load_acts(hidden_at, hidden_width)
    load(w_mlp_far, w_mlp)
    load_acts(hidden_at + hidden_width, hidden_width)
    load(w_hidden_far, w_hidden)
    load_acts(heads_at, 4 * head_width + LANES)
    load(w_attn_far, w_attn)
    load(w_qkv_far, w_qkv)

    loads[0].wait()
    loads[1].wait()
    mixed = dot_plain(acts[:, hidden_at : hidden_at + hidden_width], w_mlp[...])
    loads[2].wait()
    loads[3].wait()
    grad_normed = dot_last(acts[:, hidden_at + hidden_width : heads_at], w_hidden[...])
    for copy in loads[4:]:
        copy.wait()
    mixed = mixed + dot_plain(acts[:, heads_at : heads_at + head_width], w_attn[...])
    terms[:, :local_width] = mixed.astype(BF16)
    for part in range(3):
        start = heads_at + (1 + part) * head_width
        grad_normed = grad_normed + dot_last(acts[:, start : start + head_width], w_qkv[part])
    terms[:, local_width : 2 * local_width] = grad_normed.astype(BF16)
    terms[:, 2 * local_width :] = acts[:, heads_at + 4 * head_width :]


def weight_kernel(
    head_width, hidden_width, n_dp, place, own, peer, here_far, far_far, relayed_far, direct_far,
    acts, norm_t, mix_t, act_t, here, far, relayed, direct, arrived, left_for,
):
    row_count, local_width = own.shape[0], norm_t.shape[0]
    hidden_at = 2 * local_width
    heads_at = hidden_at + 2 * hidden_width
    core, chip, chips = place[0] % 2, place[0] // 2, n_dp // 2
    toward = 1 - 2 * core
    outs = (far, relayed, direct, here)
    outs_far = (far_far, relayed_far, direct_far, here_far)
    owners = [2 * ((chip + chips + step) % chips) + core for step in (2, toward, -toward, 0)]
    spans = (
        (0, local_width),
        (heads_at + head_width, 3 * head_width),
        (hidden_at + hidden_width, hidden_width),
        (hidden_at, hidden_width),
        (local_width, local_width),
        (heads_at, head_width),
    )
    loads = []
    for index, (start, length) in enumerate(spans):
        columns = pl.ds(start, length)
        for side, source in enumerate((own, peer)):
            target = acts.at[pl.ds(side * row_count, row_count), columns]
            load = pltpu.make_async_copy(source.at[:, columns], target, arrived.at[2 * index + side])
            load.start()
            loads.append(load)

    def ready(index):
        loads[2 * index].wait()
        loads[2 * index + 1].wait()

    def both(start, length):
        return acts[:, start : start + length]

    def rows(ref, length):
        return jnp.concatenate(
            [ref[pl.ds(pl.multiple_of(owner * length, 16), length), :] for owner in owners], axis=0
        )

    row, sent, sends = 0, 0, []

    def emit(left, right):
        nonlocal row
        length = left.shape[0] // len(owners)
        product = dot_plain(left, right)
        for step, out in enumerate(outs):
            out[row : row + length, :] = product[step * length : (step + 1) * length].astype(out.dtype)
        row += length

    def send():
        nonlocal sent
        part = pl.ds(sent, row - sent)
        for out, out_far in zip(outs, outs_far):
            copy = pltpu.make_async_copy(out.at[part, :], out_far.at[part, :], left_for.at[len(sends)])
            copy.start()
            sends.append(copy)
        sent = row

    ready(0)
    norm_t[...] = both(0, local_width).T
    norm_rows = rows(norm_t, local_width // n_dp)
    ready(1)
    for part in range(3):
        emit(norm_rows, both(heads_at + (1 + part) * head_width, head_width))
    send()
    ready(2)
    for block in range(hidden_width // head_width):
        emit(norm_rows, both(hidden_at + hidden_width + block * head_width, head_width))
    send()
    for index in (3, 4, 5):
        ready(index)
    mix_t[...] = both(heads_at, head_width).T
    act_t[...] = both(hidden_at, hidden_width).T
    cotangent = both(local_width, local_width)
    emit(rows(mix_t, head_width // n_dp), cotangent)
    emit(rows(act_t, hidden_width // n_dp), cotangent)
    send()
    for copy in sends:
        copy.wait()


def token_kernel(place, got, full, tokens, ln_gain, cotangent, mixed, grad_tokens):
    out_rows, local_width = mixed.shape
    parts = got.shape[0] // out_rows
    width = place[1]
    first = pl.multiple_of(place[0] * out_rows, 16)

    def total(start, length):
        values = got[:, start : start + length].astype(F32)
        return jnp.sum(values.reshape(parts, out_rows, length), axis=0)

    values = tokens[pl.ds(first, out_rows), :].astype(F32)
    mixed[...] = (values + total(0, local_width)).astype(BF16)
    stats = full[pl.ds(first, out_rows), full.shape[1] - LANES :].astype(F32)
    mean, inverse = from_lanes(stats, 0, 3), from_lanes(stats, 3, 3)
    normal_hat = (values - mean) * inverse
    sums = total(2 * local_width, LANES)
    share = 1.0 / width.astype(F32)
    mean_one, mean_two = from_lanes(sums, 0, 2) * share, from_lanes(sums, 2, 2) * share
    grad_hat = total(local_width, local_width) * ln_gain[...][None]
    grad = inverse * (grad_hat - mean_one - normal_hat * mean_two)
    back = cotangent[pl.ds(first, out_rows), :].astype(F32)
    grad_tokens[...] = (back + grad).astype(BF16)


def sum_kernel(
    here, relayed, direct, qkv_far, hidden_far, attn_far, mlp_far, qkv, hidden, attn, mlp, left_for
):
    length, head_width = qkv.shape[2], qkv.shape[3]
    blocks = hidden.shape[2] // head_width
    cuts = (0, 3 * length, (3 + blocks) * length, here.shape[0])

    def total(start, count):
        value = here[start : start + count, :]
        for part in (relayed, direct):
            value = value + part[start : start + count, :].astype(F32)
        return value

    sends = []

    def send(source, target):
        copy = pltpu.make_async_copy(source, target, left_for.at[len(sends)])
        copy.start()
        sends.append(copy)

    for part in range(3):
        qkv[part, 0] = total(part * length, length)
    send(qkv, qkv_far)
    for block in range(blocks):
        columns = slice(block * head_width, (block + 1) * head_width)
        hidden[0, :, columns] = total(cuts[1] + block * length, length)
    send(hidden, hidden_far)
    attn[0] = total(cuts[2], attn.shape[1])
    send(attn, attn_far)
    mlp[0] = total(cuts[2] + attn.shape[1], mlp.shape[1])
    send(mlp, mlp_far)
    for copy in sends:
        copy.wait()


def exchange(values, axis, groups=None):
    return lax.all_to_all(values, axis, 0, 0, tiled=True, axis_index_groups=groups)


def per_device(
    tokens, ln_gain, query_gain, key_gain, w_qkv, w_hidden, w_attn_out, w_mlp_out, cotangent
):
    n_dp, n_mx, n_my = lax.axis_size("dp"), lax.axis_size("mx"), lax.axis_size("my")
    row_count, local_width = tokens.shape
    head_width, hidden_width = w_qkv.shape[2], w_hidden.shape[1]
    width = local_width * n_my
    share, out_rows = row_count // n_my, row_count // n_mx
    near = 4 if n_my % 16 == 0 else 2
    near_groups = [[first + step for step in range(near)] for first in range(0, n_my, near)]
    far_groups = [list(range(first, n_my, near)) for first in range(near)]


    def shape(*dims, dtype=BF16):
        return jax.ShapeDtypeStruct(dims, dtype)

    term_width = 5 * head_width + 2 * hidden_width
    inputs = (tokens, ln_gain, w_qkv, w_hidden, cotangent, w_attn_out, w_mlp_out)
    (terms,) = run(
        lambda *refs: project_kernel(share, *refs),
        inputs,
        (shape(row_count, term_width),),
        scratch=[pltpu.VMEM(array.shape, array.dtype) for array in inputs]
        + [
            pltpu.VMEM((row_count, term_width), BF16),
            pltpu.SemaphoreType.DMA((len(inputs),)),
            pltpu.SemaphoreType.DMA((term_width // head_width,)),
        ],
        fetched=range(len(inputs)),
        written=(0,),
        mebibytes=60,
    )
    got = exchange(terms, "my", near_groups)
    (terms,) = run(
        lambda *refs: merge_kernel(share, near, local_width, head_width, *refs),
        (got,),
        (shape(row_count // near, term_width),),
    )
    got = exchange(terms, "my", far_groups)
    spread, gain_sums = run(
        lambda *refs: share_kernel(n_my // near, near * local_width, head_width, *refs),
        (got,),
        (
            shape(row_count // near, 4 * head_width + 2 * hidden_width + LANES),
            shape(share, head_width, dtype=F32),
        ),
    )
    part = exchange(spread, "my", far_groups)
    spread = jnp.broadcast_to(part[None], (near, *part.shape)).reshape(row_count, part.shape[1])
    full = exchange(spread, "my", near_groups)
    act_width = 2 * local_width + 2 * hidden_width + 4 * head_width + LANES
    (acts,) = run(
        lambda *refs: attend_kernel(head_width, hidden_width, *refs),
        (full, gain_sums, tokens, ln_gain, query_gain, key_gain, cotangent),
        (shape(row_count, act_width),),
    )
    peer_acts = lax.ppermute(acts, "dp", [(source, source ^ 1) for source in range(n_dp)])
    (out_terms,) = run(
        terms_kernel,
        (acts, w_mlp_out, w_hidden, w_attn_out, w_qkv),
        (shape(row_count, 2 * local_width + LANES),),
        scratch=[
            pltpu.VMEM(array.shape, BF16) for array in (acts, w_mlp_out, w_hidden, w_attn_out, w_qkv)
        ]
        + [pltpu.SemaphoreType.DMA((7,))],
        fetched=(0, 1, 2, 3, 4),
        mebibytes=60,
    )
    peer_acts, out_terms = lax.optimization_barrier((peer_acts, out_terms))
    out_got = exchange(out_terms, "mx")
    block_rows = (3 * local_width + local_width * hidden_width // head_width + head_width + hidden_width) // n_dp
    block = shape(block_rows, local_width)
    place = lax.axis_index("dp").reshape(1)
    weight_outs = (shape(block_rows, local_width, dtype=F32),) + (block,) * 3
    here, far, relayed, direct = run(
        lambda *refs: weight_kernel(head_width, hidden_width, n_dp, *refs),
        (place, acts, peer_acts),
        weight_outs,
        scratch=[
            pltpu.VMEM((2 * row_count, act_width), BF16),
            pltpu.VMEM((local_width, 2 * row_count), BF16),
            pltpu.VMEM((head_width, 2 * row_count), BF16),
            pltpu.VMEM((hidden_width, 2 * row_count), BF16),
            *(pltpu.VMEM(out.shape, out.dtype) for out in weight_outs),
            pltpu.SemaphoreType.DMA((12,)),
            pltpu.SemaphoreType.DMA((12,)),
        ],
        scalar=True,
        fetched=(1, 2),
        written=(0, 1, 2, 3),
        mebibytes=60,
    )

    def pass_on(values, step):
        ways = [(s, (s + 2 * step * (1 - 2 * (s % 2))) % n_dp) for s in range(n_dp)]
        return lax.ppermute(values, "dp", ways)

    passing = pass_on(far, 1)
    got_direct = pass_on(direct, -1)
    joined = (relayed.astype(F32) + passing.astype(F32)).astype(BF16)
    joined, out_got = lax.optimization_barrier((joined, out_got))
    got_relayed = pass_on(joined, 1)
    place = jnp.stack([lax.axis_index("mx"), jnp.int32(width)])
    mixed, grad_tokens = run(
        token_kernel,
        (place, out_got, full, tokens, ln_gain, cotangent),
        (shape(out_rows, local_width), shape(out_rows, local_width)),
        scalar=True,
    )
    grad_shapes = (
        shape(3, 1, local_width // n_dp, head_width, dtype=F32),
        shape(1, local_width // n_dp, hidden_width, dtype=F32),
        shape(1, head_width // n_dp, local_width, dtype=F32),
        shape(1, hidden_width // n_dp, local_width, dtype=F32),
    )
    grads = run(
        sum_kernel,
        (here, got_relayed, got_direct),
        grad_shapes,
        scratch=[pltpu.VMEM(grad.shape, grad.dtype) for grad in grad_shapes] + [pltpu.SemaphoreType.DMA((4,))],
        written=(0, 1, 2, 3),
    )
    return (mixed, grad_tokens, *grads)


def solution(mesh):
    placed = (
        P("dp", "my"),
        P("my"),
        P(),
        P(),
        P(None, "my", "mx"),
        P("my", "mx"),
        P("mx", "my"),
        P("mx", "my"),
        P("dp", "my"),
    )
    return jax.shard_map(
        per_device,
        mesh=mesh,
        in_specs=placed,
        out_specs=(
            P(("dp", "mx"), "my"),
            P(("dp", "mx"), "my"),
            P(None, "my", "dp", "mx"),
            P("my", "dp", "mx"),
            P("mx", "dp", "my"),
            P("mx", "dp", "my"),
        ),
        check_vma=False,
    )
```

```python
import jax
import jax.numpy as jnp
from jax import lax
from jax.experimental import pallas as pl
from jax.experimental.pallas import tpu as pltpu
from jax.sharding import PartitionSpec as P

EPSILON = 1e-06
LANES = 128
BF16 = jnp.bfloat16
F32 = jnp.float32


def dot_plain(matrix_a, matrix_b):
    return jnp.dot(matrix_a, matrix_b, preferred_element_type=F32)


def dot_first(matrix_a, matrix_b):
    return lax.dot_general(matrix_a, matrix_b, (((0,), (0,)), ((), ())), preferred_element_type=F32)


def dot_last(matrix_a, matrix_b):
    return lax.dot_general(matrix_a, matrix_b, (((1,), (1,)), ((), ())), preferred_element_type=F32)


def pieces(value, count):
    out = []
    for _ in range(count):
        part = value.astype(BF16).astype(F32)
        out.append(part)
        value = value - part
    return out


def to_lanes(columns):
    rows = columns[0].shape[0]
    lane = lax.broadcasted_iota(jnp.int32, (rows, LANES), 1)
    block = jnp.zeros((rows, LANES), F32)
    for index, column in enumerate(columns):
        block = jnp.where(lane == index, column, block)
    return block


def from_lanes(block, first, count):
    lane = lax.broadcasted_iota(jnp.int32, block.shape, block.ndim - 1)
    keep = (lane >= first) & (lane < first + count)
    return jnp.sum(jnp.where(keep, block, 0.0), axis=-1, keepdims=True)


def pack(values, share, width):
    rows = values[0].shape[0]
    lane = lax.broadcasted_iota(jnp.int32, (rows, width), 1)
    token = lax.broadcasted_iota(jnp.int32, (rows, width), 0) % share
    block = jnp.zeros((rows, width), F32)
    for index, value in enumerate(values):
        block = jnp.where(lane == token * len(values) + index, value, block)
    return jnp.sum(block.reshape(rows // share, share, width), axis=1, keepdims=True)


def unpack(row, share, count, offset):
    shape = (row.shape[0], share, row.shape[2])
    lane = lax.broadcasted_iota(jnp.int32, shape, 2)
    first = lax.broadcasted_iota(jnp.int32, shape, 1) * count + offset
    keep = (lane >= first) & (lane < first + 3)
    return jnp.sum(jnp.where(keep, jnp.broadcast_to(row, shape), 0.0), axis=2, keepdims=True)


class Merge:
    def __init__(self, got, share, parts, part_width, head_width, compact):
        self.got, self.parts, self.head_width = got, parts, head_width
        rows, columns = got.shape
        self.rows, self.kept = rows, rows // parts
        lines = head_width // LANES
        if compact:
            share, start = self.kept, columns - LANES
            block = self.take(start, LANES).reshape(parts, share, LANES)
            blocks = (start // head_width - 4) // 2 + 3
            self.gain_rows = [
                jnp.concatenate([block[:, row : row + 1, :] for row in range(first, first + lines)], axis=2)
                for first in range(0, blocks * lines, lines)
            ]
            last = blocks * lines
            local_mean = unpack(block[:, last : last + 1, :], share, 3, 0)
            local_squares = unpack(block[:, last + 1 : last + 2, :], share, 3, 0)
        else:
            start = columns - head_width
            block = self.take(start, head_width).reshape(rows // share, share, head_width)
            self.gain_rows = [block[:, row : row + 1, :] for row in range(share - 1)]
            local_mean = unpack(block[:, share - 1 : share, :], share, 6, 0)
            local_squares = unpack(block[:, share - 1 : share, :], share, 6, 3)
        self.mean = self.add(local_mean.reshape(rows, 1)) / parts
        everywhere = jnp.broadcast_to(self.mean[None], (parts, self.kept, 1))
        self.shift = local_mean - everywhere.reshape(rows // share, share, 1)
        squares = local_squares + part_width * self.shift * self.shift
        self.squares = self.add(squares.reshape(rows, 1))

    def take(self, start, length):
        return self.got[:, start : start + length].astype(F32)

    def add(self, values):
        return jnp.sum(values.reshape(self.parts, self.kept, values.shape[1]), axis=0)

    def plain(self, block):
        return self.add(self.take(block * self.head_width, self.head_width))

    def projected(self, block):
        change = self.shift * self.gain_rows[block]
        return self.plain(block) + self.add(change.reshape(self.rows, self.head_width))

    def gain_sum(self, block):
        return jnp.sum(self.gain_rows[block], axis=0)


def run(kernel, operands, out_shape, scratch=(), scalar=False, fetched=(), written=(), mebibytes=16):
    in_specs = [pl.BlockSpec(memory_space=pltpu.VMEM)] * len(operands)
    out_specs = [pl.BlockSpec(memory_space=pltpu.VMEM)] * len(out_shape)
    if scalar:
        in_specs[0] = pl.BlockSpec(memory_space=pltpu.SMEM)
    for index in fetched:
        in_specs[index] = pl.BlockSpec(memory_space=pltpu.HBM)
    for index in written:
        out_specs[index] = pl.BlockSpec(memory_space=pltpu.HBM)
    return pl.pallas_call(
        kernel,
        in_specs=in_specs,
        out_specs=out_specs,
        out_shape=out_shape,
        scratch_shapes=list(scratch),
        compiler_params=pltpu.CompilerParams(vmem_limit_bytes=mebibytes * 1024 * 1024),
    )(*operands)


def project_kernel(kept, *refs):
    far, out_far, near, out, arrived, left_for = refs[:7], refs[7], refs[8:15], refs[15], refs[16], refs[17]
    tokens, ln_gain, w_qkv, w_hidden, cotangent, w_attn, w_mlp = near
    rows, width = tokens.shape
    head_width = w_qkv.shape[2]
    blocks = w_hidden.shape[1] // head_width
    loads = [
        pltpu.make_async_copy(source, target, arrived.at[index])
        for index, (source, target) in enumerate(zip(far, near))
    ]
    for load in loads:
        load.start()
    sends = []

    def emit(values):
        columns = pl.ds(sum(send[1] for send in sends), values.shape[1])
        out[:, columns] = values.astype(BF16)
        copy = pltpu.make_async_copy(out.at[:, columns], out_far.at[:, columns], left_for.at[len(sends)])
        copy.start()
        sends.append((copy, values.shape[1]))

    loads[0].wait()
    loads[1].wait()
    values = tokens[...].astype(F32)
    mean = jnp.sum(values, axis=1, keepdims=True) / width
    centred = values - mean
    squares = jnp.sum(centred * centred, axis=1, keepdims=True)
    gain = ln_gain[...][None]
    scaled = (centred * gain).astype(BF16)
    high, low = pieces(gain, 2)
    row_id = lax.broadcasted_iota(jnp.int32, (16, width), 0)
    gain_rows = jnp.where(row_id == 0, high, jnp.where(row_id == 1, low, 0.0)).astype(BF16)
    left = jnp.concatenate([scaled, gain_rows], axis=0)
    lines = head_width // LANES
    line_id = lax.broadcasted_iota(jnp.int32, (kept, LANES), 0)
    gain_sums = jnp.zeros((kept, LANES), F32)
    for block in range(3 + blocks):
        if block == 0 or block == 3:
            loads[2 + block // 3].wait()
        if block < 3:
            weight = w_qkv[block]
        else:
            weight = w_hidden[:, (block - 3) * head_width : (block - 2) * head_width]
        product = dot_plain(left, weight)
        emit(product[:rows])
        both = product[rows : rows + 1] + product[rows + 1 : rows + 2]
        for line in range(lines):
            value = both[:, line * LANES : (line + 1) * LANES]
            gain_sums = jnp.where(line_id == block * lines + line, value, gain_sums)
    loads[4].wait()
    loads[5].wait()
    back = cotangent[...]
    emit(dot_last(back, w_attn[...]))
    loads[6].wait()
    for block in range(blocks):
        emit(dot_last(back, w_mlp[block * head_width : (block + 1) * head_width, :]))
    last = (3 + blocks) * lines
    spread = jnp.where(line_id[None] == last, pack(pieces(mean, 3), kept, LANES), gain_sums[None])
    spread = jnp.where(line_id[None] == last + 1, pack(pieces(squares, 3), kept, LANES), spread)
    emit(spread.reshape(rows, LANES))
    for copy, _ in sends:
        copy.wait()


def merge_kernel(share, parts, part_width, head_width, got, out):
    merge = Merge(got, share, parts, part_width, head_width, True)
    last = (got.shape[1] - LANES) // head_width
    blocks = (last - 4) // 2
    shape = (merge.kept // share, share, head_width)
    share_id = lax.broadcasted_iota(jnp.int32, shape, 1)
    sums = jnp.zeros(shape, F32)
    for block in range(last):
        if block < 3 + blocks:
            value = merge.projected(block)
            sums = jnp.where(share_id == block, merge.gain_sum(block)[None], sums)
        else:
            value = merge.plain(block)
        out[:, block * head_width : (block + 1) * head_width] = value.astype(BF16)
    row = pack(pieces(merge.mean, 3) + pieces(merge.squares, 3), share, head_width)
    sums = jnp.where(share_id == share - 1, row, sums)
    out[:, last * head_width :] = sums.reshape(merge.kept, head_width).astype(BF16)


def share_kernel(parts, part_width, head_width, got, out, sums_out):
    rows, columns = got.shape
    share = rows // parts
    hidden_width = (columns - 5 * head_width) // 2
    blocks = hidden_width // head_width
    merge = Merge(got, share, parts, part_width, head_width, False)
    inverse = lax.rsqrt(merge.squares / (parts * part_width) + EPSILON)
    share_id = lax.broadcasted_iota(jnp.int32, sums_out.shape, 0)
    gain_sums = jnp.zeros(sums_out.shape, F32)
    for block in range(3 + blocks):
        gain_sums = jnp.where(share_id == block, merge.gain_sum(block), gain_sums)
    sums_out[...] = gain_sums

    def spread(value):
        length = value.shape[1]
        tiled = jnp.broadcast_to(value[None], (out.shape[0] // share, share, length))
        return tiled.reshape(out.shape[0], length).astype(BF16)

    def projected(block):
        return (inverse * merge.projected(block)).astype(BF16).astype(F32)

    back_at = 3 + blocks
    for block in range(3):
        out[:, block * head_width : (block + 1) * head_width] = spread(projected(block))
    out[:, 3 * head_width : 4 * head_width] = spread(merge.plain(back_at))
    plain_sum = jnp.zeros((share, 1), F32)
    hat_sum = jnp.zeros((share, 1), F32)
    inner_scale = 0.7978845608028654
    for block in range(blocks):
        pre = projected(3 + block)
        grad_act = merge.plain(back_at + 1 + block).astype(BF16).astype(F32)
        squared = pre * pre
        bent = jnp.tanh(inner_scale * (pre + 0.044715 * squared * pre))
        active = 0.5 * pre * (1.0 + bent)
        slope = 0.5 * (1.0 + bent) + 0.5 * pre * (1.0 - bent * bent) * inner_scale * (
            1.0 + 3.0 * 0.044715 * squared
        )
        grad_pre = (grad_act * slope).astype(BF16).astype(F32)
        plain_sum += jnp.sum(grad_pre * gain_sums[3 + block : 4 + block], axis=1, keepdims=True)
        hat_sum += jnp.sum(grad_pre * pre, axis=1, keepdims=True)
        start = (4 + block) * head_width
        out[:, start : start + head_width] = spread(active)
        start += hidden_width
        out[:, start : start + head_width] = spread(grad_pre)
    scalars = pieces(merge.mean, 3) + pieces(inverse, 3) + pieces(plain_sum, 2) + pieces(hat_sum, 2)
    out[:, 4 * head_width + 2 * hidden_width :] = spread(to_lanes(scalars))


def attend_kernel(
    head_width, hidden_width, full, gain_sums, tokens, ln_gain, query_gain, key_gain, cotangent, acts
):
    head_size = query_gain.shape[0]
    query_row, key_row = query_gain[...][None], key_gain[...][None]
    local_width = tokens.shape[1]
    stats = full[:, 4 * head_width + 2 * hidden_width :].astype(F32)
    mean, inverse = from_lanes(stats, 0, 3), from_lanes(stats, 3, 3)
    plain_sum, hat_sum = from_lanes(stats, 6, 2), from_lanes(stats, 8, 2)
    normal_hat = (tokens[...].astype(F32) - mean) * inverse
    acts[:, :local_width] = (normal_hat * ln_gain[...][None]).astype(BF16)
    acts[:, local_width : 2 * local_width] = cotangent[...]
    hidden_at = 4 * head_width
    acts_hidden = 2 * local_width
    acts[:, acts_hidden : acts_hidden + 2 * hidden_width] = full[:, hidden_at : hidden_at + 2 * hidden_width]
    acts_heads = acts_hidden + 2 * hidden_width
    scale = head_size ** (-0.5)

    def normalise(values):
        centred = values - jnp.mean(values, axis=1, keepdims=True)
        root = lax.rsqrt(jnp.mean(centred * centred, axis=1, keepdims=True) + EPSILON)
        return centred * root, root

    def back(grad, hat, root, gain):
        grad = grad * gain
        centred = grad - jnp.mean(grad, axis=1, keepdims=True)
        centred = centred - hat * jnp.mean(grad * hat, axis=1, keepdims=True)
        return (root * centred).astype(BF16)

    for head in range(head_width // head_size):
        low, high = head * head_size, (head + 1) * head_size
        query = full[:, low:high].astype(F32)
        key = full[:, head_width + low : head_width + high].astype(F32)
        value_low = full[:, 2 * head_width + low : 2 * head_width + high]
        grad_mix = full[:, 3 * head_width + low : 3 * head_width + high]
        query_hat, query_root = normalise(query)
        key_hat, key_root = normalise(key)
        query_norm = (query_hat * query_row).astype(BF16)
        key_norm = (key_hat * key_row).astype(BF16)
        scores = dot_last(query_norm, key_norm) * scale
        weights = jnp.exp(scores - jnp.max(scores, axis=1, keepdims=True))
        probs = weights / jnp.sum(weights, axis=1, keepdims=True)
        probs_low = probs.astype(BF16)
        acts[:, acts_heads + low : acts_heads + high] = dot_plain(probs_low, value_low).astype(BF16)
        grad_probs = dot_last(grad_mix, value_low)
        grad_value = dot_first(probs_low, grad_mix).astype(BF16)
        grad_scores = probs * (grad_probs - jnp.sum(grad_probs * probs, axis=1, keepdims=True))
        grad_scores = grad_scores.astype(BF16)
        grad_query = back(
            dot_plain(grad_scores, key_norm) * scale, query_hat, query_root, query_row
        )
        grad_key = back(
            dot_first(grad_scores, query_norm) * scale, key_hat, key_root, key_row
        )
        plain = jnp.zeros_like(query)
        with_hat = jnp.zeros_like(query)
        for part, (grad, pre) in enumerate(
            ((grad_query, query), (grad_key, key), (grad_value, value_low.astype(F32)))
        ):
            start = acts_heads + (1 + part) * head_width
            acts[:, start + low : start + high] = grad
            grad = grad.astype(F32)
            plain = plain + grad * gain_sums[part : part + 1, low:high]
            with_hat = with_hat + grad * pre
        plain_sum = plain_sum + jnp.sum(plain, axis=1, keepdims=True)
        hat_sum = hat_sum + jnp.sum(with_hat, axis=1, keepdims=True)

    acts[:, acts_heads + 4 * head_width :] = to_lanes(pieces(plain_sum, 2) + pieces(hat_sum, 2)).astype(BF16)


def terms_kernel(
    acts_far, w_mlp_far, w_hidden_far, w_attn_far, w_qkv_far, terms,
    acts, w_mlp, w_hidden, w_attn, w_qkv, arrived,
):
    head_width = w_qkv.shape[2]
    hidden_width, local_width = w_mlp.shape
    hidden_at = 2 * local_width
    heads_at = hidden_at + 2 * hidden_width
    loads = []

    def load(source, target):
        copy = pltpu.make_async_copy(source, target, arrived.at[len(loads)])
        copy.start()
        loads.append(copy)

    def load_acts(start, length):
        load(acts_far.at[:, pl.ds(start, length)], acts.at[:, pl.ds(start, length)])

    load_acts(hidden_at, hidden_width)
    load(w_mlp_far, w_mlp)
    load_acts(hidden_at + hidden_width, hidden_width)
    load(w_hidden_far, w_hidden)
    load_acts(heads_at, 4 * head_width + LANES)
    load(w_attn_far, w_attn)
    load(w_qkv_far, w_qkv)

    loads[0].wait()
    loads[1].wait()
    mixed = dot_plain(acts[:, hidden_at : hidden_at + hidden_width], w_mlp[...])
    loads[2].wait()
    loads[3].wait()
    grad_normed = dot_last(acts[:, hidden_at + hidden_width : heads_at], w_hidden[...])
    for copy in loads[4:]:
        copy.wait()
    mixed = mixed + dot_plain(acts[:, heads_at : heads_at + head_width], w_attn[...])
    terms[:, :local_width] = mixed.astype(BF16)
    for part in range(3):
        start = heads_at + (1 + part) * head_width
        grad_normed = grad_normed + dot_last(acts[:, start : start + head_width], w_qkv[part])
    terms[:, local_width : 2 * local_width] = grad_normed.astype(BF16)
    terms[:, 2 * local_width :] = acts[:, heads_at + 4 * head_width :]


def weight_kernel(
    head_width, hidden_width, n_dp, place, own, peer, here_far, far_far, relayed_far, direct_far,
    acts, norm_t, mix_t, act_t, here, far, relayed, direct, arrived, left_for,
):
    row_count, local_width = own.shape[0], norm_t.shape[0]
    hidden_at = 2 * local_width
    heads_at = hidden_at + 2 * hidden_width
    core, chip, chips = place[0] % 2, place[0] // 2, n_dp // 2
    toward = 1 - 2 * core
    outs = (far, relayed, direct, here)
    outs_far = (far_far, relayed_far, direct_far, here_far)
    owners = [2 * ((chip + chips + step) % chips) + core for step in (2, toward, -toward, 0)]
    spans = (
        (0, local_width),
        (heads_at + head_width, 3 * head_width),
        (hidden_at + hidden_width, hidden_width),
        (hidden_at, hidden_width),
        (local_width, local_width),
        (heads_at, head_width),
    )
    loads = []
    for index, (start, length) in enumerate(spans):
        columns = pl.ds(start, length)
        for side, source in enumerate((own, peer)):
            target = acts.at[pl.ds(side * row_count, row_count), columns]
            load = pltpu.make_async_copy(source.at[:, columns], target, arrived.at[2 * index + side])
            load.start()
            loads.append(load)

    def ready(index):
        loads[2 * index].wait()
        loads[2 * index + 1].wait()

    def both(start, length):
        return acts[:, start : start + length]

    def rows(ref, length):
        return jnp.concatenate(
            [ref[pl.ds(pl.multiple_of(owner * length, 16), length), :] for owner in owners], axis=0
        )

    row, sent, sends = 0, 0, []

    def emit(left, right):
        nonlocal row
        length = left.shape[0] // len(owners)
        product = dot_plain(left, right)
        for step, out in enumerate(outs):
            out[row : row + length, :] = product[step * length : (step + 1) * length].astype(out.dtype)
        row += length

    def send():
        nonlocal sent
        part = pl.ds(sent, row - sent)
        for out, out_far in zip(outs, outs_far):
            copy = pltpu.make_async_copy(out.at[part, :], out_far.at[part, :], left_for.at[len(sends)])
            copy.start()
            sends.append(copy)
        sent = row

    ready(0)
    norm_t[...] = both(0, local_width).T
    norm_rows = rows(norm_t, local_width // n_dp)
    ready(1)
    for part in range(3):
        emit(norm_rows, both(heads_at + (1 + part) * head_width, head_width))
    send()
    ready(2)
    for block in range(hidden_width // head_width):
        emit(norm_rows, both(hidden_at + hidden_width + block * head_width, head_width))
    send()
    for index in (3, 4, 5):
        ready(index)
    mix_t[...] = both(heads_at, head_width).T
    act_t[...] = both(hidden_at, hidden_width).T
    cotangent = both(local_width, local_width)
    emit(rows(mix_t, head_width // n_dp), cotangent)
    emit(rows(act_t, hidden_width // n_dp), cotangent)
    send()
    for copy in sends:
        copy.wait()


def token_kernel(place, got, full, tokens, ln_gain, cotangent, mixed, grad_tokens):
    out_rows, local_width = mixed.shape
    parts = got.shape[0] // out_rows
    width = place[1]
    first = pl.multiple_of(place[0] * out_rows, 16)

    def total(start, length):
        values = got[:, start : start + length].astype(F32)
        return jnp.sum(values.reshape(parts, out_rows, length), axis=0)

    values = tokens[pl.ds(first, out_rows), :].astype(F32)
    mixed[...] = (values + total(0, local_width)).astype(BF16)
    stats = full[pl.ds(first, out_rows), full.shape[1] - LANES :].astype(F32)
    mean, inverse = from_lanes(stats, 0, 3), from_lanes(stats, 3, 3)
    normal_hat = (values - mean) * inverse
    sums = total(2 * local_width, LANES)
    share = 1.0 / width.astype(F32)
    mean_one, mean_two = from_lanes(sums, 0, 2) * share, from_lanes(sums, 2, 2) * share
    grad_hat = total(local_width, local_width) * ln_gain[...][None]
    grad = inverse * (grad_hat - mean_one - normal_hat * mean_two)
    back = cotangent[pl.ds(first, out_rows), :].astype(F32)
    grad_tokens[...] = (back + grad).astype(BF16)


def sum_kernel(
    here, relayed_far, direct, qkv_far, hidden_far, attn_far, mlp_far,
    relayed, qkv, hidden, attn, mlp, arrived, left_for,
):
    length, head_width = qkv.shape[2], qkv.shape[3]
    blocks = hidden.shape[2] // head_width
    cuts = (0, 3 * length, (3 + blocks) * length, here.shape[0])
    loads = []
    for index, (start, end) in enumerate(zip(cuts, cuts[1:])):
        part = pl.ds(start, end - start)
        loads.append(
            pltpu.make_async_copy(relayed_far.at[part, :], relayed.at[part, :], arrived.at[index])
        )
        loads[index].start()

    def total(start, count):
        value = here[start : start + count, :]
        for part in (relayed, direct):
            value = value + part[start : start + count, :].astype(F32)
        return value

    sends = []

    def send(source, target):
        copy = pltpu.make_async_copy(source, target, left_for.at[len(sends)])
        copy.start()
        sends.append(copy)

    loads[0].wait()
    for part in range(3):
        qkv[part, 0] = total(part * length, length)
    send(qkv, qkv_far)
    loads[1].wait()
    for block in range(blocks):
        columns = slice(block * head_width, (block + 1) * head_width)
        hidden[0, :, columns] = total(cuts[1] + block * length, length)
    send(hidden, hidden_far)
    loads[2].wait()
    attn[0] = total(cuts[2], attn.shape[1])
    send(attn, attn_far)
    mlp[0] = total(cuts[2] + attn.shape[1], mlp.shape[1])
    send(mlp, mlp_far)
    for copy in sends:
        copy.wait()


def exchange(values, axis, groups=None):
    return lax.all_to_all(values, axis, 0, 0, tiled=True, axis_index_groups=groups)


def per_device(
    tokens, ln_gain, query_gain, key_gain, w_qkv, w_hidden, w_attn_out, w_mlp_out, cotangent
):
    n_dp, n_mx, n_my = lax.axis_size("dp"), lax.axis_size("mx"), lax.axis_size("my")
    row_count, local_width = tokens.shape
    head_width, hidden_width = w_qkv.shape[2], w_hidden.shape[1]
    width = local_width * n_my
    share, out_rows = row_count // n_my, row_count // n_mx
    near = 4 if n_my % 16 == 0 else 2
    near_groups = [[first + step for step in range(near)] for first in range(0, n_my, near)]
    far_groups = [list(range(first, n_my, near)) for first in range(near)]


    def shape(*dims, dtype=BF16):
        return jax.ShapeDtypeStruct(dims, dtype)

    near_width = 4 * head_width + 2 * hidden_width + LANES
    inputs = (tokens, ln_gain, w_qkv, w_hidden, cotangent, w_attn_out, w_mlp_out)
    (terms,) = run(
        lambda *refs: project_kernel(row_count // near, *refs),
        inputs,
        (shape(row_count, near_width),),
        scratch=[pltpu.VMEM(array.shape, array.dtype) for array in inputs]
        + [
            pltpu.VMEM((row_count, near_width), BF16),
            pltpu.SemaphoreType.DMA((len(inputs),)),
            pltpu.SemaphoreType.DMA((near_width // head_width + 1,)),
        ],
        fetched=range(len(inputs)),
        written=(0,),
        mebibytes=60,
    )
    got = exchange(terms, "my", near_groups)
    (terms,) = run(
        lambda *refs: merge_kernel(share, near, local_width, head_width, *refs),
        (got,),
        (shape(row_count // near, 5 * head_width + 2 * hidden_width),),
    )
    got = exchange(terms, "my", far_groups)
    spread, gain_sums = run(
        lambda *refs: share_kernel(n_my // near, near * local_width, head_width, *refs),
        (got,),
        (
            shape(row_count // near, 4 * head_width + 2 * hidden_width + LANES),
            shape(share, head_width, dtype=F32),
        ),
    )
    part = exchange(spread, "my", far_groups)
    spread = jnp.broadcast_to(part[None], (near, *part.shape)).reshape(row_count, part.shape[1])
    full = exchange(spread, "my", near_groups)
    act_width = 2 * local_width + 2 * hidden_width + 4 * head_width + LANES
    (acts,) = run(
        lambda *refs: attend_kernel(head_width, hidden_width, *refs),
        (full, gain_sums, tokens, ln_gain, query_gain, key_gain, cotangent),
        (shape(row_count, act_width),),
    )
    peer_acts = lax.ppermute(acts, "dp", [(source, source ^ 1) for source in range(n_dp)])
    (out_terms,) = run(
        terms_kernel,
        (acts, w_mlp_out, w_hidden, w_attn_out, w_qkv),
        (shape(row_count, 2 * local_width + LANES),),
        scratch=[
            pltpu.VMEM(array.shape, BF16) for array in (acts, w_mlp_out, w_hidden, w_attn_out, w_qkv)
        ]
        + [pltpu.SemaphoreType.DMA((7,))],
        fetched=(0, 1, 2, 3, 4),
        mebibytes=60,
    )
    peer_acts, out_terms = lax.optimization_barrier((peer_acts, out_terms))
    out_got = exchange(out_terms, "mx")
    block_rows = (3 * local_width + local_width * hidden_width // head_width + head_width + hidden_width) // n_dp
    block = shape(block_rows, local_width)
    place = lax.axis_index("dp").reshape(1)
    weight_outs = (shape(block_rows, local_width, dtype=F32),) + (block,) * 3
    here, far, relayed, direct = run(
        lambda *refs: weight_kernel(head_width, hidden_width, n_dp, *refs),
        (place, acts, peer_acts),
        weight_outs,
        scratch=[
            pltpu.VMEM((2 * row_count, act_width), BF16),
            pltpu.VMEM((local_width, 2 * row_count), BF16),
            pltpu.VMEM((head_width, 2 * row_count), BF16),
            pltpu.VMEM((hidden_width, 2 * row_count), BF16),
            *(pltpu.VMEM(out.shape, out.dtype) for out in weight_outs),
            pltpu.SemaphoreType.DMA((12,)),
            pltpu.SemaphoreType.DMA((12,)),
        ],
        scalar=True,
        fetched=(1, 2),
        written=(0, 1, 2, 3),
        mebibytes=60,
    )

    def pass_on(values, step):
        ways = [(s, (s + 2 * step * (1 - 2 * (s % 2))) % n_dp) for s in range(n_dp)]
        return lax.ppermute(values, "dp", ways)

    passing = pass_on(far, 1)
    got_direct = pass_on(direct, -1)
    joined = (relayed.astype(F32) + passing.astype(F32)).astype(BF16)
    joined, out_got = lax.optimization_barrier((joined, out_got))
    got_relayed = pass_on(joined, 1)
    place = jnp.stack([lax.axis_index("mx"), jnp.int32(width)])
    mixed, grad_tokens = run(
        token_kernel,
        (place, out_got, full, tokens, ln_gain, cotangent),
        (shape(out_rows, local_width), shape(out_rows, local_width)),
        scalar=True,
    )
    grad_shapes = (
        shape(3, 1, local_width // n_dp, head_width, dtype=F32),
        shape(1, local_width // n_dp, hidden_width, dtype=F32),
        shape(1, head_width // n_dp, local_width, dtype=F32),
        shape(1, hidden_width // n_dp, local_width, dtype=F32),
    )
    grads = run(
        sum_kernel,
        (here, got_relayed, got_direct),
        grad_shapes,
        scratch=[pltpu.VMEM(block.shape, BF16)]
        + [pltpu.VMEM(grad.shape, grad.dtype) for grad in grad_shapes]
        + [pltpu.SemaphoreType.DMA((3,)), pltpu.SemaphoreType.DMA((4,))],
        fetched=(1,),
        written=(0, 1, 2, 3),
    )
    return (mixed, grad_tokens, *grads)


def solution(mesh):
    placed = (
        P("dp", "my"),
        P("my"),
        P(),
        P(),
        P(None, "my", "mx"),
        P("my", "mx"),
        P("mx", "my"),
        P("mx", "my"),
        P("dp", "my"),
    )
    return jax.shard_map(
        per_device,
        mesh=mesh,
        in_specs=placed,
        out_specs=(
            P(("dp", "mx"), "my"),
            P(("dp", "mx"), "my"),
            P(None, "my", "dp", "mx"),
            P("my", "dp", "mx"),
            P("mx", "dp", "my"),
            P("mx", "dp", "my"),
        ),
        check_vma=False,
    )
```

```python
import jax
import jax.numpy as jnp
from jax import lax
from jax.experimental import pallas as pl
from jax.experimental.pallas import tpu as pltpu
from jax.sharding import PartitionSpec as P

EPSILON = 1e-06
LANES = 128
BF16 = jnp.bfloat16
F32 = jnp.float32


def dot_plain(matrix_a, matrix_b):
    return jnp.dot(matrix_a, matrix_b, preferred_element_type=F32)


def dot_first(matrix_a, matrix_b):
    return lax.dot_general(matrix_a, matrix_b, (((0,), (0,)), ((), ())), preferred_element_type=F32)


def dot_last(matrix_a, matrix_b):
    return lax.dot_general(matrix_a, matrix_b, (((1,), (1,)), ((), ())), preferred_element_type=F32)


def pieces(value, count):
    out = []
    for _ in range(count):
        part = value.astype(BF16).astype(F32)
        out.append(part)
        value = value - part
    return out


def to_lanes(columns):
    rows = columns[0].shape[0]
    lane = lax.broadcasted_iota(jnp.int32, (rows, LANES), 1)
    block = jnp.zeros((rows, LANES), F32)
    for index, column in enumerate(columns):
        block = jnp.where(lane == index, column, block)
    return block


def from_lanes(block, first, count):
    lane = lax.broadcasted_iota(jnp.int32, block.shape, block.ndim - 1)
    keep = (lane >= first) & (lane < first + count)
    return jnp.sum(jnp.where(keep, block, 0.0), axis=-1, keepdims=True)


def pack(values, share, width):
    rows = values[0].shape[0]
    lane = lax.broadcasted_iota(jnp.int32, (rows, width), 1)
    token = lax.broadcasted_iota(jnp.int32, (rows, width), 0) % share
    block = jnp.zeros((rows, width), F32)
    for index, value in enumerate(values):
        block = jnp.where(lane == token * len(values) + index, value, block)
    return jnp.sum(block.reshape(rows // share, share, width), axis=1, keepdims=True)


def unpack(row, share, count, offset):
    shape = (row.shape[0], share, row.shape[2])
    lane = lax.broadcasted_iota(jnp.int32, shape, 2)
    first = lax.broadcasted_iota(jnp.int32, shape, 1) * count + offset
    keep = (lane >= first) & (lane < first + 3)
    return jnp.sum(jnp.where(keep, jnp.broadcast_to(row, shape), 0.0), axis=2, keepdims=True)


class Merge:
    def __init__(self, got, share, parts, part_width, head_width, compact):
        self.got, self.parts, self.head_width = got, parts, head_width
        rows, columns = got.shape
        self.rows, self.kept = rows, rows // parts
        lines = head_width // LANES
        if compact:
            share, start = self.kept, columns - LANES
            block = self.take(start, LANES).reshape(parts, share, LANES)
            blocks = (start // head_width - 4) // 2 + 3
            self.gain_rows = [
                jnp.concatenate([block[:, row : row + 1, :] for row in range(first, first + lines)], axis=2)
                for first in range(0, blocks * lines, lines)
            ]
            last = blocks * lines
            local_mean = unpack(block[:, last : last + 1, :], share, 3, 0)
            local_squares = unpack(block[:, last + 1 : last + 2, :], share, 3, 0)
        else:
            start = columns - head_width
            block = self.take(start, head_width).reshape(rows // share, share, head_width)
            self.gain_rows = [block[:, row : row + 1, :] for row in range(share - 1)]
            local_mean = unpack(block[:, share - 1 : share, :], share, 6, 0)
            local_squares = unpack(block[:, share - 1 : share, :], share, 6, 3)
        self.mean = self.add(local_mean.reshape(rows, 1)) / parts
        everywhere = jnp.broadcast_to(self.mean[None], (parts, self.kept, 1))
        self.shift = local_mean - everywhere.reshape(rows // share, share, 1)
        squares = local_squares + part_width * self.shift * self.shift
        self.squares = self.add(squares.reshape(rows, 1))

    def take(self, start, length):
        return self.got[:, start : start + length].astype(F32)

    def add(self, values):
        return jnp.sum(values.reshape(self.parts, self.kept, values.shape[1]), axis=0)

    def plain(self, block):
        return self.add(self.take(block * self.head_width, self.head_width))

    def projected(self, block):
        change = self.shift * self.gain_rows[block]
        return self.plain(block) + self.add(change.reshape(self.rows, self.head_width))

    def gain_sum(self, block):
        return jnp.sum(self.gain_rows[block], axis=0)


def run(kernel, operands, out_shape, scratch=(), scalar=False, fetched=(), written=(), mebibytes=16):
    in_specs = [pl.BlockSpec(memory_space=pltpu.VMEM)] * len(operands)
    out_specs = [pl.BlockSpec(memory_space=pltpu.VMEM)] * len(out_shape)
    if scalar:
        in_specs[0] = pl.BlockSpec(memory_space=pltpu.SMEM)
    for index in fetched:
        in_specs[index] = pl.BlockSpec(memory_space=pltpu.HBM)
    for index in written:
        out_specs[index] = pl.BlockSpec(memory_space=pltpu.HBM)
    return pl.pallas_call(
        kernel,
        in_specs=in_specs,
        out_specs=out_specs,
        out_shape=out_shape,
        scratch_shapes=list(scratch),
        compiler_params=pltpu.CompilerParams(vmem_limit_bytes=mebibytes * 1024 * 1024),
    )(*operands)


def project_kernel(kept, *refs):
    far, out_far, near, out, arrived, left_for = refs[:7], refs[7], refs[8:15], refs[15], refs[16], refs[17]
    tokens, ln_gain, w_qkv, w_hidden, cotangent, w_attn, w_mlp = near
    rows, width = tokens.shape
    head_width = w_qkv.shape[2]
    blocks = w_hidden.shape[1] // head_width
    loads = [
        pltpu.make_async_copy(source, target, arrived.at[index])
        for index, (source, target) in enumerate(zip(far, near))
    ]
    for load in loads:
        load.start()
    sends = []

    def emit(values):
        columns = pl.ds(sum(send[1] for send in sends), values.shape[1])
        out[:, columns] = values.astype(BF16)
        copy = pltpu.make_async_copy(out.at[:, columns], out_far.at[:, columns], left_for.at[len(sends)])
        copy.start()
        sends.append((copy, values.shape[1]))

    loads[0].wait()
    loads[1].wait()
    values = tokens[...].astype(F32)
    mean = jnp.sum(values, axis=1, keepdims=True) / width
    centred = values - mean
    squares = jnp.sum(centred * centred, axis=1, keepdims=True)
    gain = ln_gain[...][None]
    scaled = (centred * gain).astype(BF16)
    high, low = pieces(gain, 2)
    row_id = lax.broadcasted_iota(jnp.int32, (16, width), 0)
    gain_rows = jnp.where(row_id == 0, high, jnp.where(row_id == 1, low, 0.0)).astype(BF16)
    left = jnp.concatenate([scaled, gain_rows], axis=0)
    lines = head_width // LANES
    line_id = lax.broadcasted_iota(jnp.int32, (kept, LANES), 0)
    gain_sums = jnp.zeros((kept, LANES), F32)
    for block in range(3 + blocks):
        if block == 0 or block == 3:
            loads[2 + block // 3].wait()
        if block < 3:
            weight = w_qkv[block]
        else:
            weight = w_hidden[:, (block - 3) * head_width : (block - 2) * head_width]
        product = dot_plain(left, weight)
        emit(product[:rows])
        both = product[rows : rows + 1] + product[rows + 1 : rows + 2]
        for line in range(lines):
            value = both[:, line * LANES : (line + 1) * LANES]
            gain_sums = jnp.where(line_id == block * lines + line, value, gain_sums)
    loads[4].wait()
    loads[5].wait()
    back = cotangent[...]
    emit(dot_last(back, w_attn[...]))
    loads[6].wait()
    for block in range(blocks):
        emit(dot_last(back, w_mlp[block * head_width : (block + 1) * head_width, :]))
    last = (3 + blocks) * lines
    spread = jnp.where(line_id[None] == last, pack(pieces(mean, 3), kept, LANES), gain_sums[None])
    spread = jnp.where(line_id[None] == last + 1, pack(pieces(squares, 3), kept, LANES), spread)
    emit(spread.reshape(rows, LANES))
    for copy, _ in sends:
        copy.wait()


def merge_kernel(share, parts, part_width, head_width, got, out):
    merge = Merge(got, share, parts, part_width, head_width, True)
    last = (got.shape[1] - LANES) // head_width
    blocks = (last - 4) // 2
    shape = (merge.kept // share, share, head_width)
    share_id = lax.broadcasted_iota(jnp.int32, shape, 1)
    sums = jnp.zeros(shape, F32)
    for block in range(last):
        if block < 3 + blocks:
            value = merge.projected(block)
            sums = jnp.where(share_id == block, merge.gain_sum(block)[None], sums)
        else:
            value = merge.plain(block)
        out[:, block * head_width : (block + 1) * head_width] = value.astype(BF16)
    row = pack(pieces(merge.mean, 3) + pieces(merge.squares, 3), share, head_width)
    sums = jnp.where(share_id == share - 1, row, sums)
    out[:, last * head_width :] = sums.reshape(merge.kept, head_width).astype(BF16)


def share_kernel(parts, part_width, head_width, got, out, sums_out):
    rows, columns = got.shape
    share = rows // parts
    hidden_width = (columns - 5 * head_width) // 2
    blocks = hidden_width // head_width
    merge = Merge(got, share, parts, part_width, head_width, False)
    inverse = lax.rsqrt(merge.squares / (parts * part_width) + EPSILON)
    share_id = lax.broadcasted_iota(jnp.int32, sums_out.shape, 0)
    gain_sums = jnp.zeros(sums_out.shape, F32)
    for block in range(3 + blocks):
        gain_sums = jnp.where(share_id == block, merge.gain_sum(block), gain_sums)
    sums_out[...] = gain_sums

    def spread(value):
        length = value.shape[1]
        tiled = jnp.broadcast_to(value[None], (out.shape[0] // share, share, length))
        return tiled.reshape(out.shape[0], length).astype(BF16)

    def projected(block):
        return (inverse * merge.projected(block)).astype(BF16).astype(F32)

    back_at = 3 + blocks
    for block in range(3):
        out[:, block * head_width : (block + 1) * head_width] = spread(projected(block))
    out[:, 3 * head_width : 4 * head_width] = spread(merge.plain(back_at))
    plain_sum = jnp.zeros((share, 1), F32)
    hat_sum = jnp.zeros((share, 1), F32)
    inner_scale = 0.7978845608028654
    for block in range(blocks):
        pre = projected(3 + block)
        grad_act = merge.plain(back_at + 1 + block).astype(BF16).astype(F32)
        squared = pre * pre
        bent = jnp.tanh(inner_scale * (pre + 0.044715 * squared * pre))
        active = 0.5 * pre * (1.0 + bent)
        slope = 0.5 * (1.0 + bent) + 0.5 * pre * (1.0 - bent * bent) * inner_scale * (
            1.0 + 3.0 * 0.044715 * squared
        )
        grad_pre = (grad_act * slope).astype(BF16).astype(F32)
        plain_sum += jnp.sum(grad_pre * gain_sums[3 + block : 4 + block], axis=1, keepdims=True)
        hat_sum += jnp.sum(grad_pre * pre, axis=1, keepdims=True)
        start = (4 + block) * head_width
        out[:, start : start + head_width] = spread(active)
        start += hidden_width
        out[:, start : start + head_width] = spread(grad_pre)
    scalars = pieces(merge.mean, 3) + pieces(inverse, 3) + pieces(plain_sum, 2) + pieces(hat_sum, 2)
    out[:, 4 * head_width + 2 * hidden_width :] = spread(to_lanes(scalars))


def attend_kernel(
    head_width, hidden_width, full, gain_sums, tokens, ln_gain, query_gain, key_gain, cotangent, acts
):
    head_size = query_gain.shape[0]
    query_row, key_row = query_gain[...][None], key_gain[...][None]
    local_width = tokens.shape[1]
    stats = full[:, 4 * head_width + 2 * hidden_width :].astype(F32)
    mean, inverse = from_lanes(stats, 0, 3), from_lanes(stats, 3, 3)
    plain_sum, hat_sum = from_lanes(stats, 6, 2), from_lanes(stats, 8, 2)
    normal_hat = (tokens[...].astype(F32) - mean) * inverse
    acts[:, :local_width] = (normal_hat * ln_gain[...][None]).astype(BF16)
    acts[:, local_width : 2 * local_width] = cotangent[...]
    hidden_at = 4 * head_width
    acts_hidden = 2 * local_width
    acts[:, acts_hidden : acts_hidden + 2 * hidden_width] = full[:, hidden_at : hidden_at + 2 * hidden_width]
    acts_heads = acts_hidden + 2 * hidden_width
    scale = head_size ** (-0.5)

    def normalise(values):
        centred = values - jnp.mean(values, axis=1, keepdims=True)
        root = lax.rsqrt(jnp.mean(centred * centred, axis=1, keepdims=True) + EPSILON)
        return centred * root, root

    def back(grad, hat, root, gain):
        grad = grad * gain
        centred = grad - jnp.mean(grad, axis=1, keepdims=True)
        centred = centred - hat * jnp.mean(grad * hat, axis=1, keepdims=True)
        return (root * centred).astype(BF16)

    heads = [
        (head * head_size, (head + 1) * head_size) for head in range(head_width // head_size)
    ]

    def of(part):
        return [full[:, part * head_width + low : part * head_width + high] for low, high in heads]

    queries, keys = [x.astype(F32) for x in of(0)], [x.astype(F32) for x in of(1)]
    values, grad_mixes = of(2), of(3)
    query_hats, query_roots = zip(*map(normalise, queries))
    key_hats, key_roots = zip(*map(normalise, keys))
    query_norms = [(hat * query_row).astype(BF16) for hat in query_hats]
    key_norms = [(hat * key_row).astype(BF16) for hat in key_hats]
    scores = [dot_last(query, key) * scale for query, key in zip(query_norms, key_norms)]
    grad_probs = [dot_last(grad, value) for grad, value in zip(grad_mixes, values)]
    raised = [jnp.exp(score - jnp.max(score, axis=1, keepdims=True)) for score in scores]
    probs = [value / jnp.sum(value, axis=1, keepdims=True) for value in raised]
    probs_low = [prob.astype(BF16) for prob in probs]
    mixes = [dot_plain(prob, value).astype(BF16) for prob, value in zip(probs_low, values)]
    grad_values = [dot_first(prob, grad).astype(BF16) for prob, grad in zip(probs_low, grad_mixes)]
    grad_scores = [
        (prob * (grad - jnp.sum(grad * prob, axis=1, keepdims=True))).astype(BF16)
        for prob, grad in zip(probs, grad_probs)
    ]
    grad_queries = [
        back(dot_plain(grad, key) * scale, hat, root, query_row)
        for grad, key, hat, root in zip(grad_scores, key_norms, query_hats, query_roots)
    ]
    grad_keys = [
        back(dot_first(grad, query) * scale, hat, root, key_row)
        for grad, query, hat, root in zip(grad_scores, query_norms, key_hats, key_roots)
    ]
    plain = jnp.zeros_like(queries[0])
    with_hat = jnp.zeros_like(queries[0])
    for index, (low, high) in enumerate(heads):
        acts[:, acts_heads + low : acts_heads + high] = mixes[index]
        for part, (grads, pres) in enumerate(
            ((grad_queries, queries), (grad_keys, keys), (grad_values, values))
        ):
            start = acts_heads + (1 + part) * head_width
            acts[:, start + low : start + high] = grads[index]
            grad = grads[index].astype(F32)
            plain = plain + grad * gain_sums[part : part + 1, low:high]
            with_hat = with_hat + grad * pres[index].astype(F32)
    plain_sum = plain_sum + jnp.sum(plain, axis=1, keepdims=True)
    hat_sum = hat_sum + jnp.sum(with_hat, axis=1, keepdims=True)
    acts[:, acts_heads + 4 * head_width :] = to_lanes(pieces(plain_sum, 2) + pieces(hat_sum, 2)).astype(BF16)


def terms_kernel(
    acts_far, w_mlp_far, w_hidden_far, w_attn_far, w_qkv_far, terms,
    acts, w_mlp, w_hidden, w_attn, w_qkv, arrived,
):
    head_width = w_qkv.shape[2]
    hidden_width, local_width = w_mlp.shape
    hidden_at = 2 * local_width
    heads_at = hidden_at + 2 * hidden_width
    loads = []

    def load(source, target):
        copy = pltpu.make_async_copy(source, target, arrived.at[len(loads)])
        copy.start()
        loads.append(copy)

    def load_acts(start, length):
        load(acts_far.at[:, pl.ds(start, length)], acts.at[:, pl.ds(start, length)])

    load_acts(heads_at, 4 * head_width + LANES)
    load(w_attn_far, w_attn)
    load(w_qkv_far, w_qkv)
    load_acts(hidden_at, hidden_width)
    load(w_mlp_far, w_mlp)
    load_acts(hidden_at + hidden_width, hidden_width)
    load(w_hidden_far, w_hidden)

    def ready(*which):
        for index in which:
            loads[index].wait()

    ready(0, 1)
    mixed = dot_plain(acts[:, heads_at : heads_at + head_width], w_attn[...])
    ready(2)
    grad_normed = jnp.zeros(mixed.shape, F32)
    for part in range(3):
        start = heads_at + (1 + part) * head_width
        grad_normed = grad_normed + dot_last(acts[:, start : start + head_width], w_qkv[part])
    ready(3, 4)
    mixed = mixed + dot_plain(acts[:, hidden_at : hidden_at + hidden_width], w_mlp[...])
    terms[:, :local_width] = mixed.astype(BF16)
    ready(5, 6)
    grad_normed = grad_normed + dot_last(acts[:, hidden_at + hidden_width : heads_at], w_hidden[...])
    terms[:, local_width : 2 * local_width] = grad_normed.astype(BF16)
    terms[:, 2 * local_width :] = acts[:, heads_at + 4 * head_width :]


def weight_kernel(
    head_width, hidden_width, n_dp, place, own, peer, here_far, far_far, relayed_far, direct_far,
    acts, norm_t, mix_t, act_t, here, far, relayed, direct, arrived, left_for,
):
    row_count, local_width = own.shape[0], norm_t.shape[0]
    hidden_at = 2 * local_width
    heads_at = hidden_at + 2 * hidden_width
    core, chip, chips = place[0] % 2, place[0] // 2, n_dp // 2
    toward = 1 - 2 * core
    outs = (far, relayed, direct, here)
    outs_far = (far_far, relayed_far, direct_far, here_far)
    owners = [2 * ((chip + chips + step) % chips) + core for step in (2, toward, -toward, 0)]
    spans = (
        (0, local_width),
        (heads_at + head_width, 3 * head_width),
        (hidden_at + hidden_width, hidden_width),
        (hidden_at, hidden_width),
        (local_width, local_width),
        (heads_at, head_width),
    )
    loads = []
    for index, (start, length) in enumerate(spans):
        columns = pl.ds(start, length)
        for side, source in enumerate((own, peer)):
            target = acts.at[pl.ds(side * row_count, row_count), columns]
            load = pltpu.make_async_copy(source.at[:, columns], target, arrived.at[2 * index + side])
            load.start()
            loads.append(load)

    def ready(index):
        loads[2 * index].wait()
        loads[2 * index + 1].wait()

    def both(start, length):
        return acts[:, start : start + length]

    def rows(ref, length):
        return jnp.concatenate(
            [ref[pl.ds(pl.multiple_of(owner * length, 16), length), :] for owner in owners], axis=0
        )

    row, sent, sends = 0, 0, []

    def emit(left, right):
        nonlocal row
        length = left.shape[0] // len(owners)
        product = dot_plain(left, right)
        for step, out in enumerate(outs):
            out[row : row + length, :] = product[step * length : (step + 1) * length].astype(out.dtype)
        row += length

    def send():
        nonlocal sent
        part = pl.ds(sent, row - sent)
        for out, out_far in zip(outs, outs_far):
            copy = pltpu.make_async_copy(out.at[part, :], out_far.at[part, :], left_for.at[len(sends)])
            copy.start()
            sends.append(copy)
        sent = row

    ready(0)
    norm_t[...] = both(0, local_width).T
    norm_rows = rows(norm_t, local_width // n_dp)
    ready(1)
    for part in range(3):
        emit(norm_rows, both(heads_at + (1 + part) * head_width, head_width))
    send()
    ready(2)
    for block in range(hidden_width // head_width):
        emit(norm_rows, both(hidden_at + hidden_width + block * head_width, head_width))
    send()
    for index in (3, 4, 5):
        ready(index)
    mix_t[...] = both(heads_at, head_width).T
    act_t[...] = both(hidden_at, hidden_width).T
    cotangent = both(local_width, local_width)
    emit(rows(mix_t, head_width // n_dp), cotangent)
    emit(rows(act_t, hidden_width // n_dp), cotangent)
    send()
    for copy in sends:
        copy.wait()


def token_kernel(place, got, full, tokens, ln_gain, cotangent, mixed, grad_tokens):
    out_rows, local_width = mixed.shape
    parts = got.shape[0] // out_rows
    width = place[1]
    first = pl.multiple_of(place[0] * out_rows, 16)

    def total(start, length):
        values = got[:, start : start + length].astype(F32)
        return jnp.sum(values.reshape(parts, out_rows, length), axis=0)

    values = tokens[pl.ds(first, out_rows), :].astype(F32)
    mixed[...] = (values + total(0, local_width)).astype(BF16)
    stats = full[pl.ds(first, out_rows), full.shape[1] - LANES :].astype(F32)
    mean, inverse = from_lanes(stats, 0, 3), from_lanes(stats, 3, 3)
    normal_hat = (values - mean) * inverse
    sums = total(2 * local_width, LANES)
    share = 1.0 / width.astype(F32)
    mean_one, mean_two = from_lanes(sums, 0, 2) * share, from_lanes(sums, 2, 2) * share
    grad_hat = total(local_width, local_width) * ln_gain[...][None]
    grad = inverse * (grad_hat - mean_one - normal_hat * mean_two)
    back = cotangent[pl.ds(first, out_rows), :].astype(F32)
    grad_tokens[...] = (back + grad).astype(BF16)


def sum_kernel(
    here, relayed_far, direct, qkv_far, hidden_far, attn_far, mlp_far,
    relayed, qkv, hidden, attn, mlp, arrived, left_for,
):
    length, head_width = qkv.shape[2], qkv.shape[3]
    blocks = hidden.shape[2] // head_width
    cuts = (0, 3 * length, (3 + blocks) * length, here.shape[0])
    loads = []
    for index, (start, end) in enumerate(zip(cuts, cuts[1:])):
        part = pl.ds(start, end - start)
        loads.append(
            pltpu.make_async_copy(relayed_far.at[part, :], relayed.at[part, :], arrived.at[index])
        )
        loads[index].start()

    def total(start, count):
        value = here[start : start + count, :]
        for part in (relayed, direct):
            value = value + part[start : start + count, :].astype(F32)
        return value

    sends = []

    def send(source, target):
        copy = pltpu.make_async_copy(source, target, left_for.at[len(sends)])
        copy.start()
        sends.append(copy)

    loads[0].wait()
    for part in range(3):
        qkv[part, 0] = total(part * length, length)
    send(qkv, qkv_far)
    loads[1].wait()
    for block in range(blocks):
        columns = slice(block * head_width, (block + 1) * head_width)
        hidden[0, :, columns] = total(cuts[1] + block * length, length)
    send(hidden, hidden_far)
    loads[2].wait()
    attn[0] = total(cuts[2], attn.shape[1])
    send(attn, attn_far)
    mlp[0] = total(cuts[2] + attn.shape[1], mlp.shape[1])
    send(mlp, mlp_far)
    for copy in sends:
        copy.wait()


def exchange(values, axis, groups=None):
    return lax.all_to_all(values, axis, 0, 0, tiled=True, axis_index_groups=groups)


def per_device(
    tokens, ln_gain, query_gain, key_gain, w_qkv, w_hidden, w_attn_out, w_mlp_out, cotangent
):
    n_dp, n_mx, n_my = lax.axis_size("dp"), lax.axis_size("mx"), lax.axis_size("my")
    row_count, local_width = tokens.shape
    head_width, hidden_width = w_qkv.shape[2], w_hidden.shape[1]
    width = local_width * n_my
    share, out_rows = row_count // n_my, row_count // n_mx
    near = 4 if n_my % 16 == 0 else 2
    near_groups = [[first + step for step in range(near)] for first in range(0, n_my, near)]
    far_groups = [list(range(first, n_my, near)) for first in range(near)]


    def shape(*dims, dtype=BF16):
        return jax.ShapeDtypeStruct(dims, dtype)

    near_width = 4 * head_width + 2 * hidden_width + LANES
    inputs = (tokens, ln_gain, w_qkv, w_hidden, cotangent, w_attn_out, w_mlp_out)
    (terms,) = run(
        lambda *refs: project_kernel(row_count // near, *refs),
        inputs,
        (shape(row_count, near_width),),
        scratch=[pltpu.VMEM(array.shape, array.dtype) for array in inputs]
        + [
            pltpu.VMEM((row_count, near_width), BF16),
            pltpu.SemaphoreType.DMA((len(inputs),)),
            pltpu.SemaphoreType.DMA((near_width // head_width + 1,)),
        ],
        fetched=range(len(inputs)),
        written=(0,),
        mebibytes=60,
    )
    got = exchange(terms, "my", near_groups)
    (terms,) = run(
        lambda *refs: merge_kernel(share, near, local_width, head_width, *refs),
        (got,),
        (shape(row_count // near, 5 * head_width + 2 * hidden_width),),
    )
    got = exchange(terms, "my", far_groups)
    spread, gain_sums = run(
        lambda *refs: share_kernel(n_my // near, near * local_width, head_width, *refs),
        (got,),
        (
            shape(row_count // near, 4 * head_width + 2 * hidden_width + LANES),
            shape(share, head_width, dtype=F32),
        ),
    )
    part = exchange(spread, "my", far_groups)
    spread = jnp.broadcast_to(part[None], (near, *part.shape)).reshape(row_count, part.shape[1])
    full = exchange(spread, "my", near_groups)
    act_width = 2 * local_width + 2 * hidden_width + 4 * head_width + LANES
    (acts,) = run(
        lambda *refs: attend_kernel(head_width, hidden_width, *refs),
        (full, gain_sums, tokens, ln_gain, query_gain, key_gain, cotangent),
        (shape(row_count, act_width),),
    )
    peer_acts = lax.ppermute(acts, "dp", [(source, source ^ 1) for source in range(n_dp)])
    (out_terms,) = run(
        terms_kernel,
        (acts, w_mlp_out, w_hidden, w_attn_out, w_qkv),
        (shape(row_count, 2 * local_width + LANES),),
        scratch=[
            pltpu.VMEM(array.shape, BF16) for array in (acts, w_mlp_out, w_hidden, w_attn_out, w_qkv)
        ]
        + [pltpu.SemaphoreType.DMA((7,))],
        fetched=(0, 1, 2, 3, 4),
        mebibytes=60,
    )
    peer_acts, out_terms = lax.optimization_barrier((peer_acts, out_terms))
    out_got = exchange(out_terms, "mx")
    block_rows = (3 * local_width + local_width * hidden_width // head_width + head_width + hidden_width) // n_dp
    block = shape(block_rows, local_width)
    place = lax.axis_index("dp").reshape(1)
    weight_outs = (shape(block_rows, local_width, dtype=F32),) + (block,) * 3
    here, far, relayed, direct = run(
        lambda *refs: weight_kernel(head_width, hidden_width, n_dp, *refs),
        (place, acts, peer_acts),
        weight_outs,
        scratch=[
            pltpu.VMEM((2 * row_count, act_width), BF16),
            pltpu.VMEM((local_width, 2 * row_count), BF16),
            pltpu.VMEM((head_width, 2 * row_count), BF16),
            pltpu.VMEM((hidden_width, 2 * row_count), BF16),
            *(pltpu.VMEM(out.shape, out.dtype) for out in weight_outs),
            pltpu.SemaphoreType.DMA((12,)),
            pltpu.SemaphoreType.DMA((12,)),
        ],
        scalar=True,
        fetched=(1, 2),
        written=(0, 1, 2, 3),
        mebibytes=60,
    )

    def pass_on(values, step):
        ways = [(s, (s + 2 * step * (1 - 2 * (s % 2))) % n_dp) for s in range(n_dp)]
        return lax.ppermute(values, "dp", ways)

    passing = pass_on(far, 1)
    got_direct = pass_on(direct, -1)
    joined = (relayed.astype(F32) + passing.astype(F32)).astype(BF16)
    joined, out_got = lax.optimization_barrier((joined, out_got))
    got_relayed = pass_on(joined, 1)
    place = jnp.stack([lax.axis_index("mx"), jnp.int32(width)])
    mixed, grad_tokens = run(
        token_kernel,
        (place, out_got, full, tokens, ln_gain, cotangent),
        (shape(out_rows, local_width), shape(out_rows, local_width)),
        scalar=True,
    )
    grad_shapes = (
        shape(3, 1, local_width // n_dp, head_width, dtype=F32),
        shape(1, local_width // n_dp, hidden_width, dtype=F32),
        shape(1, head_width // n_dp, local_width, dtype=F32),
        shape(1, hidden_width // n_dp, local_width, dtype=F32),
    )
    grads = run(
        sum_kernel,
        (here, got_relayed, got_direct),
        grad_shapes,
        scratch=[pltpu.VMEM(block.shape, BF16)]
        + [pltpu.VMEM(grad.shape, grad.dtype) for grad in grad_shapes]
        + [pltpu.SemaphoreType.DMA((3,)), pltpu.SemaphoreType.DMA((4,))],
        fetched=(1,),
        written=(0, 1, 2, 3),
    )
    return (mixed, grad_tokens, *grads)


def solution(mesh):
    placed = (
        P("dp", "my"),
        P("my"),
        P(),
        P(),
        P(None, "my", "mx"),
        P("my", "mx"),
        P("mx", "my"),
        P("mx", "my"),
        P("dp", "my"),
    )
    return jax.shard_map(
        per_device,
        mesh=mesh,
        in_specs=placed,
        out_specs=(
            P(("dp", "mx"), "my"),
            P(("dp", "mx"), "my"),
            P(None, "my", "dp", "mx"),
            P("my", "dp", "mx"),
            P("mx", "dp", "my"),
            P("mx", "dp", "my"),
        ),
        check_vma=False,
    )
```
